32 devices in a mesh: mic: 4 (over y, core), tm: 8 (over z, x).
Axes of the slice: x: 2, y: 2, z: 4, core: 2. Of those that a mesh axis runs over, the one named last changes fastest.
Arguments:
- frames: bfloat16 [8, 1024, 512], P('mic', 'tm'), may hold values from -6 to 6
- cotangent: bfloat16 [8, 1024, 512], P('mic', 'tm'), may hold values from -6 to 6
- kernel: float32 [31, 512], replicated, may hold values from -1 to 1
- w_query: bfloat16 [512, 512], replicated, may hold values from -0.25 to 0.25
- w_key: bfloat16 [512, 512], replicated, may hold values from -0.25 to 0.25
- w_value: bfloat16 [512, 512], replicated, may hold values from -0.25 to 0.25
- w_out: bfloat16 [512, 512], replicated, may hold values from -0.25 to 0.25
Outputs:
- layer_out: bfloat16 [8, 1024, 512], P('mic', 'tm')
- frame_grad: bfloat16 [8, 1024, 512], P('mic', 'tm')
- kernel_grad: float32 [31, 512], replicated
- query_grad: float32 [512, 512], replicated
- key_grad: float32 [512, 512], replicated
- value_grad: float32 [512, 512], replicated
- out_grad: float32 [512, 512], replicated
The draws below stay inside these ranges and needn't reach their ends.
All inputs are finite; a program needn't handle non-finite values.
Results may differ from the reference program's by a relative error of at most 0.013.
Values may be sent and summed in bfloat16 or wider, within the bound.
No kernel may reach another device: no remote copies, remote signals or barrier semaphores. Data moves between devices by JAX's collectives and lax.ppermute only.
A program may use at most 128 MiB of HBM per device.

```python
import math
import jax
import jax.numpy as jnp
from jax import lax

D = 512
HEADS = 8
KERNEL = 31
MICS = 8
TIME = 1024


def block_scale(rng, shape, cuts, low, largest):
    level, own = 1.0, jax.random.fold_in(rng, 6)
    for axis_at, blocks in cuts:
        heights = jnp.exp(jax.random.uniform(jax.random.fold_in(own, axis_at), (blocks,), jnp.float32, low / len(cuts), largest / len(cuts)))
        level = level * jnp.repeat(heights, shape[axis_at] // blocks).reshape([-1 if axis == axis_at else 1 for axis in range(len(shape))])
    return level


def gaussian(own_key, extent, scale, most, pieces=(), kind=jnp.bfloat16):
    level = block_scale(own_key, extent, pieces, -0.22, 0.18) if pieces else 1.0
    entries = jax.random.normal(own_key, extent, jnp.float32) * scale * level
    return jnp.minimum(jnp.maximum(entries, -most), most).astype(kind)


def setup_inputs(seed: int = 0) -> dict:
    key_of = jax.random.split(jax.random.key(seed), 8)
    return {
        "frames": gaussian(key_of[0], (MICS, TIME, D), 1.0, 6.0, ((0, 4), (1, 8))),
        "cotangent": gaussian(key_of[1], (MICS, TIME, D), 1.0, 6.0, ((0, 4), (1, 8))),
        "kernel": gaussian(key_of[2], (KERNEL, D), KERNEL ** -0.5, 1.0, (), jnp.float32),
        "w_query": gaussian(key_of[3], (D, D), D ** -0.5, 0.25),
        "w_key": gaussian(key_of[4], (D, D), D ** -0.5, 0.25),
        "w_value": gaussian(key_of[5], (D, D), D ** -0.5, 0.25),
        "w_out": gaussian(key_of[6], (D, D), D ** -0.5, 0.25),
    }


def depthwise(padded, kernel, length):
    summed = jnp.zeros((padded.shape[0], length, padded.shape[2]), jnp.float32)
    for offset in range(kernel.shape[0]):
        summed = summed + padded[:, offset:offset + length, :].astype(jnp.float32) * kernel[offset]
    return summed

def transposed(padded, kernel, length):
    reach = kernel.shape[0] - 1
    summed = jnp.zeros((padded.shape[0], length, padded.shape[2]), jnp.float32)
    for offset in range(kernel.shape[0]):
        start = reach - offset
        summed = summed + padded[:, start:start + length, :] * kernel[offset]
    return summed

def kernel_terms(padded, gradient, taps):
    length = gradient.shape[1]
    rows_out = []
    for offset in range(taps):
        rows_out.append(lax.optimization_barrier(jnp.sum(padded[:, offset:offset + length, :].astype(jnp.float32) * gradient, axis=(0, 1))))
    return jnp.stack(rows_out)

def attend(queries, key_rows, value_rows, head_count):
    first, length, width = queries.shape
    others = key_rows.shape[0]
    depth = width // head_count
    factor = 1.0 / math.sqrt(depth)
    query_heads = queries.astype(jnp.float32).reshape(first, length, head_count, depth)
    key_heads = key_rows.astype(jnp.float32).reshape(others, length, head_count, depth)
    value_heads = value_rows.astype(jnp.float32).reshape(others, length, head_count, depth)
    scores = jnp.einsum('athe,bthe->abth', query_heads, key_heads) * factor
    weights = jnp.exp(scores)
    weights = weights / lax.optimization_barrier(jnp.sum(weights, axis=1, keepdims=True))
    mixed = jnp.einsum('abth,bthe->athe', weights, value_heads).reshape(first, length, width)
    return (mixed, weights)

def attend_back(queries, key_rows, value_rows, weights, upstream, head_count):
    first, length, width = queries.shape
    others = key_rows.shape[0]
    depth = width // head_count
    factor = 1.0 / math.sqrt(depth)
    query_heads = queries.astype(jnp.float32).reshape(first, length, head_count, depth)
    key_heads = key_rows.astype(jnp.float32).reshape(others, length, head_count, depth)
    value_heads = value_rows.astype(jnp.float32).reshape(others, length, head_count, depth)
    up_heads = upstream.astype(jnp.float32).reshape(first, length, head_count, depth)
    products = jnp.einsum('athe,bthe->abth', up_heads, value_heads)
    inner = weights * (products - lax.optimization_barrier(jnp.sum(weights * products, axis=1, keepdims=True))) * factor
    dquery = jnp.einsum('abth,bthe->athe', inner, key_heads).reshape(first, length, width)
    key_terms = jnp.einsum('abth,athe->bthe', inner, query_heads).reshape(others, length, width)
    value_terms = jnp.einsum('abth,athe->bthe', weights, up_heads).reshape(others, length, width)
    return (dquery, key_terms, value_terms)

def project(inputs, matrix):
    width = inputs.shape[-1]
    return jnp.dot(inputs.reshape(-1, width), matrix, preferred_element_type=jnp.float32).reshape(inputs.shape[:-1] + (matrix.shape[1],))

def outer(left, right):
    width = left.shape[-1]
    return jnp.dot(left.reshape(-1, width).T, right.reshape(-1, right.shape[-1]), preferred_element_type=jnp.float32)

def reference(frames, cotangent, kernel, w_query, w_key, w_value, w_out):
    reach = kernel.shape[0] // 2
    length = frames.shape[1]
    padded = jnp.pad(frames, ((0, 0), (reach, reach), (0, 0)))
    conv = depthwise(padded, kernel, length)
    acted = jax.nn.silu(conv).astype(jnp.bfloat16)
    queries = project(acted, w_query).astype(jnp.bfloat16)
    key_rows = project(acted, w_key).astype(jnp.bfloat16)
    value_rows = project(acted, w_value).astype(jnp.bfloat16)
    mixed, weights = attend(queries, key_rows, value_rows, HEADS)
    mixed = mixed.astype(jnp.bfloat16)
    layer_out = (frames.astype(jnp.float32) + project(mixed, w_out)).astype(jnp.bfloat16)
    upstream = project(cotangent, w_out.T).astype(jnp.bfloat16)
    out_term = outer(mixed, cotangent)
    dquery, key_terms, value_terms = attend_back(queries, key_rows, value_rows, weights, upstream, HEADS)
    dquery = dquery.astype(jnp.bfloat16)
    dkey = key_terms.astype(jnp.bfloat16)
    dvalue = value_terms.astype(jnp.bfloat16)
    dacted = project(dquery, w_query.T) + project(dkey, w_key.T) + project(dvalue, w_value.T)
    sig = jax.nn.sigmoid(conv)
    dconv = dacted * sig * (1.0 + conv * (1.0 - sig))
    grad_pad = jnp.pad(dconv, ((0, 0), (reach, reach), (0, 0)))
    frame_grad = (cotangent.astype(jnp.float32) + transposed(grad_pad, kernel, length)).astype(jnp.bfloat16)
    norm_factor = 1.0 / math.sqrt(frames.shape[0] * frames.shape[1])
    kernel_grad = kernel_terms(padded, dconv, kernel.shape[0]) * norm_factor
    query_grad = outer(acted, dquery) * norm_factor
    key_grad = outer(acted, dkey) * norm_factor
    value_grad = outer(acted, dvalue) * norm_factor
    out_grad = out_term * norm_factor
    return (layer_out, frame_grad, kernel_grad, query_grad, key_grad, value_grad, out_grad)
```

```python
import functools
import math

import jax
import jax.numpy as jnp
from jax import lax
from jax.experimental import pallas as pl
from jax.experimental.pallas import tpu as pltpu
from jax.sharding import PartitionSpec as P

HEADS = 8
LANES = 128
HALO = 16
NT = (((1,), (1,)), ((), ()))
TN = (((0,), (0,)), ((), ()))
BF = jnp.bfloat16
F32 = jnp.float32
VMEM_LIMIT = 56 * 1024 * 1024


def mm(left, right, dims=(((1,), (0,)), ((), ()))):
    return lax.dot_general(left, right, dims, preferred_element_type=F32)


def rolled(x, shift):
    return x if shift == 0 else pltpu.roll(x, x.shape[0] - shift, axis=0)


def window(x, taps, rows):
    acc = None
    for r in range(8):
        xr = rolled(x, r)
        for k in range(4):
            o = 8 * k + r
            if o == 0:
                continue
            term = xr[8 * k : 8 * k + rows] * taps(o)
            acc = term if acc is None else acc + term
    return acc


def main_kernel(
    plan, got, before, after, kern, wq, wk, wv, wo, back, packed,
    conv_s, act_s, cot_s, q_s, k_s, v_s, u_s, mix_s, dq_s, dk_s, dv_s, dconv_s, tap_s,
):
    groups, count, sub, width, chunks, factor = plan
    mics = groups * count
    cuts = sub // HALO
    block = mics * HALO
    cols = width // LANES

    def frames_window(a, m, lanes):
        return jnp.concatenate(
            [before[a, m, :, lanes], got[a, 0, m, :, lanes], after[a, m, :, lanes]], axis=0
        ).astype(F32)

    def conv_step(n, _):
        a, m = n // count, n % count
        for lc in range(cols):
            lanes = slice(lc * LANES, (lc + 1) * LANES)
            conv = window(
                frames_window(a, m, lanes), lambda o: kern[o - 1 : o, lanes], sub
            )
            acted = (conv * jax.nn.sigmoid(conv)).astype(BF)
            for c in range(cuts):
                at = pl.multiple_of(c * block + n * HALO, HALO)
                conv_s[pl.ds(at, HALO), lanes] = conv[c * HALO : (c + 1) * HALO]
                act_s[pl.ds(at, HALO), lanes] = acted[c * HALO : (c + 1) * HALO]
        for c in range(cuts):
            at = pl.multiple_of(c * block + n * HALO, HALO)
            cot_s[pl.ds(at, HALO), :] = got[a, 1, m, c * HALO : (c + 1) * HALO, :]
        return 0

    lax.fori_loop(0, mics, conv_step, 0)
    acted = act_s[...]
    cot = cot_s[...]
    q_s[...] = mm(acted, wq[...]).astype(BF)
    k_s[...] = mm(acted, wk[...]).astype(BF)
    v_s[...] = mm(acted, wv[...]).astype(BF)
    u_s[...] = mm(cot, wo[...], NT).astype(BF)

    depth = width // HEADS
    per = LANES // depth
    lane = lax.broadcasted_iota(jnp.int32, (block, LANES), 1)
    row_i = lax.broadcasted_iota(jnp.int32, (block, per * block), 0)
    col_i = lax.broadcasted_iota(jnp.int32, (block, per * block), 1)
    same = (row_i % HALO) == (col_i % HALO)

    def by_head(x):
        return jnp.concatenate(
            [jnp.where(lane // depth == h, x, jnp.zeros_like(x)) for h in range(per)], axis=0
        )

    def sums(x):
        return [
            jnp.sum(x[:, h * block : (h + 1) * block], axis=1, keepdims=True) for h in range(per)
        ]

    def each(x, values, op):
        return jnp.concatenate(
            [op(x[:, h * block : (h + 1) * block], values[h]) for h in range(per)], axis=1
        )

    def pick(x):
        out = x[:block]
        for h in range(1, per):
            out = jnp.where(lane // depth == h, x[h * block : (h + 1) * block], out)
        return out

    for c in range(cuts):
        rows = slice(c * block, (c + 1) * block)
        for p in range(cols):
            lanes = slice(p * LANES, (p + 1) * LANES)
            q, u = q_s[rows, lanes], u_s[rows, lanes]
            kc, vc = by_head(k_s[rows, lanes]), by_head(v_s[rows, lanes])
            e = jnp.where(same, jnp.exp(mm(q, kc, NT) * factor), 0.0)
            w = each(e, sums(e), lambda x, s: x / s)
            up = mm(u, vc, NT)
            wup = w * up
            inner = each(up, sums(wup), lambda x, s: x - s) * w * factor
            wb, ib = w.astype(BF), inner.astype(BF)
            mix_s[rows, lanes] = mm(wb, vc).astype(BF)
            dq_s[rows, lanes] = mm(ib, kc).astype(BF)
            dk_s[rows, lanes] = pick(mm(ib, q, TN)).astype(BF)
            dv_s[rows, lanes] = pick(mm(wb, u, TN)).astype(BF)

    dacted = mm(dq_s[...], wq[...], NT) + mm(dk_s[...], wk[...], NT) + mm(dv_s[...], wv[...], NT)
    conv = conv_s[...]
    sig = jax.nn.sigmoid(conv)
    dconv_s[...] = dacted * sig * (1.0 + conv * (1.0 - sig))
    proj = mm(mix_s[...], wo[...])
    for n in range(mics):
        a, m = n // count, n % count
        for c in range(cuts):
            at = c * block + n * HALO
            part = slice(c * HALO, (c + 1) * HALO)
            back[a, 0, m, part, :] = (
                got[a, 0, m, part, :].astype(F32) + proj[at : at + HALO]
            ).astype(BF)
            back[a, 1, m, part, :] = dconv_s[at : at + HALO, :].astype(BF)

    per_chunk = 4 * cols * width // chunks
    act_t = acted.T
    mix_t = mix_s[...].T
    for i, (left, right) in enumerate(
        ((act_t, dq_s), (act_t, dk_s), (act_t, dv_s), (mix_t, cot_s))
    ):
        grad = mm(left, right[...]).astype(BF)
        for cb in range(cols):
            for at in range(0, width, per_chunk):
                g = ((i * cols + cb) * width + at) // per_chunk
                packed[g, 0:per_chunk, :] = grad[at : at + per_chunk, cb * LANES : (cb + 1) * LANES]

    for lc in range(cols):
        lanes = slice(lc * LANES, (lc + 1) * LANES)

        def tap_step(n, accs):
            a, m = n // count, n % count
            x = frames_window(a, m, lanes)
            d = jnp.concatenate(
                [
                    dconv_s[pl.ds(pl.multiple_of(c * block + n * HALO, HALO), HALO), lanes]
                    for c in range(cuts)
                ],
                axis=0,
            )
            out = list(accs)
            for r in range(8):
                xr = rolled(x, r)
                for k in range(4):
                    o = 8 * k + r
                    if o == 0:
                        continue
                    prod = xr[8 * k : 8 * k + sub] * d
                    out[o - 1] = out[o - 1] + jnp.sum(prod.reshape(sub // 8, 8, LANES), axis=0)
            return tuple(out)

        accs = lax.fori_loop(0, mics, tap_step, tuple(jnp.zeros((8, LANES), F32) for _ in range(31)))
        tap_s[lc * 32 : lc * 32 + 32, :] = jnp.concatenate(
            [jnp.sum(x, axis=0, keepdims=True) for x in accs] + [jnp.zeros((1, LANES), F32)], axis=0
        )

    tap_rows = max(1, cols * 32 // chunks)
    for g in range(chunks):
        tail = jnp.zeros((HALO, LANES), F32)
        if g * tap_rows < cols * 32:
            tail = jnp.concatenate(
                [tap_s[g * tap_rows : (g + 1) * tap_rows, :], tail[tap_rows:]], axis=0
            )
        packed[g, per_chunk : per_chunk + HALO, :] = tail.astype(BF)


def final_kernel(plan, got, taps, *outs):
    chunks, width, norm, order = plan
    cols = width // LANES
    per_chunk = 4 * cols * width // chunks
    tap_rows = max(1, cols * 32 // chunks)
    for f in range(chunks):
        g = order[f]
        flat = g * per_chunk
        i, cb, at = flat // (cols * width), (flat // width) % cols, flat % width
        outs[i][at : at + per_chunk, cb * LANES : (cb + 1) * LANES] = (
            got[f, 0:per_chunk, :].astype(F32) * norm
        )
        row = g * tap_rows
        if row < cols * 32:
            lc, j = row // 32, row % 32
            kept = min(tap_rows, 31 - j)
            if kept > 0:
                tail = got[f, per_chunk : per_chunk + HALO, :].astype(F32) * norm
                taps[j : j + kept, lc * LANES : (lc + 1) * LANES] = tail[0:kept]


def frame_kernel(plan, got, before, after, cot, kern, layer_out, frame_grad):
    groups, count, sub, width = plan
    cols = width // LANES

    def edge(a, m, lanes):
        first = before[m, :, lanes] if a == 0 else got[a - 1, 1, m, sub - HALO :, lanes]
        last = after[m, :, lanes] if a == groups - 1 else got[a + 1, 1, m, :HALO, lanes]
        return jnp.concatenate([first, got[a, 1, m, :, lanes], last], axis=0).astype(F32)

    def step(m, _):
        for a in range(groups):
            part = slice(a * sub, (a + 1) * sub)
            layer_out[m, part, :] = got[a, 0, m, :, :]
            for lc in range(cols):
                lanes = slice(lc * LANES, (lc + 1) * LANES)
                total = window(edge(a, m, lanes), lambda o: kern[31 - o : 32 - o, lanes], sub)
                frame_grad[m, part, lanes] = (cot[m, part, lanes].astype(F32) + total).astype(BF)
        return 0

    lax.fori_loop(0, count, step, 0)


def call(body, outs, scratch, *args):
    return pl.pallas_call(
        body,
        out_shape=outs,
        in_specs=[pl.BlockSpec(memory_space=pltpu.VMEM)] * len(args),
        out_specs=jax.tree.map(lambda _: pl.BlockSpec(memory_space=pltpu.VMEM), outs),
        scratch_shapes=scratch,
        compiler_params=pltpu.CompilerParams(vmem_limit_bytes=VMEM_LIMIT),
    )(*args)


def neighbours(groups, blocks):
    def flat(s):
        return (s % groups) * blocks + s // groups

    return [(flat(s), flat(s + 1)) for s in range(groups * blocks - 1)]


def summed_over(x, groups, size):
    got = lax.all_to_all(
        x.reshape(size, x.shape[0] // size, *x.shape[1:]),
        ("mic", "tm"), 0, 0, tiled=True, axis_index_groups=groups,
    )
    return jnp.sum(got.astype(F32), axis=0).astype(BF)


def shards(frames, cotangent, kernel, w_query, w_key, w_value, w_out):
    groups, blocks = lax.axis_size("mic"), lax.axis_size("tm")
    count, length, width = frames.shape
    sub = length // groups
    chunks = groups * blocks
    rows = groups * count * sub
    shape = jax.ShapeDtypeStruct

    send = jnp.stack([frames, cotangent]).reshape(2, count, groups, sub, width)
    got = lax.all_to_all(send.transpose(2, 0, 1, 3, 4), "mic", 0, 0, tiled=True)
    up = neighbours(groups, blocks)
    down = [(j, i) for i, j in up]
    before = lax.ppermute(got[:, 0, :, sub - HALO :, :], ("mic", "tm"), up)
    after = lax.ppermute(got[:, 0, :, :HALO, :], ("mic", "tm"), down)

    factor = 1.0 / math.sqrt(width // HEADS)
    per_chunk = 4 * width * width // LANES // chunks
    big = pltpu.VMEM((rows, width), BF)
    wide = pltpu.VMEM((rows, width), F32)
    back, packed = call(
        functools.partial(main_kernel, (groups, count, sub, width, chunks, factor)),
        (
            shape((groups, 2, count, sub, width), BF),
            shape((chunks, per_chunk + HALO, LANES), BF),
        ),
        [wide] + [big] * 10 + [wide, pltpu.VMEM((32 * width // LANES, LANES), F32)],
        got, before, after, kernel, w_query, w_key, w_value, w_out,
    )

    cores, xs = 2, 2
    ys, zs = groups // cores, blocks // xs

    def device(y, core, z, x):
        return ((y * cores + core) * zs + z) * xs + x

    over_core = [
        [device(y, core, z, x) for core in range(cores)]
        for y in range(ys) for z in range(zs) for x in range(xs)
    ]
    over_plane = [
        [device(y, core, z, x) for y in range(ys) for x in range(xs)]
        for core in range(cores) for z in range(zs)
    ]
    over_line = [
        [device(y, core, z, x) for z in range(zs)]
        for y in range(ys) for core in range(cores) for x in range(xs)
    ]
    order = [0] * chunks
    for y in range(ys):
        for core in range(cores):
            for z in range(zs):
                for x in range(xs):
                    order[device(y, core, z, x)] = ((core * ys + y) * xs + x) * zs + z
    part = summed_over(packed, over_core, cores)
    part = summed_over(part, over_plane, ys * xs)
    part = summed_over(part, over_line, zs)
    whole = lax.all_gather(part[0], ("mic", "tm"), axis=0, tiled=False)

    home = lax.all_to_all(back, "mic", 0, 0, tiled=True)
    up = [(i, i + 1) for i in range(blocks - 1)]
    down = [(j, i) for i, j in up]
    before = lax.ppermute(home[groups - 1, 1, :, sub - HALO :, :], "tm", up)
    after = lax.ppermute(home[0, 1, :, :HALO, :], "tm", down)
    layer_out, frame_grad = call(
        functools.partial(frame_kernel, (groups, count, sub, width)),
        (shape((count, length, width), BF), shape((count, length, width), BF)),
        [], home, before, after, cotangent, kernel,
    )
    norm = 1.0 / math.sqrt(groups * count * blocks * length)
    square = shape((width, width), F32)
    grads = call(
        functools.partial(final_kernel, (chunks, width, norm, order)),
        (shape((31, width), F32), square, square, square, square),
        [], whole,
    )
    return (layer_out, frame_grad, *grads)


def solution(mesh):
    in_specs = (P("mic", "tm", None), P("mic", "tm", None), P(), P(), P(), P(), P())
    out_specs = (P("mic", "tm", None), P("mic", "tm", None), P(), P(), P(), P(), P())
    return jax.shard_map(shards, mesh=mesh, in_specs=in_specs, out_specs=out_specs, check_vma=False)
```

```python
import functools
import math

import jax
import jax.numpy as jnp
from jax import lax
from jax.experimental import pallas as pl
from jax.experimental.pallas import tpu as pltpu
from jax.sharding import PartitionSpec as P

HEADS = 8
LANES = 128
HALO = 16
NT = (((1,), (1,)), ((), ()))
TN = (((0,), (0,)), ((), ()))
BF = jnp.bfloat16
F32 = jnp.float32
VMEM_LIMIT = 56 * 1024 * 1024


def mm(left, right, dims=(((1,), (0,)), ((), ()))):
    return lax.dot_general(left, right, dims, preferred_element_type=F32)


def rolled(x, shift):
    return x if shift == 0 else pltpu.roll(x, x.shape[0] - shift, axis=0)


def window(x, taps, rows):
    acc = None
    for r in range(8):
        xr = rolled(x, r)
        for k in range(4):
            o = 8 * k + r
            if o == 0:
                continue
            term = xr[8 * k : 8 * k + rows] * taps(o)
            acc = term if acc is None else acc + term
    return acc


def main_kernel(
    plan, bits, got, before, after, kern, wq, wk, wv, wo, back, keep, send,
    conv_s, left_s, right_s, q_s, k_s, v_s, u_s, dconv_s, tap_s,
):
    groups, count, sub, width, factor = plan
    act_s, mix_s = left_s.at[0], left_s.at[1]
    dq_s, dk_s, dv_s, cot_s = (right_s.at[i] for i in range(4))
    mics = groups * count
    cuts = sub // HALO
    block = mics * HALO
    cols = width // LANES

    def frames_window(a, m, lanes):
        return jnp.concatenate(
            [before[a, m, :, lanes], got[a, 0, m, :, lanes], after[a, m, :, lanes]], axis=0
        ).astype(F32)

    def conv_step(n, _):
        a, m = n // count, n % count
        for lc in range(cols):
            lanes = slice(lc * LANES, (lc + 1) * LANES)
            conv = window(
                frames_window(a, m, lanes), lambda o: kern[o - 1 : o, lanes], sub
            )
            acted = (conv * jax.nn.sigmoid(conv)).astype(BF)
            for c in range(cuts):
                at = pl.multiple_of(c * block + n * HALO, HALO)
                conv_s[pl.ds(at, HALO), lanes] = conv[c * HALO : (c + 1) * HALO]
                act_s[pl.ds(at, HALO), lanes] = acted[c * HALO : (c + 1) * HALO]
        for c in range(cuts):
            at = pl.multiple_of(c * block + n * HALO, HALO)
            cot_s[pl.ds(at, HALO), :] = got[a, 1, m, c * HALO : (c + 1) * HALO, :]
        return 0

    lax.fori_loop(0, mics, conv_step, 0)
    acted = act_s[...]
    cot = cot_s[...]
    q_s[...] = mm(acted, wq[...]).astype(BF)
    k_s[...] = mm(acted, wk[...]).astype(BF)
    v_s[...] = mm(acted, wv[...]).astype(BF)
    u_s[...] = mm(cot, wo[...], NT).astype(BF)

    depth = width // HEADS
    per = LANES // depth
    lane = lax.broadcasted_iota(jnp.int32, (block, LANES), 1)
    row_i = lax.broadcasted_iota(jnp.int32, (block, per * block), 0)
    col_i = lax.broadcasted_iota(jnp.int32, (block, per * block), 1)
    same = (row_i % HALO) == (col_i % HALO)

    def by_head(x):
        return jnp.concatenate(
            [jnp.where(lane // depth == h, x, jnp.zeros_like(x)) for h in range(per)], axis=0
        )

    def sums(x):
        return [
            jnp.sum(x[:, h * block : (h + 1) * block], axis=1, keepdims=True) for h in range(per)
        ]

    def each(x, values, op):
        return jnp.concatenate(
            [op(x[:, h * block : (h + 1) * block], values[h]) for h in range(per)], axis=1
        )

    def pick(x):
        out = x[:block]
        for h in range(1, per):
            out = jnp.where(lane // depth == h, x[h * block : (h + 1) * block], out)
        return out

    for c in range(cuts):
        rows = slice(c * block, (c + 1) * block)
        for p in range(cols):
            lanes = slice(p * LANES, (p + 1) * LANES)
            q, u = q_s[rows, lanes], u_s[rows, lanes]
            kc, vc = by_head(k_s[rows, lanes]), by_head(v_s[rows, lanes])
            e = jnp.where(same, jnp.exp(mm(q, kc, NT) * factor), 0.0)
            w = each(e, sums(e), lambda x, s: x / s)
            up = mm(u, vc, NT)
            wup = w * up
            inner = each(up, sums(wup), lambda x, s: x - s) * w * factor
            wb, ib = w.astype(BF), inner.astype(BF)
            mix_s[rows, lanes] = mm(wb, vc).astype(BF)
            dq_s[rows, lanes] = mm(ib, kc).astype(BF)
            dk_s[rows, lanes] = pick(mm(ib, q, TN)).astype(BF)
            dv_s[rows, lanes] = pick(mm(wb, u, TN)).astype(BF)

    dacted = mm(dq_s[...], wq[...], NT) + mm(dk_s[...], wk[...], NT) + mm(dv_s[...], wv[...], NT)
    conv = conv_s[...]
    sig = jax.nn.sigmoid(conv)
    dconv_s[...] = dacted * sig * (1.0 + conv * (1.0 - sig))
    proj = mm(mix_s[...], wo[...])
    for n in range(mics):
        a, m = n // count, n % count
        for c in range(cuts):
            at = c * block + n * HALO
            part = slice(c * HALO, (c + 1) * HALO)
            back[a, 0, m, part, :] = (
                got[a, 0, m, part, :].astype(F32) + proj[at : at + HALO]
            ).astype(BF)
            back[a, 1, m, part, :] = dconv_s[at : at + HALO, :].astype(BF)

    for lc in range(cols):
        lanes = slice(lc * LANES, (lc + 1) * LANES)

        def tap_step(n, accs):
            a, m = n // count, n % count
            x = frames_window(a, m, lanes)
            d = jnp.concatenate(
                [
                    dconv_s[pl.ds(pl.multiple_of(c * block + n * HALO, HALO), HALO), lanes]
                    for c in range(cuts)
                ],
                axis=0,
            )
            out = list(accs)
            for r in range(8):
                xr = rolled(x, r)
                for k in range(4):
                    o = 8 * k + r
                    if o == 0:
                        continue
                    prod = xr[8 * k : 8 * k + sub] * d
                    out[o - 1] = out[o - 1] + jnp.sum(prod.reshape(sub // 8, 8, LANES), axis=0)
            return tuple(out)

        accs = lax.fori_loop(0, mics, tap_step, tuple(jnp.zeros((8, LANES), F32) for _ in range(31)))
        tap_s[lc * 32 : lc * 32 + 32, :] = jnp.concatenate(
            [jnp.sum(x, axis=0, keepdims=True) for x in accs] + [jnp.zeros((1, LANES), F32)], axis=0
        )

    tap_s[cols * 32 :, :] = jnp.zeros((HALO, LANES), F32)
    core = bits[0]
    size = cols * width // 8
    tap_rows = cols
    for out, owner in ((keep, core), (send, 1 - core)):
        for h in range(2):
            i = owner * 2 + h
            grad = mm(left_s[i // 3], right_s[i], TN).astype(BF)
            for piece in range(8):
                flat = piece * size
                cb, at = flat // width, flat % width
                tail = tap_s[pl.ds(pl.multiple_of((i * 8 + piece) * tap_rows, tap_rows), HALO), :]
                out[h, piece // 4, piece // 2 % 2, piece % 2, 0:size, :] = grad[
                    at : at + size, cb * LANES : (cb + 1) * LANES
                ]
                out[h, piece // 4, piece // 2 % 2, piece % 2, size : size + HALO, :] = tail.astype(BF)


def add(left, right):
    return (left.astype(F32) + right.astype(F32)).astype(BF)


def split_core(bits, keep, got, a_keep, a_send, b_keep, b_send):
    y, x = bits[1], bits[2]
    for h, bit, mine, theirs in ((0, x, a_keep, a_send), (1, y, b_keep, b_send)):
        theirs[...] = add(keep[h, 1 - bit], got[h, 1 - bit])
        mine[...] = add(keep[h, bit], got[h, bit])


def split_plane(which, bits, keep, got, mine, theirs):
    bit = bits[which]
    theirs[...] = add(keep[1 - bit], got[1 - bit])
    mine[...] = add(keep[bit], got[bit])


def split_line(bits, a_keep, a_got, b_keep, b_got, mine, theirs):
    bit = bits[3]
    for h, keep, got in ((0, a_keep, a_got), (1, b_keep, b_got)):
        theirs[h] = add(keep[1 - bit], got[1 - bit])
        mine[h] = add(keep[bit], got[bit])


def final_kernel(plan, bits, own, far, other_own, other_far, taps, *refs):
    width, norm = plan
    outs, tap_s = refs[:4], refs[4]
    cols = width // LANES
    size = cols * width // 8
    core, y, x, z = bits[0], bits[1], bits[2], bits[3]

    def emit(which, near, across):
        for h in range(2):
            i = 2 * which + h
            first, second = (x, y) if h == 0 else (y, x)
            for b1 in range(2):
                for b2 in range(2):
                    for b3 in range(2):
                        part = (near, across)[b1]
                        piece = (first ^ b1) * 4 + (second ^ b2) * 2 + (z ^ b3)
                        flat = piece * size
                        cb, at = flat // width, flat % width
                        outs[i][
                            pl.ds(pl.multiple_of(at, size), size),
                            pl.ds(pl.multiple_of(cb * LANES, LANES), LANES),
                        ] = part[h, b2, b3, 0:size, :].astype(F32) * norm
                        tap_s[i * 8 + piece] = part[h, b2, b3, size : size + HALO, :].astype(F32) * norm

    for which in range(2):
        @pl.when(core == which)
        def _():
            emit(which, own, far)
            emit(1 - which, other_own, other_far)

    for g in range(32):
        row = g * cols
        lc, j = row // 32, row % 32
        kept = min(cols, 31 - j)
        taps[j : j + kept, lc * LANES : (lc + 1) * LANES] = tap_s[g, 0:kept]


def frame_kernel(plan, got, before, after, cot, kern, layer_out, frame_grad):
    groups, count, sub, width = plan
    cols = width // LANES

    def edge(a, m, lanes):
        first = before[m, :, lanes] if a == 0 else got[a - 1, 1, m, sub - HALO :, lanes]
        last = after[m, :, lanes] if a == groups - 1 else got[a + 1, 1, m, :HALO, lanes]
        return jnp.concatenate([first, got[a, 1, m, :, lanes], last], axis=0).astype(F32)

    def step(m, _):
        for a in range(groups):
            part = slice(a * sub, (a + 1) * sub)
            layer_out[m, part, :] = got[a, 0, m, :, :]
            for lc in range(cols):
                lanes = slice(lc * LANES, (lc + 1) * LANES)
                total = window(edge(a, m, lanes), lambda o: kern[31 - o : 32 - o, lanes], sub)
                frame_grad[m, part, lanes] = (cot[m, part, lanes].astype(F32) + total).astype(BF)
        return 0

    lax.fori_loop(0, count, step, 0)


def call(body, outs, scratch, *args):
    return pl.pallas_call(
        body,
        out_shape=outs,
        in_specs=[
            pl.BlockSpec(memory_space=pltpu.SMEM if x.dtype == jnp.int32 else pltpu.VMEM)
            for x in args
        ],
        out_specs=jax.tree.map(lambda _: pl.BlockSpec(memory_space=pltpu.VMEM), outs),
        scratch_shapes=scratch,
        compiler_params=pltpu.CompilerParams(vmem_limit_bytes=VMEM_LIMIT),
    )(*args)


def neighbours(groups, blocks):
    def flat(s):
        return (s % groups) * blocks + s // groups

    return [(flat(s), flat(s + 1)) for s in range(groups * blocks - 1)]


def shards(frames, cotangent, kernel, w_query, w_key, w_value, w_out):
    groups, blocks = lax.axis_size("mic"), lax.axis_size("tm")
    count, length, width = frames.shape
    sub = length // groups
    rows = groups * count * sub
    shape = jax.ShapeDtypeStruct

    send = jnp.stack([frames, cotangent]).reshape(2, count, groups, sub, width)
    got = lax.all_to_all(send.transpose(2, 0, 1, 3, 4), "mic", 0, 0, tiled=True)
    up = neighbours(groups, blocks)
    down = [(j, i) for i, j in up]
    before = lax.ppermute(got[:, 0, :, sub - HALO :, :], ("mic", "tm"), up)
    after = lax.ppermute(got[:, 0, :, :HALO, :], ("mic", "tm"), down)

    mic, tm = lax.axis_index("mic"), lax.axis_index("tm")
    bits = jnp.stack([mic % 2, mic // 2, tm % 2, tm // 2 % 2]).astype(jnp.int32)
    over_core, over_y, over_x, over_z = blocks, 2 * blocks, 1, 2

    def swap(x, mask):
        return lax.ppermute(x, ("mic", "tm"), [(f, f ^ mask) for f in range(groups * blocks)])

    factor = 1.0 / math.sqrt(width // HEADS)
    piece = (width * width // LANES // 8 + HALO, LANES)
    big = pltpu.VMEM((rows, width), BF)
    wide = pltpu.VMEM((rows, width), F32)
    halves = shape((2, 2, 2, 2, *piece), BF)
    back, keep, send = call(
        functools.partial(main_kernel, (groups, count, sub, width, factor)),
        (shape((groups, 2, count, sub, width), BF), halves, halves),
        [
            wide, pltpu.VMEM((2, rows, width), BF), pltpu.VMEM((4, rows, width), BF),
            big, big, big, big, wide, pltpu.VMEM((32 * width // LANES + HALO, LANES), F32),
        ],
        bits, got, before, after, kernel, w_query, w_key, w_value, w_out,
    )

    quarter, eighth, pair = (shape((*lead, *piece), BF) for lead in ((2, 2), (2,), (2,)))
    a_keep, a_send, b_keep, b_send = call(
        split_core, (quarter,) * 4, [], bits, keep, swap(send, over_core)
    )
    a_got, b_got = swap(a_send, over_x), swap(b_send, over_y)
    a_keep, a_send = call(
        functools.partial(split_plane, 1), (eighth,) * 2, [], bits, a_keep, a_got
    )
    b_keep, b_send = call(
        functools.partial(split_plane, 2), (eighth,) * 2, [], bits, b_keep, b_got
    )
    a_got, b_got = swap(a_send, over_y), swap(b_send, over_x)
    mine, theirs = call(split_line, (pair,) * 2, [], bits, a_keep, a_got, b_keep, b_got)
    mine = add(mine, swap(theirs, over_z))
    mask = 2 * over_z
    while mask < blocks:
        mine = add(mine, swap(mine, mask))
        mask *= 2
    line = jnp.stack([mine, swap(mine, over_z)], axis=1)
    plane = jnp.stack([line, jnp.stack([swap(line[0], over_y), swap(line[1], over_x)])], axis=1)
    other_plane = swap(plane, over_core)
    far = jnp.stack([swap(plane[0], over_x), swap(plane[1], over_y)])
    other_far = swap(far, over_core)

    home = lax.all_to_all(back, "mic", 0, 0, tiled=True)
    up = [(i, i + 1) for i in range(blocks - 1)]
    down = [(j, i) for i, j in up]
    before = lax.ppermute(home[groups - 1, 1, :, sub - HALO :, :], "tm", up)
    after = lax.ppermute(home[0, 1, :, :HALO, :], "tm", down)
    layer_out, frame_grad = call(
        functools.partial(frame_kernel, (groups, count, sub, width)),
        (shape((count, length, width), BF), shape((count, length, width), BF)),
        [], home, before, after, cotangent, kernel,
    )
    norm = 1.0 / math.sqrt(groups * count * blocks * length)
    square = shape((width, width), F32)
    grads = call(
        functools.partial(final_kernel, (width, norm)),
        (shape((31, width), F32), square, square, square, square),
        [pltpu.VMEM((32, HALO, LANES), F32)],
        bits, plane, far, other_plane, other_far,
    )
    return (layer_out, frame_grad, *grads)


def solution(mesh):
    in_specs = (P("mic", "tm", None), P("mic", "tm", None), P(), P(), P(), P(), P())
    out_specs = (P("mic", "tm", None), P("mic", "tm", None), P(), P(), P(), P(), P())
    return jax.shard_map(shards, mesh=mesh, in_specs=in_specs, out_specs=out_specs, check_vma=False)
```

```python
import functools
import math

import jax
import jax.numpy as jnp
from jax import lax
from jax.experimental import pallas as pl
from jax.experimental.pallas import tpu as pltpu
from jax.sharding import PartitionSpec as P

HEADS = 8
LANES = 128
HALO = 16
NT = (((1,), (1,)), ((), ()))
TN = (((0,), (0,)), ((), ()))
BF = jnp.bfloat16
F32 = jnp.float32
MIB = 1024 * 1024


def mm(left, right, dims=(((1,), (0,)), ((), ()))):
    return lax.dot_general(left, right, dims, preferred_element_type=F32)


def rolled(x, shift):
    return x if shift == 0 else pltpu.roll(x, x.shape[0] - shift, axis=0)


def window(x, taps, rows):
    acc = None
    for r in range(8):
        xr = rolled(x, r)
        for k in range(4):
            o = 8 * k + r
            if o == 0:
                continue
            term = xr[8 * k : 8 * k + rows] * taps(o)
            acc = term if acc is None else acc + term
    return acc


def main_kernel(
    plan, bits, got, before, after, kern, wq, wk, wv, wo, back, keep, send,
    conv_s, left_s, right_s, q_s, k_s, v_s, u_s, dconv_s, tap_s,
):
    groups, count, sub, width, factor = plan
    act_s, mix_s = left_s.at[0], left_s.at[1]
    dq_s, dk_s, dv_s, cot_s = (right_s.at[i] for i in range(4))
    mics = groups * count
    cuts = sub // HALO
    block = mics * HALO
    cols = width // LANES

    def frames_window(a, m, lanes):
        return jnp.concatenate(
            [before[a, m, :, lanes], got[a, 0, m, :, lanes], after[a, m, :, lanes]], axis=0
        ).astype(F32)

    def conv_step(n, _):
        a, m = n // count, n % count
        for lc in range(cols):
            lanes = slice(lc * LANES, (lc + 1) * LANES)
            conv = window(
                frames_window(a, m, lanes), lambda o: kern[o - 1 : o, lanes], sub
            )
            acted = (conv * jax.nn.sigmoid(conv)).astype(BF)
            for c in range(cuts):
                at = pl.multiple_of(c * block + n * HALO, HALO)
                conv_s[pl.ds(at, HALO), lanes] = conv[c * HALO : (c + 1) * HALO]
                act_s[pl.ds(at, HALO), lanes] = acted[c * HALO : (c + 1) * HALO]
        for c in range(cuts):
            at = pl.multiple_of(c * block + n * HALO, HALO)
            cot_s[pl.ds(at, HALO), :] = got[a, 1, m, c * HALO : (c + 1) * HALO, :]
        return 0

    lax.fori_loop(0, mics, conv_step, 0)
    acted = act_s[...]
    cot = cot_s[...]
    q_s[...] = mm(acted, wq[...]).astype(BF)
    k_s[...] = mm(acted, wk[...]).astype(BF)
    v_s[...] = mm(acted, wv[...]).astype(BF)
    u_s[...] = mm(cot, wo[...], NT).astype(BF)

    depth = width // HEADS
    per = LANES // depth
    lane = lax.broadcasted_iota(jnp.int32, (block, LANES), 1)
    row_i = lax.broadcasted_iota(jnp.int32, (block, per * block), 0)
    col_i = lax.broadcasted_iota(jnp.int32, (block, per * block), 1)
    same = (row_i % HALO) == (col_i % HALO)

    def by_head(x):
        return jnp.concatenate(
            [jnp.where(lane // depth == h, x, jnp.zeros_like(x)) for h in range(per)], axis=0
        )

    def sums(x):
        return [
            jnp.sum(x[:, h * block : (h + 1) * block], axis=1, keepdims=True) for h in range(per)
        ]

    def each(x, values, op):
        return jnp.concatenate(
            [op(x[:, h * block : (h + 1) * block], values[h]) for h in range(per)], axis=1
        )

    def pick(x):
        out = x[:block]
        for h in range(1, per):
            out = jnp.where(lane // depth == h, x[h * block : (h + 1) * block], out)
        return out

    for c in range(cuts):
        rows = slice(c * block, (c + 1) * block)
        for p in range(cols):
            lanes = slice(p * LANES, (p + 1) * LANES)
            q, u = q_s[rows, lanes], u_s[rows, lanes]
            kc, vc = by_head(k_s[rows, lanes]), by_head(v_s[rows, lanes])
            e = jnp.where(same, jnp.exp(mm(q, kc, NT) * factor), 0.0)
            w = each(e, sums(e), lambda x, s: x / s)
            up = mm(u, vc, NT)
            wup = w * up
            inner = each(up, sums(wup), lambda x, s: x - s) * w * factor
            wb, ib = w.astype(BF), inner.astype(BF)
            mix_s[rows, lanes] = mm(wb, vc).astype(BF)
            dq_s[rows, lanes] = mm(ib, kc).astype(BF)
            dk_s[rows, lanes] = pick(mm(ib, q, TN)).astype(BF)
            dv_s[rows, lanes] = pick(mm(wb, u, TN)).astype(BF)

    dacted = mm(dq_s[...], wq[...], NT) + mm(dk_s[...], wk[...], NT) + mm(dv_s[...], wv[...], NT)
    conv = conv_s[...]
    sig = jax.nn.sigmoid(conv)
    dconv_s[...] = dacted * sig * (1.0 + conv * (1.0 - sig))
    proj = mm(mix_s[...], wo[...])
    for n in range(mics):
        a, m = n // count, n % count
        for c in range(cuts):
            at = c * block + n * HALO
            part = slice(c * HALO, (c + 1) * HALO)
            back[a, 0, m, part, :] = (
                got[a, 0, m, part, :].astype(F32) + proj[at : at + HALO]
            ).astype(BF)
            back[a, 1, m, part, :] = dconv_s[at : at + HALO, :].astype(BF)

    for lc in range(cols):
        lanes = slice(lc * LANES, (lc + 1) * LANES)

        def tap_step(n, accs):
            a, m = n // count, n % count
            x = frames_window(a, m, lanes)
            d = jnp.concatenate(
                [
                    dconv_s[pl.ds(pl.multiple_of(c * block + n * HALO, HALO), HALO), lanes]
                    for c in range(cuts)
                ],
                axis=0,
            )
            out = list(accs)
            for r in range(8):
                xr = rolled(x, r)
                for k in range(4):
                    o = 8 * k + r
                    if o == 0:
                        continue
                    prod = xr[8 * k : 8 * k + sub] * d
                    out[o - 1] = out[o - 1] + jnp.sum(prod.reshape(sub // 8, 8, LANES), axis=0)
            return tuple(out)

        accs = lax.fori_loop(0, mics, tap_step, tuple(jnp.zeros((8, LANES), F32) for _ in range(31)))
        tap_s[lc * 32 : lc * 32 + 32, :] = jnp.concatenate(
            [jnp.sum(x, axis=0, keepdims=True) for x in accs] + [jnp.zeros((1, LANES), F32)], axis=0
        )

    tap_s[cols * 32 :, :] = jnp.zeros((HALO, LANES), F32)
    core = bits[0]
    size = cols * width // 8
    tap_rows = cols
    for out, owner in ((keep, core), (send, 1 - core)):
        for h in range(2):
            i = owner * 2 + h
            grad = mm(left_s[i // 3], right_s[i], TN).astype(BF)
            for piece in range(8):
                flat = piece * size
                cb, at = flat // width, flat % width
                tail = tap_s[pl.ds(pl.multiple_of((i * 8 + piece) * tap_rows, tap_rows), HALO), :]
                out[h, piece // 4, piece // 2 % 2, piece % 2, 0:size, :] = grad[
                    at : at + size, cb * LANES : (cb + 1) * LANES
                ]
                out[h, piece // 4, piece // 2 % 2, piece % 2, size : size + HALO, :] = tail.astype(BF)


def at(x, *where):
    for i in where:
        x = lax.dynamic_index_in_dim(x, i, 0, keepdims=False)
    return x


def total(*parts):
    return functools.reduce(lambda x, y: x + y, [x.astype(F32) for x in parts]).astype(BF)


def final_kernel(plan, bits, own, far, other_own, other_far, taps, *refs):
    width, norm = plan
    outs, tap_s = refs[:4], refs[4]
    cols = width // LANES
    size = cols * width // 8
    core, y, x, z = bits[0], bits[1], bits[2], bits[3]

    def emit(which, near, across):
        for h in range(2):
            i = 2 * which + h
            first, second = (x, y) if h == 0 else (y, x)
            for b1 in range(2):
                for b2 in range(2):
                    for b3 in range(2):
                        part = (near, across)[b1]
                        piece = (first ^ b1) * 4 + (second ^ b2) * 2 + (z ^ b3)
                        flat = piece * size
                        cb, at = flat // width, flat % width
                        outs[i][
                            pl.ds(pl.multiple_of(at, size), size),
                            pl.ds(pl.multiple_of(cb * LANES, LANES), LANES),
                        ] = part[h, b2, b3, 0:size, :].astype(F32) * norm
                        tap_s[i * 8 + piece] = part[h, b2, b3, size : size + HALO, :].astype(F32) * norm

    for which in range(2):
        @pl.when(core == which)
        def _():
            emit(which, own, far)
            emit(1 - which, other_own, other_far)

    for g in range(32):
        row = g * cols
        lc, j = row // 32, row % 32
        kept = min(cols, 31 - j)
        taps[j : j + kept, lc * LANES : (lc + 1) * LANES] = tap_s[g, 0:kept]


def frame_kernel(plan, got, before, after, cot, kern, layer_out, frame_grad):
    groups, count, sub, width = plan
    cols = width // LANES

    def edge(a, m, lanes):
        first = before[m, :, lanes] if a == 0 else got[a - 1, 1, m, sub - HALO :, lanes]
        last = after[m, :, lanes] if a == groups - 1 else got[a + 1, 1, m, :HALO, lanes]
        return jnp.concatenate([first, got[a, 1, m, :, lanes], last], axis=0).astype(F32)

    def step(m, _):
        for a in range(groups):
            part = slice(a * sub, (a + 1) * sub)
            layer_out[m, part, :] = got[a, 0, m, :, :]
            for lc in range(cols):
                lanes = slice(lc * LANES, (lc + 1) * LANES)
                total = window(edge(a, m, lanes), lambda o: kern[31 - o : 32 - o, lanes], sub)
                frame_grad[m, part, lanes] = (cot[m, part, lanes].astype(F32) + total).astype(BF)
        return 0

    lax.fori_loop(0, count, step, 0)


def call(body, outs, scratch, limit, *args):
    return pl.pallas_call(
        body,
        out_shape=outs,
        in_specs=[
            pl.BlockSpec(memory_space=pltpu.SMEM if x.dtype == jnp.int32 else pltpu.VMEM)
            for x in args
        ],
        out_specs=jax.tree.map(lambda _: pl.BlockSpec(memory_space=pltpu.VMEM), outs),
        scratch_shapes=scratch,
        compiler_params=pltpu.CompilerParams(vmem_limit_bytes=limit * MIB),
    )(*args)


def neighbours(groups, blocks):
    def flat(s):
        return (s % groups) * blocks + s // groups

    return [(flat(s), flat(s + 1)) for s in range(groups * blocks - 1)]


def shards(frames, cotangent, kernel, w_query, w_key, w_value, w_out):
    groups, blocks = lax.axis_size("mic"), lax.axis_size("tm")
    count, length, width = frames.shape
    sub = length // groups
    rows = groups * count * sub
    shape = jax.ShapeDtypeStruct

    send = jnp.stack([frames, cotangent]).reshape(2, count, groups, sub, width)
    got = lax.all_to_all(send.transpose(2, 0, 1, 3, 4), "mic", 0, 0, tiled=True)
    up = neighbours(groups, blocks)
    down = [(j, i) for i, j in up]
    before = lax.ppermute(got[:, 0, :, sub - HALO :, :], ("mic", "tm"), up)
    after = lax.ppermute(got[:, 0, :, :HALO, :], ("mic", "tm"), down)

    mic, tm = lax.axis_index("mic"), lax.axis_index("tm")
    bits = jnp.stack([mic % 2, mic // 2, tm % 2, tm // 2 % 2]).astype(jnp.int32)
    over_core, over_y, over_x, over_z = blocks, 2 * blocks, 1, 2

    def swap(x, mask):
        return lax.ppermute(x, ("mic", "tm"), [(f, f ^ mask) for f in range(groups * blocks)])

    factor = 1.0 / math.sqrt(width // HEADS)
    piece = (width * width // LANES // 8 + HALO, LANES)
    big = pltpu.VMEM((rows, width), BF)
    wide = pltpu.VMEM((rows, width), F32)
    halves = shape((2, 2, 2, 2, *piece), BF)
    back, keep, send = call(
        functools.partial(main_kernel, (groups, count, sub, width, factor)),
        (shape((groups, 2, count, sub, width), BF), halves, halves),
        [
            wide, pltpu.VMEM((2, rows, width), BF), pltpu.VMEM((4, rows, width), BF),
            big, big, big, big, wide, pltpu.VMEM((32 * width // LANES + HALO, LANES), F32),
        ],
        24, bits, got, before, after, kernel, w_query, w_key, w_value, w_out,
    )

    core_got = swap(send, over_core)
    home = lax.all_to_all(back, "mic", 0, 0, tiled=True)
    y, x, z = bits[1], bits[2], bits[3]
    a, b = [keep[0], core_got[0]], [keep[1], core_got[1]]
    a_got = swap(total(*(at(t, 1 - x) for t in a)), over_x)
    b_got = swap(total(*(at(t, 1 - y) for t in b)), over_y)
    a, b = [at(t, x) for t in a] + [a_got], [at(t, y) for t in b] + [b_got]
    a_got = swap(total(*(at(t, 1 - y) for t in a)), over_y)
    b_got = swap(total(*(at(t, 1 - x) for t in b)), over_x)
    a, b = [at(t, y) for t in a] + [a_got], [at(t, x) for t in b] + [b_got]
    theirs = jnp.stack([total(*(at(t, 1 - z) for t in h)) for h in (a, b)])
    theirs, home = lax.optimization_barrier((theirs, home))
    z_got = swap(theirs, over_z)
    mine = jnp.stack(
        [total(*(at(t, z) for t in h), z_got[i]) for i, h in enumerate((a, b))]
    )
    mask = 2 * over_z
    while mask < blocks:
        mine = total(mine, swap(mine, mask))
        mask *= 2

    up = [(i, i + 1) for i in range(blocks - 1)]
    down = [(j, i) for i, j in up]
    before = lax.ppermute(home[groups - 1, 1, :, sub - HALO :, :], "tm", up)
    after = lax.ppermute(home[0, 1, :, :HALO, :], "tm", down)

    line = jnp.stack([mine, swap(mine, over_z)], axis=1)
    line, before, after = lax.optimization_barrier((line, before, after))
    layer_out, frame_grad = call(
        functools.partial(frame_kernel, (groups, count, sub, width)),
        (shape((count, length, width), BF), shape((count, length, width), BF)),
        [], 12, home, before, after, cotangent, kernel,
    )
    plane = jnp.stack([line, jnp.stack([swap(line[0], over_y), swap(line[1], over_x)])], axis=1)
    other_plane = swap(plane, over_core)
    far = jnp.stack([swap(plane[0], over_x), swap(plane[1], over_y)])
    far, layer_out, frame_grad = lax.optimization_barrier((far, layer_out, frame_grad))
    other_far = swap(far, over_core)

    norm = 1.0 / math.sqrt(groups * count * blocks * length)
    square = shape((width, width), F32)
    grads = call(
        functools.partial(final_kernel, (width, norm)),
        (shape((31, width), F32), square, square, square, square),
        [pltpu.VMEM((32, HALO, LANES), F32)],
        16, bits, plane, far, other_plane, other_far,
    )
    return (layer_out, frame_grad, *grads)


def solution(mesh):
    in_specs = (P("mic", "tm", None), P("mic", "tm", None), P(), P(), P(), P(), P())
    out_specs = (P("mic", "tm", None), P("mic", "tm", None), P(), P(), P(), P(), P())
    return jax.shard_map(shards, mesh=mesh, in_specs=in_specs, out_specs=out_specs, check_vma=False)
```

```python
import functools
import math

import jax
import jax.numpy as jnp
from jax import lax
from jax.experimental import pallas as pl
from jax.experimental.pallas import tpu as pltpu
from jax.sharding import PartitionSpec as P

HEADS = 8
LANES = 128
HALO = 16
NT = (((1,), (1,)), ((), ()))
TN = (((0,), (0,)), ((), ()))
BF = jnp.bfloat16
F32 = jnp.float32
MIB = 1024 * 1024


def mm(left, right, dims=(((1,), (0,)), ((), ()))):
    return lax.dot_general(left, right, dims, preferred_element_type=F32)


def rolled(x, shift):
    return x if shift == 0 else pltpu.roll(x, x.shape[0] - shift, axis=0)


def window(x, taps, rows):
    acc = None
    for r in range(8):
        xr = rolled(x, r)
        for k in range(4):
            o = 8 * k + r
            if o == 0:
                continue
            term = xr[8 * k : 8 * k + rows] * taps(o)
            acc = term if acc is None else acc + term
    return acc


def sigmoid(v):
    return 0.5 * jnp.tanh(0.5 * v) + 0.5


def main_kernel(
    plan, bits, got, before, after, kern, wq_hbm, wk_hbm, wv_hbm, wo_hbm,
    back_out, a_keep, b_keep, a_send, b_send,
    frame_s, w_s, conv_s, left_s, right_s, q_s, k_s, v_s, u_s, dconv_s, tap_s, back, stage,
    frame_sem, cot_sem, w_sem, out_sem,
):
    groups, count, sub, width, factor = plan
    mics = groups * count
    cuts = sub // HALO
    block = mics * HALO
    rows = cuts * block
    cols = width // LANES

    loads = [
        pltpu.make_async_copy(got.at[a, 0], frame_s.at[a], frame_sem.at[a]) for a in range(groups)
    ]
    cots = [
        pltpu.make_async_copy(
            got.at[:, 1, :, pl.ds(c * HALO, HALO)], right_s.at[3, c], cot_sem.at[c]
        )
        for c in range(cuts)
    ]
    weights = [
        pltpu.make_async_copy(w, w_s.at[i], w_sem.at[i])
        for i, w in enumerate((wq_hbm, wk_hbm, wv_hbm, wo_hbm))
    ]
    for copy in loads + weights + cots:
        copy.start()
    for copy in loads:
        copy.wait()

    def frames_window(a, m, lanes):
        return jnp.concatenate(
            [before[a, m, :, lanes], frame_s[a, m, :, lanes], after[a, m, :, lanes]], axis=0
        ).astype(F32)

    def conv_step(n, _):
        a, m = n // count, n % count
        for lc in range(cols):
            lanes = slice(lc * LANES, (lc + 1) * LANES)
            conv = window(
                frames_window(a, m, lanes), lambda o: kern[o - 1 : o, lanes], sub
            )
            acted = (conv * sigmoid(conv)).astype(BF)
            for c in range(cuts):
                at = pl.multiple_of(c * block + n * HALO, HALO)
                conv_s[pl.ds(at, HALO), lanes] = conv[c * HALO : (c + 1) * HALO]
                left_s[0, pl.ds(at, HALO), lanes] = acted[c * HALO : (c + 1) * HALO]
        return 0

    lax.fori_loop(0, mics, conv_step, 0)
    for copy in weights + cots:
        copy.wait()

    def flat(i):
        return right_s[i].reshape(rows, width)

    def put(i, c, lanes, x):
        right_s[i, c, :, :, :, lanes] = x.astype(BF).reshape(groups, count, HALO, LANES)

    acted = left_s[0]
    q_s[...] = mm(acted, w_s[0]).astype(BF)
    k_s[...] = mm(acted, w_s[1]).astype(BF)
    v_s[...] = mm(acted, w_s[2]).astype(BF)
    u_s[...] = mm(flat(3), w_s[3], NT).astype(BF)

    depth = width // HEADS
    per = LANES // depth
    lane = lax.broadcasted_iota(jnp.int32, (block, LANES), 1)
    row_i = lax.broadcasted_iota(jnp.int32, (block, per * block), 0)
    col_i = lax.broadcasted_iota(jnp.int32, (block, per * block), 1)
    same = (row_i % HALO) == (col_i % HALO)

    def by_head(x):
        return jnp.concatenate(
            [jnp.where(lane // depth == h, x, jnp.zeros_like(x)) for h in range(per)], axis=0
        )

    def sums(x):
        return [
            jnp.sum(x[:, h * block : (h + 1) * block], axis=1, keepdims=True) for h in range(per)
        ]

    def each(x, values, op):
        return jnp.concatenate(
            [op(x[:, h * block : (h + 1) * block], values[h]) for h in range(per)], axis=1
        )

    def pick(x):
        out = x[:block]
        for h in range(1, per):
            out = jnp.where(lane // depth == h, x[h * block : (h + 1) * block], out)
        return out

    for c in range(cuts):
        part = slice(c * block, (c + 1) * block)
        for p in range(cols):
            lanes = slice(p * LANES, (p + 1) * LANES)
            q, u = q_s[part, lanes], u_s[part, lanes]
            kc, vc = by_head(k_s[part, lanes]), by_head(v_s[part, lanes])
            e = jnp.where(same, jnp.exp(mm(q, kc, NT) * factor), 0.0)
            w = each(e, [1.0 / x for x in sums(e)], lambda x, s: x * s)
            up = mm(u, vc, NT)
            inner = each(up, sums(w * up), lambda x, s: x - s) * w * factor
            wb, ib = w.astype(BF), inner.astype(BF)
            left_s[1, part, lanes] = mm(wb, vc).astype(BF)
            put(0, c, lanes, mm(ib, kc))
            put(1, c, lanes, pick(mm(ib, q, TN)))
            put(2, c, lanes, pick(mm(wb, u, TN)))

    dacted = mm(flat(0), w_s[0], NT) + mm(flat(1), w_s[1], NT) + mm(flat(2), w_s[2], NT)
    conv = conv_s[...]
    sig = sigmoid(conv)
    dconv_s[...] = dacted * sig * (1.0 + conv * (1.0 - sig))

    for lc in range(cols):
        lanes = slice(lc * LANES, (lc + 1) * LANES)

        def tap_step(n, accs):
            a, m = n // count, n % count
            x = frames_window(a, m, lanes)
            d = jnp.concatenate(
                [
                    dconv_s[pl.ds(pl.multiple_of(c * block + n * HALO, HALO), HALO), lanes]
                    for c in range(cuts)
                ],
                axis=0,
            )
            out = list(accs)
            for r in range(8):
                xr = rolled(x, r)
                for k in range(4):
                    o = 8 * k + r
                    if o == 0:
                        continue
                    prod = xr[8 * k : 8 * k + sub] * d
                    out[o - 1] = out[o - 1] + jnp.sum(prod.reshape(sub // 8, 8, LANES), axis=0)
            return tuple(out)

        accs = lax.fori_loop(0, mics, tap_step, tuple(jnp.zeros((8, LANES), F32) for _ in range(31)))
        tap_s[lc * 32 : lc * 32 + 32, :] = jnp.concatenate(
            [jnp.sum(x, axis=0, keepdims=True) for x in accs] + [jnp.zeros((1, LANES), F32)], axis=0
        )

    tap_s[cols * 32 :, :] = jnp.zeros((HALO, LANES), F32)
    core = bits[0]
    size = cols * width // 8
    copies = []
    for n, (out, owner, h) in enumerate(
        ((a_send, 1 - core, 0), (b_send, 1 - core, 1), (a_keep, core, 0), (b_keep, core, 1))
    ):
        i = owner * 2 + h
        grad = mm(left_s[i // 3], flat(i), TN).astype(BF)
        for piece in range(8):
            at = piece * size
            cb, at = at // width, at % width
            tail = tap_s[pl.ds(pl.multiple_of((i * 8 + piece) * cols, cols), HALO), :]
            where = (n, piece // 4, piece // 2 % 2, piece % 2)
            stage[(*where, slice(0, size), slice(None))] = grad[
                at : at + size, cb * LANES : (cb + 1) * LANES
            ]
            stage[(*where, slice(size, size + HALO), slice(None))] = tail.astype(BF)
        copy = pltpu.make_async_copy(stage.at[n], out, out_sem.at[n])
        copy.start()
        copies.append(copy)

    proj = mm(left_s[1], w_s[3])
    for n in range(mics):
        a, m = n // count, n % count
        for c in range(cuts):
            at = c * block + n * HALO
            part = slice(c * HALO, (c + 1) * HALO)
            back[a, 0, m, part, :] = (
                frame_s[a, m, part, :].astype(F32) + proj[at : at + HALO]
            ).astype(BF)
            back[a, 1, m, part, :] = dconv_s[at : at + HALO, :].astype(BF)
    copy = pltpu.make_async_copy(back, back_out, out_sem.at[4])
    copy.start()
    for copy in copies + [copy]:
        copy.wait()


def at(x, *where):
    rest = x.shape[len(where) :]
    start = [jnp.asarray(i, jnp.int32) for i in where] + [jnp.int32(0)] * len(rest)
    return lax.dynamic_slice(x, start, (1,) * len(where) + rest).reshape(rest)


def total(*parts):
    return functools.reduce(lambda x, y: x + y, [x.astype(F32) for x in parts]).astype(BF)


def final_kernel(
    plan, bits, a_own, b_own, a_far, b_far, a_other, b_other, a_other_far, b_other_far, taps, *refs
):
    width, norm = plan
    outs, tap_s = refs[:4], refs[4]
    cols = width // LANES
    size = cols * width // 8
    core, y, x, z = bits[0], bits[1], bits[2], bits[3]

    def emit(which, parts):
        for h in range(2):
            i = 2 * which + h
            first, second = (x, y) if h == 0 else (y, x)
            for b1 in range(2):
                part = parts[b1][h]
                for b2 in range(2):
                    for b3 in range(2):
                        piece = (first ^ b1) * 4 + (second ^ b2) * 2 + (z ^ b3)
                        flat = piece * size
                        cb, at = flat // width, flat % width
                        outs[i][
                            pl.ds(pl.multiple_of(at, size), size),
                            pl.ds(pl.multiple_of(cb * LANES, LANES), LANES),
                        ] = part[b2, b3, 0:size, :].astype(F32) * norm
                        tap_s[i * 8 + piece] = part[b2, b3, size : size + HALO, :].astype(F32) * norm

    for which in range(2):
        @pl.when(core == which)
        def _():
            emit(which, ((a_own, b_own), (a_far, b_far)))
            emit(1 - which, ((a_other, b_other), (a_other_far, b_other_far)))

    for g in range(32):
        row = g * cols
        lc, j = row // 32, row % 32
        kept = min(cols, 31 - j)
        taps[j : j + kept, lc * LANES : (lc + 1) * LANES] = tap_s[g, 0:kept]


def frame_kernel(plan, got, before, after, cot, kern, layer_out, frame_grad):
    groups, count, sub, width = plan
    cols = width // LANES

    def edge(a, m, lanes):
        first = before[m, :, lanes] if a == 0 else got[a - 1, 1, m, sub - HALO :, lanes]
        last = after[m, :, lanes] if a == groups - 1 else got[a + 1, 1, m, :HALO, lanes]
        return jnp.concatenate([first, got[a, 1, m, :, lanes], last], axis=0).astype(F32)

    def step(m, _):
        for a in range(groups):
            part = slice(a * sub, (a + 1) * sub)
            layer_out[m, part, :] = got[a, 0, m, :, :]
            for lc in range(cols):
                lanes = slice(lc * LANES, (lc + 1) * LANES)
                total = window(edge(a, m, lanes), lambda o: kern[31 - o : 32 - o, lanes], sub)
                frame_grad[m, part, lanes] = (cot[m, part, lanes].astype(F32) + total).astype(BF)
        return 0

    lax.fori_loop(0, count, step, 0)


def call(body, outs, scratch, limit, *args, spaces=(), out_space=pltpu.VMEM):
    spaces = list(spaces) + [pltpu.VMEM] * (len(args) - len(spaces))
    return pl.pallas_call(
        body,
        out_shape=outs,
        in_specs=[
            pl.BlockSpec(memory_space=pltpu.SMEM if x.dtype == jnp.int32 else space)
            for x, space in zip(args, spaces)
        ],
        out_specs=jax.tree.map(lambda _: pl.BlockSpec(memory_space=out_space), outs),
        scratch_shapes=scratch,
        compiler_params=pltpu.CompilerParams(vmem_limit_bytes=limit * MIB),
    )(*args)


def neighbours(groups, blocks):
    def flat(s):
        return (s % groups) * blocks + s // groups

    return [(flat(s), flat(s + 1)) for s in range(groups * blocks - 1)]


def shards(frames, cotangent, kernel, w_query, w_key, w_value, w_out):
    groups, blocks = lax.axis_size("mic"), lax.axis_size("tm")
    count, length, width = frames.shape
    sub = length // groups
    rows = groups * count * sub
    shape = jax.ShapeDtypeStruct

    send = jnp.stack([frames, cotangent]).reshape(2, count, groups, sub, width)
    got = lax.all_to_all(send.transpose(2, 0, 1, 3, 4), "mic", 0, 0, tiled=True)
    up = neighbours(groups, blocks)
    down = [(j, i) for i, j in up]
    before = lax.ppermute(got[:, 0, :, sub - HALO :, :], ("mic", "tm"), up)
    after = lax.ppermute(got[:, 0, :, :HALO, :], ("mic", "tm"), down)

    mic, tm = lax.axis_index("mic"), lax.axis_index("tm")
    bits = jnp.stack([mic % 2, mic // 2, tm % 2, tm // 2 % 2]).astype(jnp.int32)
    over_core, over_y, over_x, over_z = blocks, 2 * blocks, 1, 2

    def swap(x, mask):
        return lax.ppermute(x, ("mic", "tm"), [(f, f ^ mask) for f in range(groups * blocks)])

    factor = 1.0 / math.sqrt(width // HEADS)
    piece = (width * width // LANES // 8 + HALO, LANES)
    big = pltpu.VMEM((rows, width), BF)
    wide = pltpu.VMEM((rows, width), F32)
    half = shape((2, 2, 2, *piece), BF)
    moved = (groups, 2, count, sub, width)
    cuts = sub // HALO
    back, a_keep, b_keep, a_send, b_send = call(
        functools.partial(main_kernel, (groups, count, sub, width, factor)),
        (shape(moved, BF), half, half, half, half),
        [
            pltpu.VMEM((groups, count, sub, width), BF),
            pltpu.VMEM((4, width, width), BF),
            wide,
            pltpu.VMEM((2, rows, width), BF),
            pltpu.VMEM((4, cuts, groups, count, HALO, width), BF),
            big, big, big, big, wide,
            pltpu.VMEM((32 * width // LANES + HALO, LANES), F32),
            pltpu.VMEM(moved, BF),
            pltpu.VMEM((4, 2, 2, 2, *piece), BF),
            pltpu.SemaphoreType.DMA((groups,)),
            pltpu.SemaphoreType.DMA((cuts,)),
            pltpu.SemaphoreType.DMA((4,)),
            pltpu.SemaphoreType.DMA((5,)),
        ],
        28, bits, got, before, after, kernel, w_query, w_key, w_value, w_out,
        spaces=(pltpu.SMEM, pl.ANY, pltpu.VMEM, pltpu.VMEM, pltpu.VMEM) + (pl.ANY,) * 4,
        out_space=pl.ANY,
    )

    y, x, z = bits[1], bits[2], bits[3]
    a, b = [a_keep, swap(a_send, over_core)], [b_keep, swap(b_send, over_core)]
    home = lax.all_to_all(back, "mic", 0, 0, tiled=True)

    def halved(parts, bit, mask):
        got = swap(total(*(at(t, 1 - bit) for t in parts)), mask)
        return [at(t, bit) for t in parts] + [got]

    def line_sum(parts):
        mine = total(*halved(parts, z, over_z))
        mask = 2 * over_z
        while mask < blocks:
            mine = total(mine, swap(mine, mask))
            mask *= 2
        return mine

    a = halved(a, x, over_x)
    b = halved(b, y, over_y)
    a = halved(a, y, over_y)
    b = halved(b, x, over_x)
    b[-1], home = lax.optimization_barrier((b[-1], home))
    a, b = line_sum(a), line_sum(b)

    up = [(i, i + 1) for i in range(blocks - 1)]
    down = [(j, i) for i, j in up]
    before = lax.ppermute(home[groups - 1, 1, :, sub - HALO :, :], "tm", up)
    after = lax.ppermute(home[0, 1, :, :HALO, :], "tm", down)

    a = jnp.stack([a, swap(a, over_z)])
    b = jnp.stack([b, swap(b, over_z)])
    b, before, after = lax.optimization_barrier((b, before, after))
    layer_out, frame_grad = call(
        functools.partial(frame_kernel, (groups, count, sub, width)),
        (shape((count, length, width), BF), shape((count, length, width), BF)),
        [], 12, home, before, after, cotangent, kernel,
    )
    a = jnp.stack([a, swap(a, over_y)])
    b = jnp.stack([b, swap(b, over_x)])
    a_far, b_far = swap(a, over_x), swap(b, over_y)
    a_other, b_other = swap(a, over_core), swap(b, over_core)
    b_far, layer_out, frame_grad = lax.optimization_barrier((b_far, layer_out, frame_grad))
    a_other_far, b_other_far = swap(a_far, over_core), swap(b_far, over_core)

    norm = 1.0 / math.sqrt(groups * count * blocks * length)
    square = shape((width, width), F32)
    grads = call(
        functools.partial(final_kernel, (width, norm)),
        (shape((31, width), F32), square, square, square, square),
        [pltpu.VMEM((32, HALO, LANES), F32)],
        16, bits, a, b, a_far, b_far, a_other, b_other, a_other_far, b_other_far,
    )
    return (layer_out, frame_grad, *grads)


def solution(mesh):
    in_specs = (P("mic", "tm", None), P("mic", "tm", None), P(), P(), P(), P(), P())
    out_specs = (P("mic", "tm", None), P("mic", "tm", None), P(), P(), P(), P(), P())
    return jax.shard_map(shards, mesh=mesh, in_specs=in_specs, out_specs=out_specs, check_vma=False)
```

```python
import functools
import math

import jax
import jax.numpy as jnp
from jax import lax
from jax.experimental import pallas as pl
from jax.experimental.pallas import tpu as pltpu
from jax.sharding import PartitionSpec as P

HEADS = 8
LANES = 128
HALO = 16
NT = (((1,), (1,)), ((), ()))
TN = (((0,), (0,)), ((), ()))
BF = jnp.bfloat16
F32 = jnp.float32
MIB = 1024 * 1024
CORE, Y, X, Z, ODD, SKIP, BLOCK_AT = range(7)


def mm(left, right, dims=(((1,), (0,)), ((), ()))):
    return lax.dot_general(left, right, dims, preferred_element_type=F32)


def rolled(x, shift):
    return x if shift == 0 else pltpu.roll(x, x.shape[0] - shift, axis=0)


def window(x, taps, rows):
    acc = None
    for r in range(8):
        xr = rolled(x, r)
        for k in range(4):
            o = 8 * k + r
            if o == 0:
                continue
            term = xr[8 * k : 8 * k + rows] * taps(o)
            acc = term if acc is None else acc + term
    return acc


def sigmoid(v):
    return 0.5 * jnp.tanh(0.5 * v) + 0.5


def scatter_kernel(plan, bits, frames, cot, *refs):
    sub, outs, sems = plan, refs[:8], refs[8]
    copies = []
    for i, source in enumerate((frames, cot)):
        for d in range(4):
            rows = pl.ds(pl.multiple_of(bits[BLOCK_AT + d] * sub, sub), sub)
            n = 4 * i + d
            copies.append(pltpu.make_async_copy(source.at[:, rows], outs[n], sems.at[n]))
    for copy in copies:
        copy.start()
    for copy in copies:
        copy.wait()


def edge_kernel(sub, bits, f0, f1, f2, f3, near, side):
    odd = bits[ODD]
    for d, f in enumerate((f0, f1, f2, f3)):
        last = sub - HALO
        near[d] = f[:, pl.ds(pl.multiple_of((1 - odd) * last, HALO), HALO), :]
        side[d] = f[:, pl.ds(pl.multiple_of(odd * last, HALO), HALO), :]


def main_kernel(
    plan, bits, f0, f1, f2, f3, c0, c1, c2, c3, near, side, kern, wq, wk, wv, wo,
    a_keep, b_keep, a_send, b_send, back_keep,
    frame_s, conv_s, left_s, right_s, q_s, k_s, v_s, u_s, dconv_s, tap_s,
):
    groups, count, sub, width, factor = plan
    mics = groups * count
    cuts = sub // HALO
    block = mics * HALO
    rows = cuts * block
    cols = width // LANES
    odd, skip = bits[ODD], bits[SKIP]
    is_odd = jnp.broadcast_to(odd, (HALO, LANES)) == 1

    for d, (f, cot) in enumerate(((f0, c0), (f1, c1), (f2, c2), (f3, c3))):
        frame_s[d] = f[...]
        for m in range(count):
            for c in range(cuts):
                right_s[3, c, d, m] = cot[m, c * HALO : (c + 1) * HALO, :]

    def frames_window(a, m, lanes):
        one = near[a ^ 1, m, :, lanes].astype(F32)
        two = side[a ^ skip, m, :, lanes].astype(F32)
        return jnp.concatenate(
            [
                jnp.where(is_odd, one, two),
                frame_s[a, m, :, lanes].astype(F32),
                jnp.where(is_odd, two, one),
            ],
            axis=0,
        )

    def conv_step(n, _):
        a, m = n // count, n % count
        for lc in range(cols):
            lanes = slice(lc * LANES, (lc + 1) * LANES)
            conv = window(
                frames_window(a, m, lanes), lambda o: kern[o - 1 : o, lanes], sub
            )
            acted = (conv * sigmoid(conv)).astype(BF)
            for c in range(cuts):
                at = pl.multiple_of(c * block + n * HALO, HALO)
                conv_s[pl.ds(at, HALO), lanes] = conv[c * HALO : (c + 1) * HALO]
                left_s[0, pl.ds(at, HALO), lanes] = acted[c * HALO : (c + 1) * HALO]
        return 0

    lax.fori_loop(0, mics, conv_step, 0)

    def flat(i):
        return right_s[i].reshape(rows, width)

    def put(i, c, lanes, x):
        right_s[i, c, :, :, :, lanes] = x.astype(BF).reshape(groups, count, HALO, LANES)

    acted = left_s[0]
    q_s[...] = mm(acted, wq[...]).astype(BF)
    k_s[...] = mm(acted, wk[...]).astype(BF)
    v_s[...] = mm(acted, wv[...]).astype(BF)
    u_s[...] = mm(flat(3), wo[...], NT).astype(BF)

    depth = width // HEADS
    per = LANES // depth
    lane = lax.broadcasted_iota(jnp.int32, (block, LANES), 1)
    row_i = lax.broadcasted_iota(jnp.int32, (block, per * block), 0)
    col_i = lax.broadcasted_iota(jnp.int32, (block, per * block), 1)
    same = (row_i % HALO) == (col_i % HALO)

    def by_head(x):
        return jnp.concatenate(
            [jnp.where(lane // depth == h, x, jnp.zeros_like(x)) for h in range(per)], axis=0
        )

    def sums(x):
        return [
            jnp.sum(x[:, h * block : (h + 1) * block], axis=1, keepdims=True) for h in range(per)
        ]

    def each(x, values, op):
        return jnp.concatenate(
            [op(x[:, h * block : (h + 1) * block], values[h]) for h in range(per)], axis=1
        )

    def pick(x):
        out = x[:block]
        for h in range(1, per):
            out = jnp.where(lane // depth == h, x[h * block : (h + 1) * block], out)
        return out

    for c in range(cuts):
        part = slice(c * block, (c + 1) * block)
        for p in range(cols):
            lanes = slice(p * LANES, (p + 1) * LANES)
            q, u = q_s[part, lanes], u_s[part, lanes]
            kc, vc = by_head(k_s[part, lanes]), by_head(v_s[part, lanes])
            e = jnp.where(same, jnp.exp(mm(q, kc, NT) * factor), 0.0)
            w = each(e, [1.0 / x for x in sums(e)], lambda x, s: x * s)
            up = mm(u, vc, NT)
            inner = each(up, sums(w * up), lambda x, s: x - s) * w * factor
            wb, ib = w.astype(BF), inner.astype(BF)
            left_s[1, part, lanes] = mm(wb, vc).astype(BF)
            put(0, c, lanes, mm(ib, kc))
            put(1, c, lanes, pick(mm(ib, q, TN)))
            put(2, c, lanes, pick(mm(wb, u, TN)))

    dacted = mm(flat(0), wq[...], NT) + mm(flat(1), wk[...], NT) + mm(flat(2), wv[...], NT)
    conv = conv_s[...]
    sig = sigmoid(conv)
    dconv_s[...] = dacted * sig * (1.0 + conv * (1.0 - sig))

    for lc in range(cols):
        lanes = slice(lc * LANES, (lc + 1) * LANES)

        def tap_step(n, accs):
            a, m = n // count, n % count
            x = frames_window(a, m, lanes)
            d = jnp.concatenate(
                [
                    dconv_s[pl.ds(pl.multiple_of(c * block + n * HALO, HALO), HALO), lanes]
                    for c in range(cuts)
                ],
                axis=0,
            )
            out = list(accs)
            for r in range(8):
                xr = rolled(x, r)
                for k in range(4):
                    o = 8 * k + r
                    if o == 0:
                        continue
                    prod = xr[8 * k : 8 * k + sub] * d
                    out[o - 1] = out[o - 1] + jnp.sum(prod.reshape(sub // 8, 8, LANES), axis=0)
            return tuple(out)

        accs = lax.fori_loop(0, mics, tap_step, tuple(jnp.zeros((8, LANES), F32) for _ in range(31)))
        tap_s[lc * 32 : lc * 32 + 32, :] = jnp.concatenate(
            [jnp.sum(x, axis=0, keepdims=True) for x in accs] + [jnp.zeros((1, LANES), F32)], axis=0
        )

    tap_s[cols * 32 :, :] = jnp.zeros((HALO, LANES), F32)
    size = cols * width // 8
    span = size + HALO
    core, y, x, z = bits[CORE], bits[Y], bits[X], bits[Z]
    for out, owner, h in (
        (a_send, 1 - core, 0), (b_send, 1 - core, 1), (a_keep, core, 0), (b_keep, core, 1)
    ):
        i = owner * 2 + h
        first, second = (x, y) if h == 0 else (y, x)
        grad = mm(left_s[i // 3], flat(i), TN).astype(BF)
        for piece in range(8):
            cb, at = piece * size // width, piece * size % width
            tail = tap_s[pl.ds(pl.multiple_of((i * 8 + piece) * cols, cols), HALO), :]
            rel = ((piece // 4) ^ first) * 4 + ((piece // 2 % 2) ^ second) * 2 + ((piece % 2) ^ z)
            start = pl.multiple_of(rel * span, HALO)
            out[pl.ds(start, size), :] = grad[at : at + size, cb * LANES : (cb + 1) * LANES]
            out[pl.ds(pl.multiple_of(start + size, HALO), HALO), :] = tail.astype(BF)

    proj = mm(left_s[1], wo[...])
    unit = 2 * count * cols * sub
    for d, (out, base) in enumerate(
        ((back_keep, 0), (b_send, 8 * span), (back_keep, unit), (b_send, 8 * span + unit))
    ):
        for m in range(count):
            for c in range(cuts):
                at = c * block + (d * count + m) * HALO
                part = slice(c * HALO, (c + 1) * HALO)
                layer = (frame_s[d, m, part, :].astype(F32) + proj[at : at + HALO]).astype(BF)
                dconv = dconv_s[at : at + HALO, :].astype(BF)
                for lc in range(cols):
                    for kind, value in enumerate((layer, dconv)):
                        to = base + ((kind * count + m) * cols + lc) * sub + c * HALO
                        out[to : to + HALO, :] = value[:, lc * LANES : (lc + 1) * LANES]


def total(*parts):
    return functools.reduce(lambda x, y: x + y, [x.astype(F32) for x in parts]).astype(BF)


def final_kernel(
    plan, bits, a_own, b_own, a_far, b_far, a_other, b_other, a_other_far, b_other_far, taps, *refs
):
    width, norm = plan
    outs, tap_s = refs[:4], refs[4]
    cols = width // LANES
    size = cols * width // 8
    span = size + HALO
    core, y, x, z = bits[CORE], bits[Y], bits[X], bits[Z]

    def emit(which, parts):
        for h in range(2):
            i = 2 * which + h
            first, second = (x, y) if h == 0 else (y, x)
            for rel in range(8):
                part, start = parts[rel // 4][h], rel % 4 * span
                piece = (first ^ (rel // 4)) * 4 + (second ^ (rel // 2 % 2)) * 2 + (z ^ (rel % 2))
                cb, at = piece * size // width, piece * size % width
                outs[i][
                    pl.ds(pl.multiple_of(at, size), size),
                    pl.ds(pl.multiple_of(cb * LANES, LANES), LANES),
                ] = part[start : start + size, :].astype(F32) * norm
                tap_s[i * 8 + piece] = part[start + size : start + span, :].astype(F32) * norm

    for which in range(2):
        @pl.when(core == which)
        def _():
            emit(which, ((a_own, b_own), (a_far, b_far)))
            emit(1 - which, ((a_other, b_other), (a_other_far, b_other_far)))

    for g in range(32):
        row = g * cols
        lc, j = row // 32, row % 32
        kept = min(cols, 31 - j)
        taps[j : j + kept, lc * LANES : (lc + 1) * LANES] = tap_s[g, 0:kept]


def home_kernel(plan, bits, own, core_got, y_got, layer_out, dconv, x_edge, z_edge):
    count, sub, cols, core_at, y_at = plan
    unit = 2 * count * cols * sub
    odd = bits[X]
    last = 3 * sub + sub - HALO
    for d, (ref, base) in enumerate(
        ((own, 0), (core_got, core_at), (y_got, y_at), (y_got, y_at + unit))
    ):
        to = pl.ds(pl.multiple_of(bits[BLOCK_AT + d] * sub, sub), sub)
        for m in range(count):
            for lc in range(cols):
                at = base + (m * cols + lc) * sub
                layer_out[m, to, lc * LANES : (lc + 1) * LANES] = ref[at : at + sub, :]
                at += count * cols * sub
                dconv[m, lc, to, :] = ref[at : at + sub, :]
    for m in range(count):
        for lc in range(cols):
            at = (m * cols + lc) * HALO
            x_rows = pl.ds(pl.multiple_of((1 - odd) * last, HALO), HALO)
            z_rows = pl.ds(pl.multiple_of(odd * last, HALO), HALO)
            x_edge[at : at + HALO, :] = dconv[m, lc, x_rows, :]
            z_edge[at : at + HALO, :] = dconv[m, lc, z_rows, :]


def frame_kernel(plan, bits, dconv, x_got, z_got, cot, kern, frame_grad):
    count, cols, x_at, length = plan
    is_odd = jnp.broadcast_to(bits[X], (HALO, LANES)) == 1

    def step(m, _):
        for lc in range(cols):
            lanes = slice(lc * LANES, (lc + 1) * LANES)
            at = pl.multiple_of((m * cols + lc) * HALO, HALO)
            one = x_got[pl.ds(pl.multiple_of(x_at + at, HALO), HALO), :].astype(F32)
            two = z_got[pl.ds(at, HALO), :].astype(F32)
            x = jnp.concatenate(
                [
                    jnp.where(is_odd, one, two),
                    dconv[m, lc].astype(F32),
                    jnp.where(is_odd, two, one),
                ],
                axis=0,
            )
            grad = window(x, lambda o: kern[31 - o : 32 - o, lanes], length)
            frame_grad[m, :, lanes] = (cot[m, :, lanes].astype(F32) + grad).astype(BF)
        return 0

    lax.fori_loop(0, count, step, 0)


def call(body, outs, scratch, limit, *args, space=pltpu.VMEM):
    return pl.pallas_call(
        body,
        out_shape=outs,
        in_specs=[
            pl.BlockSpec(memory_space=pltpu.SMEM if x.dtype == jnp.int32 else space)
            for x in args
        ],
        out_specs=jax.tree.map(lambda _: pl.BlockSpec(memory_space=space), outs),
        scratch_shapes=scratch,
        compiler_params=pltpu.CompilerParams(vmem_limit_bytes=limit * MIB),
    )(*args)


def shards(frames, cotangent, kernel, w_query, w_key, w_value, w_out):
    groups, blocks = lax.axis_size("mic"), lax.axis_size("tm")
    count, length, width = frames.shape
    sub = length // groups
    cuts = sub // HALO
    cols = width // LANES
    rows = groups * count * sub
    shape = jax.ShapeDtypeStruct

    mic, tm = lax.axis_index("mic"), lax.axis_index("tm")
    over_core, over_y, over_x, over_z = blocks, 2 * blocks, 1, 2

    def order(a):
        return (a ^ (a >> 1)) ^ (3 * (tm % 2))

    mine = order(mic)
    bits = jnp.stack(
        [mic % 2, mic // 2, tm % 2, tm // 2 % 2, mine % 2, 2 * ((mine + 1) // 2 % 2)]
        + [order(mic ^ d) for d in range(4)]
    ).astype(jnp.int32)

    def permute(x, pairs):
        return lax.ppermute(x, ("mic", "tm"), pairs)

    def swap(x, mask):
        return permute(x, [(f, f ^ mask) for f in range(groups * blocks)])

    def both(pairs):
        return pairs + [(j, i) for i, j in pairs]

    block = shape((count, sub, width), BF)
    parts = call(
        functools.partial(scatter_kernel, sub), (block,) * 8,
        [pltpu.SemaphoreType.DMA((8,))], 8, bits, frames, cotangent, space=pl.ANY,
    )
    masks = (0, over_core, over_y, over_core + over_y)
    got = {d: swap(parts[d], masks[d]) for d in (2, 3, 1)}
    f = [parts[0], got[1], got[2], got[3]]
    got = {d: swap(parts[4 + d], masks[d]) for d in (2, 3, 1)}
    c = [parts[4], got[1], got[2], got[3]]
    edge = shape((groups, count, HALO, width), BF)
    near, side = call(functools.partial(edge_kernel, sub), (edge, edge), [], 8, bits, *f)
    near = swap(near, over_core)
    side = permute(
        side,
        both([(blocks + t, 3 * blocks + t) for t in range(blocks)])
        + both([((2 - 2 * (t % 2)) * blocks + t, (2 - 2 * (t % 2)) * blocks + t + 1)
                for t in range(blocks - 1)]),
    )

    factor = 1.0 / math.sqrt(width // HEADS)
    size = width * width // LANES // 8
    span = size + HALO
    unit = 2 * count * cols * sub
    big = pltpu.VMEM((rows, width), BF)
    wide = pltpu.VMEM((rows, width), F32)

    def flat(n):
        return shape((n, LANES), BF)

    a_keep, b_keep, a_send, b_send, back_keep = call(
        functools.partial(main_kernel, (groups, count, sub, width, factor)),
        (flat(8 * span), flat(8 * span), flat(8 * span), flat(8 * span + 2 * unit), flat(2 * unit)),
        [
            pltpu.VMEM((groups, count, sub, width), BF),
            wide,
            pltpu.VMEM((2, rows, width), BF),
            pltpu.VMEM((4, cuts, groups, count, HALO, width), BF),
            big, big, big, big, wide,
            pltpu.VMEM((32 * cols + HALO, LANES), F32),
        ],
        24, bits, *f, *c, near, side, kernel, w_query, w_key, w_value, w_out,
    )

    def sent(parts, n):
        return total(*(t[n : 2 * n] for t in parts))

    def kept(parts, got, n):
        return [t[:n] for t in parts] + [got[:n]]

    def line_sum(parts):
        got = swap(sent(parts, span), over_z)
        mine = total(*kept(parts, got, span))
        mask = 2 * over_z
        while mask < blocks:
            mine = total(mine, swap(mine, mask))
            mask *= 2
        return mine

    a = [a_keep, swap(a_send, over_core)]
    core_got = swap(b_send, over_core)
    b = [b_keep, core_got]
    a = kept(a, swap(sent(a, 4 * span), over_x), 4 * span)
    y_got = swap(
        jnp.concatenate([sent(b, 4 * span), back_keep[unit:], core_got[8 * span + unit :]]), over_y
    )
    b = kept(b, y_got, 4 * span)
    a = kept(a, swap(sent(a, 2 * span), over_y), 2 * span)
    edge = flat(count * cols * HALO)
    layer_out, dconv, x_edge, z_edge = call(
        functools.partial(home_kernel, (count, sub, cols, 8 * span, 4 * span)),
        (shape(frames.shape, BF), shape((count, cols, length, LANES), BF), edge, edge),
        [], 8, bits, back_keep, core_got, y_got,
    )
    x_got = swap(jnp.concatenate([sent(b, 2 * span), x_edge]), over_x)
    b = kept(b, x_got, 2 * span)
    z_got = permute(
        z_edge,
        both([(m * blocks + t, m * blocks + t + 1)
              for m in range(groups) for t in range(1, blocks - 1, 2)]),
    )
    a, b = line_sum(a), line_sum(b)
    a = jnp.concatenate([a, swap(a, over_z)])
    b = jnp.concatenate([b, swap(b, over_z)])
    b, z_got = lax.optimization_barrier((b, z_got))
    frame_grad = call(
        functools.partial(frame_kernel, (count, cols, 2 * span, length)),
        shape(frames.shape, BF), [], 8, bits, dconv, x_got, z_got, cotangent, kernel,
    )
    a = jnp.concatenate([a, swap(a, over_y)])
    b = jnp.concatenate([b, swap(b, over_x)])
    a_far, b_far = swap(a, over_x), swap(b, over_y)
    a_other, b_other = swap(a, over_core), swap(b, over_core)
    b_far, frame_grad = lax.optimization_barrier((b_far, frame_grad))
    a_other_far, b_other_far = swap(a_far, over_core), swap(b_far, over_core)

    norm = 1.0 / math.sqrt(groups * count * blocks * length)
    square = shape((width, width), F32)
    grads = call(
        functools.partial(final_kernel, (width, norm)),
        (shape((31, width), F32), square, square, square, square),
        [pltpu.VMEM((32, HALO, LANES), F32)],
        16, bits, a, b, a_far, b_far, a_other, b_other, a_other_far, b_other_far,
    )
    return (layer_out, frame_grad, *grads)


def solution(mesh):
    in_specs = (P("mic", "tm", None), P("mic", "tm", None), P(), P(), P(), P(), P())
    out_specs = (P("mic", "tm", None), P("mic", "tm", None), P(), P(), P(), P(), P())
    return jax.shard_map(shards, mesh=mesh, in_specs=in_specs, out_specs=out_specs, check_vma=False)
```

```python
import functools
import math

import jax
import jax.numpy as jnp
from jax import lax
from jax.experimental import pallas as pl
from jax.experimental.pallas import tpu as pltpu
from jax.sharding import PartitionSpec as P

HEADS = 8
LANES = 128
HALO = 16
NT = (((1,), (1,)), ((), ()))
TN = (((0,), (0,)), ((), ()))
BF = jnp.bfloat16
F32 = jnp.float32
MIB = 1024 * 1024
CORE, Y, X, Z, ZZ, ODD, SKIP, BLOCK_AT = range(8)


def mm(left, right, dims=(((1,), (0,)), ((), ()))):
    return lax.dot_general(left, right, dims, preferred_element_type=F32)


def rolled(x, shift):
    return x if shift == 0 else pltpu.roll(x, x.shape[0] - shift, axis=0)


def window(x, taps, rows):
    acc = None
    for r in range(8):
        xr = rolled(x, r)
        for k in range(4):
            o = 8 * k + r
            if o == 0:
                continue
            term = xr[8 * k : 8 * k + rows] * taps(o)
            acc = term if acc is None else acc + term
    return acc


def ways(bits, half):
    return [bits[i] for i in ((X, Y, Z), (Z, ZZ, X))[half]]


def sigmoid(v):
    return 0.5 * jnp.tanh(0.5 * v) + 0.5


def scatter_kernel(sub, bits, source, *refs):
    outs, sems = refs[:4], refs[4]
    copies = []
    for d in range(4):
        rows = pl.ds(pl.multiple_of(bits[BLOCK_AT + d] * sub, sub), sub)
        copies.append(pltpu.make_async_copy(source.at[:, rows], outs[d], sems.at[d]))
    for copy in copies:
        copy.start()
    for copy in copies:
        copy.wait()


def edge_kernel(sub, bits, f0, f1, f2, f3, near, side):
    odd = bits[ODD]
    for d, f in enumerate((f0, f1, f2, f3)):
        last = sub - HALO
        near[d] = f[:, pl.ds(pl.multiple_of((1 - odd) * last, HALO), HALO), :]
        side[d] = f[:, pl.ds(pl.multiple_of(odd * last, HALO), HALO), :]


def frames_window(bits, frames, near, side, a, m, lanes):
    is_odd = jnp.broadcast_to(bits[ODD], (HALO, LANES)) == 1
    one = near[a ^ 1, m, :, lanes].astype(F32)
    two = side[a ^ bits[SKIP], m, :, lanes].astype(F32)
    return jnp.concatenate(
        [
            jnp.where(is_odd, one, two),
            frames[a, m, :, lanes].astype(F32),
            jnp.where(is_odd, two, one),
        ],
        axis=0,
    )


def conv_kernel(plan, bits, f0, f1, f2, f3, near, side, kern, frames, conv_out, acted_out):
    groups, count, sub, width = plan
    mics = groups * count
    cuts = sub // HALO
    for d, f in enumerate((f0, f1, f2, f3)):
        frames[d] = f[...]

    def conv_step(n, _):
        a, m = n // count, n % count
        for lc in range(width // LANES):
            lanes = slice(lc * LANES, (lc + 1) * LANES)
            x = frames_window(bits, frames, near, side, a, m, lanes)
            conv = window(x, lambda o: kern[o - 1 : o, lanes], sub)
            acted = (conv * sigmoid(conv)).astype(BF)
            for c in range(cuts):
                at = pl.multiple_of((c * mics + n) * HALO, HALO)
                conv_out[pl.ds(at, HALO), lanes] = conv[c * HALO : (c + 1) * HALO]
                acted_out[pl.ds(at, HALO), lanes] = acted[c * HALO : (c + 1) * HALO]
        return 0

    lax.fori_loop(0, mics, conv_step, 0)


def main_kernel(
    plan, bits, frames, conv_in, acted_in, c0, c1, c2, c3, near, side, weights,
    a_keep, b_keep, a_send, b_send, back_keep, back_send,
    left_s, right_s, q_s, k_s, v_s, u_s, dconv_s, tap_s,
):
    groups, count, sub, width, factor = plan
    mics = groups * count
    cuts = sub // HALO
    block = mics * HALO
    rows = cuts * block
    cols = width // LANES

    wq, wk, wv, wo = (weights.at[i] for i in range(4))
    left_s[0] = acted_in[...]
    for d, cot in enumerate((c0, c1, c2, c3)):
        for m in range(count):
            for c in range(cuts):
                right_s[3, c, d, m] = cot[m, c * HALO : (c + 1) * HALO, :]

    def flat(i):
        return right_s[i].reshape(rows, width)

    def put(i, c, lanes, x):
        right_s[i, c, :, :, :, lanes] = x.astype(BF).reshape(groups, count, HALO, LANES)

    acted = left_s[0]
    q_s[...] = mm(acted, wq[...]).astype(BF)
    k_s[...] = mm(acted, wk[...]).astype(BF)
    v_s[...] = mm(acted, wv[...]).astype(BF)
    u_s[...] = mm(flat(3), wo[...], NT).astype(BF)

    depth = width // HEADS
    per = LANES // depth
    lane = lax.broadcasted_iota(jnp.int32, (block, LANES), 1)
    row_i = lax.broadcasted_iota(jnp.int32, (block, per * block), 0)
    col_i = lax.broadcasted_iota(jnp.int32, (block, per * block), 1)
    same = (row_i % HALO) == (col_i % HALO)

    def by_head(x):
        return jnp.concatenate(
            [jnp.where(lane // depth == h, x, jnp.zeros_like(x)) for h in range(per)], axis=0
        )

    def sums(x):
        return [
            jnp.sum(x[:, h * block : (h + 1) * block], axis=1, keepdims=True) for h in range(per)
        ]

    def each(x, values, op):
        return jnp.concatenate(
            [op(x[:, h * block : (h + 1) * block], values[h]) for h in range(per)], axis=1
        )

    def pick(x):
        out = x[:block]
        for h in range(1, per):
            out = jnp.where(lane // depth == h, x[h * block : (h + 1) * block], out)
        return out

    for c in range(cuts):
        part = slice(c * block, (c + 1) * block)
        for p in range(cols):
            lanes = slice(p * LANES, (p + 1) * LANES)
            q, u = q_s[part, lanes], u_s[part, lanes]
            kc, vc = by_head(k_s[part, lanes]), by_head(v_s[part, lanes])
            e = jnp.where(same, jnp.exp(mm(q, kc, NT) * factor), 0.0)
            w = each(e, [1.0 / x for x in sums(e)], lambda x, s: x * s)
            up = mm(u, vc, NT)
            inner = each(up, sums(w * up), lambda x, s: x - s) * w * factor
            wb, ib = w.astype(BF), inner.astype(BF)
            left_s[1, part, lanes] = mm(wb, vc).astype(BF)
            put(0, c, lanes, mm(ib, kc))
            put(1, c, lanes, pick(mm(ib, q, TN)))
            put(2, c, lanes, pick(mm(wb, u, TN)))

    dacted = mm(flat(0), wq[...], NT) + mm(flat(1), wk[...], NT) + mm(flat(2), wv[...], NT)
    conv = conv_in[...]
    sig = sigmoid(conv)
    dconv_s[...] = dacted * sig * (1.0 + conv * (1.0 - sig))

    for lc in range(cols):
        lanes = slice(lc * LANES, (lc + 1) * LANES)

        def tap_step(n, accs):
            a, m = n // count, n % count
            x = frames_window(bits, frames, near, side, a, m, lanes)
            d = jnp.concatenate(
                [
                    dconv_s[pl.ds(pl.multiple_of(c * block + n * HALO, HALO), HALO), lanes]
                    for c in range(cuts)
                ],
                axis=0,
            )
            out = list(accs)
            for r in range(8):
                xr = rolled(x, r)
                for k in range(4):
                    o = 8 * k + r
                    if o == 0:
                        continue
                    prod = xr[8 * k : 8 * k + sub] * d
                    out[o - 1] = out[o - 1] + jnp.sum(prod.reshape(sub // 8, 8, LANES), axis=0)
            return tuple(out)

        accs = lax.fori_loop(0, mics, tap_step, tuple(jnp.zeros((8, LANES), F32) for _ in range(31)))
        tap_s[lc * 32 : lc * 32 + 32, :] = jnp.concatenate(
            [jnp.sum(x, axis=0, keepdims=True) for x in accs] + [jnp.zeros((1, LANES), F32)], axis=0
        )

    tap_s[cols * 32 :, :] = jnp.zeros((HALO, LANES), F32)
    size = cols * width // 8
    span = size + HALO
    core = bits[CORE]
    for out, owner, h in (
        (a_send, 1 - core, 0), (b_send, 1 - core, 1), (a_keep, core, 0), (b_keep, core, 1)
    ):
        i = owner * 2 + h
        first, second, third = ways(bits, h)
        grad = mm(left_s[i // 3], flat(i), TN).astype(BF)
        for piece in range(8):
            cb, at = piece * size // width, piece * size % width
            tail = tap_s[pl.ds(pl.multiple_of((i * 8 + piece) * cols, cols), HALO), :]
            rel = ((piece // 4) ^ first) * 4 + ((piece // 2 % 2) ^ second) * 2 + ((piece % 2) ^ third)
            start = pl.multiple_of(rel * span, HALO)
            out[pl.ds(start, size), :] = grad[at : at + size, cb * LANES : (cb + 1) * LANES]
            out[pl.ds(pl.multiple_of(start + size, HALO), HALO), :] = tail.astype(BF)

    proj = mm(left_s[1], wo[...])
    unit = 2 * count * cols * sub
    for d, (out, base) in enumerate(
        ((back_keep, 0), (back_send, 0), (back_keep, unit), (back_send, unit))
    ):
        for m in range(count):
            for c in range(cuts):
                at = c * block + (d * count + m) * HALO
                part = slice(c * HALO, (c + 1) * HALO)
                layer = (frames[d, m, part, :].astype(F32) + proj[at : at + HALO]).astype(BF)
                dconv = dconv_s[at : at + HALO, :].astype(BF)
                for lc in range(cols):
                    for kind, value in enumerate((layer, dconv)):
                        to = base + ((kind * count + m) * cols + lc) * sub + c * HALO
                        out[to : to + HALO, :] = value[:, lc * LANES : (lc + 1) * LANES]


def total(*parts):
    return functools.reduce(lambda x, y: x + y, [x.astype(F32) for x in parts]).astype(BF)


def final_kernel(plan, first_call, bits, a_near, b_near, a_far, b_far, *refs):
    width, norm = plan
    cols = width // LANES
    size = cols * width // 8
    span = size + HALO
    if first_call:
        outs, tails, (grad_s, sems) = refs[:4], refs[4], refs[5:]
    else:
        tails, outs, taps, (grad_s, sems, tail_s) = refs[4], refs[5:9], refs[9], refs[10:]
    core = bits[CORE]
    owner = core if first_call else 1 - core
    for h in range(2):
        first, second, third = ways(bits, h)
        parts = ((a_near, a_far), (b_near, b_far))[h]
        for rel in range(8):
            part, start = parts[rel // 4], rel % 4 * span
            piece = (first ^ (rel // 4)) * 4 + (second ^ (rel // 2 % 2)) * 2 + (third ^ (rel % 2))
            cb, at = piece * size // width, piece * size % width
            grad_s[
                h,
                pl.ds(pl.multiple_of(at, size), size),
                pl.ds(pl.multiple_of(cb * LANES, LANES), LANES),
            ] = part[start : start + size, :].astype(F32) * norm
            tail = part[start + size : start + span, :].astype(F32) * norm
            if first_call:
                tails[h * 8 + piece] = tail
            else:
                tail_s[owner * 16 + h * 8 + piece] = tail
        for which in range(2):
            @pl.when(owner == which)
            def _():
                pltpu.make_async_copy(grad_s.at[h], outs[2 * which + h], sems.at[h]).start()
    if not first_call:
        for n in range(16):
            tail_s[core * 16 + n] = tails[n]
        for g in range(32):
            row = g * cols
            lc, j = row // 32, row % 32
            kept = min(cols, 31 - j)
            taps[j : j + kept, lc * LANES : (lc + 1) * LANES] = tail_s[g, 0:kept]
    for h in range(2):
        for which in range(2):
            @pl.when(owner == which)
            def _():
                pltpu.make_async_copy(grad_s.at[h], outs[2 * which + h], sems.at[h]).wait()


def home_kernel(plan, bits, own, core_got, y_got, layer_out, dconv, x_edge, z_edge):
    count, sub, cols = plan
    unit = 2 * count * cols * sub
    odd = bits[X]
    last = 3 * sub + sub - HALO
    for d, (ref, base) in enumerate(
        ((own, 0), (core_got, 0), (y_got, 0), (y_got, unit))
    ):
        to = pl.ds(pl.multiple_of(bits[BLOCK_AT + d] * sub, sub), sub)
        for m in range(count):
            for lc in range(cols):
                at = base + (m * cols + lc) * sub
                layer_out[m, to, lc * LANES : (lc + 1) * LANES] = ref[at : at + sub, :]
                at += count * cols * sub
                dconv[m, lc, to, :] = ref[at : at + sub, :]
    for m in range(count):
        for lc in range(cols):
            at = (m * cols + lc) * HALO
            x_rows = pl.ds(pl.multiple_of((1 - odd) * last, HALO), HALO)
            z_rows = pl.ds(pl.multiple_of(odd * last, HALO), HALO)
            x_edge[at : at + HALO, :] = dconv[m, lc, x_rows, :]
            z_edge[at : at + HALO, :] = dconv[m, lc, z_rows, :]


def frame_kernel(plan, bits, dconv, x_got, z_got, cot, kern, frame_grad):
    count, cols, x_at, length = plan
    is_odd = jnp.broadcast_to(bits[X], (HALO, LANES)) == 1

    def step(m, _):
        for lc in range(cols):
            lanes = slice(lc * LANES, (lc + 1) * LANES)
            at = pl.multiple_of((m * cols + lc) * HALO, HALO)
            one = x_got[pl.ds(pl.multiple_of(x_at + at, HALO), HALO), :].astype(F32)
            two = z_got[pl.ds(at, HALO), :].astype(F32)
            x = jnp.concatenate(
                [
                    jnp.where(is_odd, one, two),
                    dconv[m, lc].astype(F32),
                    jnp.where(is_odd, two, one),
                ],
                axis=0,
            )
            grad = window(x, lambda o: kern[31 - o : 32 - o, lanes], length)
            frame_grad[m, :, lanes] = (cot[m, :, lanes].astype(F32) + grad).astype(BF)
        return 0

    lax.fori_loop(0, count, step, 0)


def call(body, outs, scratch, limit, *args, hbm=(), hbm_outs=(), aliases=None):
    spaces = [pltpu.HBM if i in hbm else pltpu.VMEM for i in range(len(args))]
    return pl.pallas_call(
        body,
        out_shape=outs,
        in_specs=[
            pl.BlockSpec(memory_space=pltpu.SMEM if x.dtype == jnp.int32 else space)
            for x, space in zip(args, spaces)
        ],
        out_specs=tuple(
            pl.BlockSpec(memory_space=pltpu.HBM if i in hbm_outs else pltpu.VMEM)
            for i in range(len(outs))
        ),
        scratch_shapes=scratch,
        input_output_aliases=aliases or {},
        compiler_params=pltpu.CompilerParams(vmem_limit_bytes=limit * MIB),
    )(*args)


def shards(frames, cotangent, kernel, w_query, w_key, w_value, w_out):
    groups, blocks = lax.axis_size("mic"), lax.axis_size("tm")
    count, length, width = frames.shape
    sub = length // groups
    cuts = sub // HALO
    cols = width // LANES
    rows = groups * count * sub
    shape = jax.ShapeDtypeStruct

    mic, tm = lax.axis_index("mic"), lax.axis_index("tm")
    over_core, over_y, over_x, over_z = blocks, 2 * blocks, 1, 2

    def order(a):
        return (a ^ (a >> 1)) ^ (3 * (tm % 2))

    mine = order(mic)
    bits = jnp.stack(
        [mic % 2, mic // 2, tm % 2, tm // 2 % 2, tm // 4 % 2, mine % 2, 2 * ((mine + 1) // 2 % 2)]
        + [order(mic ^ d) for d in range(4)]
    ).astype(jnp.int32)

    def permute(x, pairs):
        return lax.ppermute(x, ("mic", "tm"), pairs)

    def swap(x, mask):
        return permute(x, [(f, f ^ mask) for f in range(groups * blocks)])

    def both(pairs):
        return pairs + [(j, i) for i, j in pairs]

    block = shape((count, sub, width), BF)
    masks = (0, over_core, over_y, over_core + over_y)

    def scattered(x):
        parts = call(
            functools.partial(scatter_kernel, sub), (block,) * 4,
            [pltpu.SemaphoreType.DMA((4,))], 8, bits, x, hbm=(1,),
        )
        got = {d: swap(parts[d], masks[d]) for d in (2, 3, 1)}
        return [parts[0], got[1], got[2], got[3]]

    f, c = scattered(frames), scattered(cotangent)
    weights = jnp.stack([w_query, w_key, w_value, w_out])
    edge = shape((groups, count, HALO, width), BF)
    near, side = call(functools.partial(edge_kernel, sub), (edge, edge), [], 8, bits, *f)
    near, side, weights = lax.optimization_barrier((near, side, weights))
    near = swap(near, over_core)
    side = permute(
        side,
        both([(blocks + t, 3 * blocks + t) for t in range(blocks)])
        + both([((2 - 2 * (t % 2)) * blocks + t, (2 - 2 * (t % 2)) * blocks + t + 1)
                for t in range(blocks - 1)]),
    )

    factor = 1.0 / math.sqrt(width // HEADS)
    size = width * width // LANES // 8
    span = size + HALO
    unit = 2 * count * cols * sub
    big = pltpu.VMEM((rows, width), BF)
    wide = pltpu.VMEM((rows, width), F32)

    def flat(n):
        return shape((n, LANES), BF)

    moved = shape((groups, count, sub, width), BF)
    placed, conv, acted = call(
        functools.partial(conv_kernel, (groups, count, sub, width)),
        (moved, shape((rows, width), F32), shape((rows, width), BF)),
        [], 8, bits, *f, near, side, kernel,
    )
    a_keep, b_keep, a_send, b_send, back_keep, back_send = call(
        functools.partial(main_kernel, (groups, count, sub, width, factor)),
        (flat(8 * span),) * 4 + (flat(2 * unit),) * 2,
        [
            pltpu.VMEM((2, rows, width), BF),
            pltpu.VMEM((4, cuts, groups, count, HALO, width), BF),
            big, big, big, big, wide,
            pltpu.VMEM((32 * cols + HALO, LANES), F32),
        ],
        24, bits, placed, conv, acted, *c, near, side, weights,
    )

    lines = [2**i for i in range(1, blocks.bit_length() - 1)]

    def sent(parts, n):
        return total(*(t[n : 2 * n] for t in parts))

    def kept(parts, got, n):
        return [t[:n] for t in parts] + [got[:n]]

    def halved(parts, n, mask):
        return kept(parts, swap(sent(parts, n), mask), n)

    def exchanged(parts, masks):
        mine = total(*parts)
        for mask in masks:
            mine = total(mine, swap(mine, mask))
        return mine

    def doubled(x, mask):
        return jnp.concatenate([x, swap(x, mask)])

    a = [a_keep, swap(a_send, over_core)]
    b = [b_keep, swap(b_send, over_core)]
    core_got = swap(back_send, over_core)
    a = halved(a, 4 * span, over_x)
    b = halved(b, 4 * span, lines[0])
    y_got = swap(jnp.concatenate([back_keep[unit:], core_got[unit:]]), over_y)
    edge = flat(count * cols * HALO)
    layer_out, dconv, x_edge, z_edge = call(
        functools.partial(home_kernel, (count, sub, cols)),
        (shape(frames.shape, BF), shape((count, cols, length, LANES), BF), edge, edge),
        [], 8, bits, back_keep, core_got, y_got,
    )
    z_got = permute(
        z_edge,
        both([(m * blocks + t, m * blocks + t + 1)
              for m in range(groups) for t in range(1, blocks - 1, 2)]),
    )
    a = halved(a, 2 * span, over_y)
    b = halved(b, 2 * span, lines[1])
    a = halved(a, span, lines[0])
    x_got = swap(jnp.concatenate([sent(b, span), x_edge]), over_x)
    b = kept(b, x_got, span)
    a = exchanged(a, lines[1:])
    b = exchanged(b, [over_y] + lines[2:])
    a = doubled(a, lines[0])
    b = doubled(b, over_x)
    b, z_got = lax.optimization_barrier((b, z_got))
    (frame_grad,) = call(
        functools.partial(frame_kernel, (count, cols, span, length)),
        (shape(frames.shape, BF),), [], 8, bits, dconv, x_got, z_got, cotangent, kernel,
    )
    a = doubled(a, over_y)
    b = doubled(b, lines[1])
    a_far, b_far = swap(a, over_x), swap(b, lines[0])
    a_other, b_other = swap(a, over_core), swap(b, over_core)
    a_other_far, b_other_far = swap(a_far, over_core), swap(b_far, over_core)

    norm = 1.0 / math.sqrt(groups * count * blocks * length)
    square = shape((width, width), F32)
    scratch = [pltpu.VMEM((2, width, width), F32), pltpu.SemaphoreType.DMA((2,))]
    final = functools.partial(final_kernel, (width, norm))
    *grads, tails = call(
        functools.partial(final, True), (square,) * 4 + (shape((16, HALO, LANES), F32),), scratch,
        8, bits, a, b, a_far, b_far, hbm_outs=range(4),
    )
    *grads, kernel_grad = call(
        functools.partial(final, False), (square,) * 4 + (shape((31, width), F32),),
        scratch + [pltpu.VMEM((32, HALO, LANES), F32)],
        8, bits, a_other, b_other, a_other_far, b_other_far, *grads, tails,
        hbm=range(5, 9), hbm_outs=range(4), aliases={5 + i: i for i in range(4)},
    )
    return (layer_out, frame_grad, kernel_grad, *grads)


def solution(mesh):
    in_specs = (P("mic", "tm", None), P("mic", "tm", None), P(), P(), P(), P(), P())
    out_specs = (P("mic", "tm", None), P("mic", "tm", None), P(), P(), P(), P(), P())
    return jax.shard_map(shards, mesh=mesh, in_specs=in_specs, out_specs=out_specs, check_vma=False)
```

```python
import functools
import math

import jax
import jax.numpy as jnp
from jax import lax
from jax.experimental import pallas as pl
from jax.experimental.pallas import tpu as pltpu
from jax.sharding import PartitionSpec as P

HEADS = 8
LANES = 128
HALO = 16
NT = (((1,), (1,)), ((), ()))
TN = (((0,), (0,)), ((), ()))
BF = jnp.bfloat16
F32 = jnp.float32
MIB = 1024 * 1024
CHAINS = 2
CORE, Y, X, Z, ZZ, BLOCK_AT = range(6)


def mm(left, right, dims=(((1,), (0,)), ((), ()))):
    return lax.dot_general(left, right, dims, preferred_element_type=F32)


def rolled(x, shift):
    return x if shift == 0 else pltpu.roll(x, x.shape[0] - shift, axis=0)


def window(x, taps, rows):
    acc = None
    for r in range(8):
        xr = rolled(x, r)
        for k in range(4):
            o = 8 * k + r
            if o == 0:
                continue
            term = xr[8 * k : 8 * k + rows] * taps(o)
            acc = term if acc is None else acc + term
    return acc


def ways(bits, half):
    return (bits[X], bits[Y], bits[Z]) if half == 0 else (bits[Z], bits[ZZ], 0)


def sigmoid(v):
    return 0.5 * jnp.tanh(0.5 * v) + 0.5


def scatter_kernel(sub, bits, source, *refs):
    outs, sems = refs[:4], refs[4]
    copies = []
    for d in range(4):
        rows = pl.ds(pl.multiple_of(bits[BLOCK_AT + d] * sub, sub), sub)
        copies.append(pltpu.make_async_copy(source.at[:, rows], outs[d], sems.at[d]))
    for copy in copies:
        copy.start()
    for copy in copies:
        copy.wait()


def padded(bits, rows, x_got, z_got, m, lanes):
    is_odd = jnp.broadcast_to(bits[X], (HALO, LANES)) == 1
    one, two = x_got[m, :, lanes].astype(F32), z_got[m, :, lanes].astype(F32)
    return jnp.concatenate(
        [
            jnp.where(is_odd, one, two),
            rows[m, :, lanes].astype(F32),
            jnp.where(is_odd, two, one),
        ],
        axis=0,
    )


def lanes_of(width):
    return [slice(at, at + LANES) for at in range(0, width, LANES)]


def conv_kernel(sub, bits, frames, x_got, z_got, kern, conv_out, *refs):
    outs, act_s = refs[:4], refs[4]
    count, length, width = frames.shape
    half = length // 2

    def step(m, _):
        for lanes in lanes_of(width):
            x = padded(bits, frames, x_got, z_got, m, lanes)
            for at in (0, half):
                conv = window(
                    x[at : at + half + 2 * HALO], lambda o: kern[o - 1 : o, lanes], half
                )
                conv_out[m, at : at + half, lanes] = conv
                act_s[m, at : at + half, lanes] = (conv * sigmoid(conv)).astype(BF)
        return 0

    lax.fori_loop(0, count, step, 0)
    for d, out in enumerate(outs):
        out[...] = act_s[:, pl.ds(pl.multiple_of(bits[BLOCK_AT + d] * sub, sub), sub), :]


def main_kernel(
    plan, bits, a0, a1, a2, a3, c0, c1, c2, c3, weights,
    a_keep, b_keep, a_send, b_send, back_keep, back_send,
    left_s, right_s, q_s, k_s, v_s, u_s,
):
    groups, count, sub, width, factor = plan
    mics = groups * count
    cuts = sub // HALO
    block = mics * HALO
    rows = cuts * block
    cols = width // LANES

    wq, wk, wv, wo = (weights.at[i] for i in range(4))
    for d, (act, cot) in enumerate(((a0, c0), (a1, c1), (a2, c2), (a3, c3))):
        for m in range(count):
            for c in range(cuts):
                part = slice(c * HALO, (c + 1) * HALO)
                at = c * block + (d * count + m) * HALO
                left_s[0, at : at + HALO, :] = act[m, part, :]
                right_s[3, c, d, m] = cot[m, part, :]

    def flat(i):
        return right_s[i].reshape(rows, width)

    def put(i, c, lanes, x):
        right_s[i, c, :, :, :, lanes] = x.astype(BF).reshape(groups, count, HALO, LANES)

    acted = left_s[0]
    q_s[...] = mm(acted, wq[...]).astype(BF)
    k_s[...] = mm(acted, wk[...]).astype(BF)
    v_s[...] = mm(acted, wv[...]).astype(BF)
    u_s[...] = mm(flat(3), wo[...], NT).astype(BF)

    depth = width // HEADS
    per = LANES // depth
    lane = lax.broadcasted_iota(jnp.int32, (block, LANES), 1)
    row_i = lax.broadcasted_iota(jnp.int32, (block, per * block), 0)
    col_i = lax.broadcasted_iota(jnp.int32, (block, per * block), 1)
    same = (row_i % HALO) == (col_i % HALO)

    def by_head(x):
        return jnp.concatenate(
            [jnp.where(lane // depth == h, x, jnp.zeros_like(x)) for h in range(per)], axis=0
        )

    def sums(x):
        return [
            jnp.sum(x[:, h * block : (h + 1) * block], axis=1, keepdims=True) for h in range(per)
        ]

    def each(x, values, op):
        return jnp.concatenate(
            [op(x[:, h * block : (h + 1) * block], values[h]) for h in range(per)], axis=1
        )

    def pick(x):
        out = x[:block]
        for h in range(1, per):
            out = jnp.where(lane // depth == h, x[h * block : (h + 1) * block], out)
        return out

    for c in range(cuts):
        part = slice(c * block, (c + 1) * block)
        for p in range(cols):
            lanes = slice(p * LANES, (p + 1) * LANES)
            q, u = q_s[part, lanes], u_s[part, lanes]
            kc, vc = by_head(k_s[part, lanes]), by_head(v_s[part, lanes])
            e = jnp.where(same, jnp.exp(mm(q, kc, NT) * factor), 0.0)
            w = each(e, [1.0 / x for x in sums(e)], lambda x, s: x * s)
            up = mm(u, vc, NT)
            inner = each(up, sums(w * up), lambda x, s: x - s) * w * factor
            wb, ib = w.astype(BF), inner.astype(BF)
            left_s[1, part, lanes] = mm(wb, vc).astype(BF)
            put(0, c, lanes, mm(ib, kc))
            put(1, c, lanes, pick(mm(ib, q, TN)))
            put(2, c, lanes, pick(mm(wb, u, TN)))

    dacted = mm(flat(0), wq[...], NT) + mm(flat(1), wk[...], NT) + mm(flat(2), wv[...], NT)
    size = cols * width // 8 // CHAINS
    core = bits[CORE]
    for out, owner, h in (
        (a_send, 1 - core, 0), (b_send, 1 - core, 1), (a_keep, core, 0), (b_keep, core, 1)
    ):
        i = owner * 2 + h
        first, second, third = ways(bits, h)
        grad = mm(left_s[i // 3], flat(i), TN).astype(BF)
        for piece in range(8):
            rel = ((piece // 4) ^ first) * 4 + ((piece // 2 % 2) ^ second) * 2 + ((piece % 2) ^ third)
            for chain in range(CHAINS):
                at = (piece * CHAINS + chain) * size
                cb, at = at // width, at % width
                start = pl.multiple_of((chain * 8 + rel) * size, size)
                out[pl.ds(start, size), :] = grad[at : at + size, cb * LANES : (cb + 1) * LANES]

    unit = 2 * count * cols * sub
    for d, (out, base) in enumerate(
        ((back_keep, 0), (back_send, 0), (back_keep, unit), (back_send, unit))
    ):
        for m in range(count):
            for c in range(cuts):
                at = c * block + (d * count + m) * HALO
                for kind in range(2):
                    rows_of = left_s[1, at : at + HALO, :] if kind == 0 else dacted[
                        at : at + HALO
                    ].astype(BF)
                    for lc in range(cols):
                        to = base + ((kind * count + m) * cols + lc) * sub + c * HALO
                        out[to : to + HALO, :] = rows_of[:, lc * LANES : (lc + 1) * LANES]


def total(*parts):
    return functools.reduce(lambda x, y: x + y, [x.astype(F32) for x in parts]).astype(BF)


def final_kernel(plan, first_call, bits, *refs):
    width, norm = plan
    cols = width // LANES
    size = cols * width // 8 // CHAINS
    got, refs = refs[: 2 * CHAINS], refs[2 * CHAINS :]
    if first_call:
        taps, outs, tap_grad, grad_s, sems = refs[0], refs[1:5], refs[5], refs[6], refs[7]
        for lc in range(cols):
            tap_grad[:, lc * LANES : (lc + 1) * LANES] = (
                taps[lc * 32 : lc * 32 + 31, :].astype(F32) * norm
            )
    else:
        outs, grad_s, sems = refs[4:8], refs[8], refs[9]
    core = bits[CORE]
    owner = core if first_call else 1 - core
    for h in range(2):
        first, second, third = ways(bits, h)
        for rel in range(8):
            piece = (first ^ (rel // 4)) * 4 + (second ^ (rel // 2 % 2)) * 2 + (third ^ (rel % 2))
            for chain in range(CHAINS):
                at = (piece * CHAINS + chain) * size
                cb, at = at // width, at % width
                grad_s[
                    h,
                    pl.ds(pl.multiple_of(at, size), size),
                    pl.ds(pl.multiple_of(cb * LANES, LANES), LANES),
                ] = got[h * CHAINS + chain][rel * size : (rel + 1) * size, :].astype(F32) * norm
        for which in range(2):
            @pl.when(owner == which)
            def _():
                pltpu.make_async_copy(grad_s.at[h], outs[2 * which + h], sems.at[h]).start()
    for h in range(2):
        for which in range(2):
            @pl.when(owner == which)
            def _():
                pltpu.make_async_copy(grad_s.at[h], outs[2 * which + h], sems.at[h]).wait()


def home_chunks(plan, bits, own, core_got, y_got, kind):
    count, sub, cols = plan
    part = count * cols * sub
    for d, (ref, base) in enumerate(
        ((own, 0), (core_got, 0), (y_got, 0), (y_got, 2 * part))
    ):
        to = pl.ds(pl.multiple_of(bits[BLOCK_AT + d] * sub, sub), sub)
        for m in range(count):
            for lc in range(cols):
                at = base + kind * part + (m * cols + lc) * sub
                yield ref[at : at + sub, :], m, to, slice(lc * LANES, (lc + 1) * LANES)


def dconv_kernel(plan, bits, own, core_got, y_got, conv_in, dconv, x_edge, z_edge):
    for dacted, m, to, lanes in home_chunks(plan, bits, own, core_got, y_got, 1):
        conv = conv_in[m, to, lanes]
        sig = sigmoid(conv)
        dconv[m, to, lanes] = dacted.astype(F32) * sig * (1.0 + conv * (1.0 - sig))
    last = dconv.shape[1] - HALO
    odd = bits[X]
    x_edge[...] = dconv[:, pl.ds(pl.multiple_of((1 - odd) * last, HALO), HALO), :].astype(BF)
    z_edge[...] = dconv[:, pl.ds(pl.multiple_of(odd * last, HALO), HALO), :].astype(BF)


def layer_kernel(plan, bits, own, core_got, y_got, frames, weights, layer_out, mix_s):
    for mixed, m, to, lanes in home_chunks(plan, bits, own, core_got, y_got, 0):
        mix_s[m, to, lanes] = mixed
    for m in range(plan[0]):
        proj = mm(mix_s[m], weights[3])
        layer_out[m] = (frames[m].astype(F32) + proj).astype(BF)


def tap_kernel(sub, bits, frames, x_got, z_got, dconv, taps, pad_s):
    count, length, width = frames.shape
    for m in range(count):
        for lanes in lanes_of(width):
            pad_s[m, :, lanes] = padded(bits, frames, x_got, z_got, m, lanes)
    for lc, lanes in enumerate(lanes_of(width)):

        def step(n, accs):
            m = n // (length // sub)
            at = pl.multiple_of(n % (length // sub) * sub, sub)
            x = pad_s[m, pl.ds(at, sub + 2 * HALO), lanes]
            d = dconv[m, pl.ds(at, sub), lanes]
            out = list(accs)
            for r in range(8):
                xr = rolled(x, r)
                for k in range(4):
                    o = 8 * k + r
                    if o == 0:
                        continue
                    prod = xr[8 * k : 8 * k + sub] * d
                    out[o - 1] = out[o - 1] + jnp.sum(prod.reshape(sub // 8, 8, LANES), axis=0)
            return tuple(out)

        zeros = tuple(jnp.zeros((8, LANES), F32) for _ in range(31))
        accs = lax.fori_loop(0, count * (length // sub), step, zeros)
        taps[lc * 32 : lc * 32 + 32, :] = jnp.concatenate(
            [jnp.sum(x, axis=0, keepdims=True) for x in accs] + [jnp.zeros((1, LANES), F32)], axis=0
        ).astype(BF)


def frame_kernel(bits, dconv, x_got, z_got, cot, kern, frame_grad):
    count, length, width = dconv.shape
    half = length // 2

    def step(m, _):
        for lanes in lanes_of(width):
            x = padded(bits, dconv, x_got, z_got, m, lanes)
            for at in (0, half):
                part = slice(at, at + half)
                grad = window(
                    x[at : at + half + 2 * HALO], lambda o: kern[31 - o : 32 - o, lanes], half
                )
                frame_grad[m, part, lanes] = (cot[m, part, lanes].astype(F32) + grad).astype(BF)
        return 0

    lax.fori_loop(0, count, step, 0)


def call(body, outs, scratch, limit, *args, hbm=(), hbm_outs=(), aliases=None):
    spaces = [pltpu.HBM if i in hbm else pltpu.VMEM for i in range(len(args))]
    return pl.pallas_call(
        body,
        out_shape=outs,
        in_specs=[
            pl.BlockSpec(memory_space=pltpu.SMEM if x.dtype == jnp.int32 else space)
            for x, space in zip(args, spaces)
        ],
        out_specs=tuple(
            pl.BlockSpec(memory_space=pltpu.HBM if i in hbm_outs else pltpu.VMEM)
            for i in range(len(outs))
        ),
        scratch_shapes=scratch,
        input_output_aliases=aliases or {},
        compiler_params=pltpu.CompilerParams(vmem_limit_bytes=limit * MIB),
    )(*args)


def shards(frames, cotangent, kernel, w_query, w_key, w_value, w_out):
    groups, blocks = lax.axis_size("mic"), lax.axis_size("tm")
    count, length, width = frames.shape
    sub = length // groups
    cuts = sub // HALO
    cols = width // LANES
    rows = groups * count * sub
    shape = jax.ShapeDtypeStruct

    mic, tm = lax.axis_index("mic"), lax.axis_index("tm")
    over_core, over_y, over_x = blocks, 2 * blocks, 1
    lines = [2**i for i in range(1, blocks.bit_length() - 1)]
    odd = tm % 2
    bits = jnp.stack(
        [mic % 2, mic // 2, odd, tm // 2 % 2, tm // 4 % 2] + [mic ^ d for d in range(4)]
    ).astype(jnp.int32)

    def permute(x, pairs):
        return lax.ppermute(x, ("mic", "tm"), pairs)

    def swap(x, mask):
        return permute(x, [(f, f ^ mask) for f in range(groups * blocks)])

    def swap_edges(x_edge, z_edge):
        pairs = [(m * blocks + t, m * blocks + t + 1)
                 for m in range(groups) for t in range(1, blocks - 1, 2)]
        return swap(x_edge, over_x), permute(z_edge, pairs + [(j, i) for i, j in pairs])

    def spread(parts):
        masks = (0, over_core, over_y, over_core + over_y)
        got = {d: swap(parts[d], masks[d]) for d in (2, 3, 1)}
        return [parts[0], got[1], got[2], got[3]]

    last = length - HALO
    frame_x, frame_z = swap_edges(
        lax.dynamic_slice_in_dim(frames, (1 - odd) * last, HALO, axis=1),
        lax.dynamic_slice_in_dim(frames, odd * last, HALO, axis=1),
    )
    block = shape((count, sub, width), BF)
    cot_parts = spread(
        call(
            functools.partial(scatter_kernel, sub), (block,) * 4,
            [pltpu.SemaphoreType.DMA((4,))], 8, bits, cotangent, hbm=(1,),
        )
    )
    weights = jnp.stack([w_query, w_key, w_value, w_out])
    wide = shape(frames.shape, F32)
    here = pltpu.VMEM(frames.shape, BF)
    conv, *acted = call(
        functools.partial(conv_kernel, sub), (wide,) + (block,) * 4, [here],
        8, bits, frames, frame_x, frame_z, kernel,
    )
    *acted, weights = lax.optimization_barrier((*acted, weights))

    factor = 1.0 / math.sqrt(width // HEADS)
    part = width * width // LANES // CHAINS
    unit = 2 * count * cols * sub
    big = pltpu.VMEM((rows, width), BF)

    def flat(n):
        return shape((n, LANES), BF)

    a_keep, b_keep, a_send, b_send, back_keep, back_send = call(
        functools.partial(main_kernel, (groups, count, sub, width, factor)),
        (flat(CHAINS * part),) * 4 + (flat(2 * unit),) * 2,
        [
            pltpu.VMEM((2, rows, width), BF),
            pltpu.VMEM((4, cuts, groups, count, HALO, width), BF),
            big, big, big, big,
        ],
        24, bits, *spread(acted), *cot_parts, weights,
    )

    def halved(parts, mask):
        n = parts[0].shape[0] // 2
        return [t[:n] for t in parts] + [swap(total(*(t[n:] for t in parts)), mask)]

    def exchanged(x, masks):
        for mask in masks:
            x = total(x, swap(x, mask))
        return x

    def doubled(x, mask):
        return jnp.concatenate([x, swap(x, mask)])

    def chains(*arrays):
        return [[t[i * part : (i + 1) * part] for t in arrays] for i in range(CHAINS)]

    def after(x, y):
        return lax.optimization_barrier((x, y))[0]

    a = chains(a_keep, swap(a_send, over_core))
    b = chains(b_keep, swap(b_send, over_core))
    core_got = swap(back_send, over_core)
    y_got = swap(jnp.concatenate([back_keep[unit:], core_got[unit:]]), over_y)
    a = [halved(t, over_x) for t in a]
    b = [halved(t, lines[0]) for t in b]
    plan = (count, sub, cols)
    y_got = after(y_got, (a[0][-1], b[0][-1]))
    home = (bits, back_keep, core_got, y_got)
    edge = shape((count, HALO, width), BF)
    dconv, x_edge, z_edge = call(
        functools.partial(dconv_kernel, plan), (wide, edge, edge), [], 8, *home, conv
    )
    x_edge, z_edge = swap_edges(x_edge, z_edge)
    a = [halved(t, over_y) for t in a]
    b = [halved(t, lines[1]) for t in b]
    (taps,) = call(
        functools.partial(tap_kernel, sub), (flat(32 * cols),),
        [pltpu.VMEM((count, length + 2 * HALO, width), F32)],
        8, bits, frames, frame_x, frame_z, after(dconv, a[0][-1]),
    )
    taps = exchanged(taps, lines + [over_x, over_y, over_core])
    a = [exchanged(total(*halved(t, lines[0])), lines[1:]) for t in a]
    b = [exchanged(total(*t), [over_x, over_y] + lines[2:]) for t in b]
    (frame_grad,) = call(
        frame_kernel, (shape(frames.shape, BF),), [], 8,
        bits, after(dconv, a[0]), x_edge, z_edge, cotangent, kernel,
    )
    a = [doubled(t, lines[0]) for t in a]
    b = [doubled(t, lines[1]) for t in b]
    (layer_out,) = call(
        functools.partial(layer_kernel, plan), (shape(frames.shape, BF),), [here],
        10, *home, after(frames, a[0]), weights,
    )
    a = [doubled(t, over_y) for t in a]
    a = [doubled(t, over_x) for t in a]
    b = [doubled(t, lines[0]) for t in b]
    *a, b[-1], frame_grad, layer_out = lax.optimization_barrier(
        (*a, b[-1], frame_grad, layer_out)
    )
    other = [swap(t, over_core) for t in a + b]

    norm = 1.0 / math.sqrt(groups * count * blocks * length)
    square = shape((width, width), F32)
    scratch = [pltpu.VMEM((2, width, width), F32), pltpu.SemaphoreType.DMA((2,))]
    final = functools.partial(final_kernel, (width, norm))
    *grads, kernel_grad = call(
        functools.partial(final, True), (square,) * 4 + (shape((31, width), F32),), scratch,
        8, bits, *a, *b, taps, hbm_outs=range(4),
    )
    first = 1 + 2 * CHAINS
    grads = call(
        functools.partial(final, False), (square,) * 4, scratch,
        8, bits, *other, *grads, hbm=range(first, first + 4), hbm_outs=range(4),
        aliases={first + i: i for i in range(4)},
    )
    return (layer_out, frame_grad, kernel_grad, *grads)


def solution(mesh):
    in_specs = (P("mic", "tm", None), P("mic", "tm", None), P(), P(), P(), P(), P())
    out_specs = (P("mic", "tm", None), P("mic", "tm", None), P(), P(), P(), P(), P())
    return jax.shard_map(shards, mesh=mesh, in_specs=in_specs, out_specs=out_specs, check_vma=False)
```

```python
import functools
import math

import jax
import jax.numpy as jnp
from jax import lax
from jax.experimental import pallas as pl
from jax.experimental.pallas import tpu as pltpu
from jax.sharding import PartitionSpec as P

HEADS = 8
LANES = 128
HALO = 16
NT = (((1,), (1,)), ((), ()))
TN = (((0,), (0,)), ((), ()))
BF = jnp.bfloat16
F32 = jnp.float32
MIB = 1024 * 1024
CORE, Y, X, Z, ZZ, BLOCK_AT = range(6)


def mm(left, right, dims=(((1,), (0,)), ((), ()))):
    return lax.dot_general(left, right, dims, preferred_element_type=F32)


def rolled(x, shift):
    return x if shift == 0 else pltpu.roll(x, x.shape[0] - shift, axis=0)


def window(x, taps, rows):
    acc = None
    for r in range(8):
        xr = rolled(x, r)
        for k in range(4):
            o = 8 * k + r
            if o == 0:
                continue
            term = xr[8 * k : 8 * k + rows] * taps(o)
            acc = term if acc is None else acc + term
    return acc


def ways(bits, half):
    return [bits[i] for i in ((X, Y, ZZ), (Z, X, Y))[half]]


def sigmoid(v):
    return 0.5 * jnp.tanh(0.5 * v) + 0.5


def padded(bits, rows, x_got, z_got, m, lanes):
    is_odd = jnp.broadcast_to(bits[X], (HALO, LANES)) == 1
    one, two = x_got[m, :, lanes].astype(F32), z_got[m, :, lanes].astype(F32)
    return jnp.concatenate(
        [
            jnp.where(is_odd, one, two),
            rows[m, :, lanes].astype(F32),
            jnp.where(is_odd, two, one),
        ],
        axis=0,
    )


def lanes_of(width):
    return [slice(at, at + LANES) for at in range(0, width, LANES)]


def conv_kernel(sub, bits, frames, x_got, z_got, kern, conv_out, *refs):
    outs, act_s = refs[:4], refs[4]
    count, length, width = frames.shape
    half = length // 2

    def step(m, _):
        for lanes in lanes_of(width):
            x = padded(bits, frames, x_got, z_got, m, lanes)
            for at in (0, half):
                conv = window(
                    x[at : at + half + 2 * HALO], lambda o: kern[o - 1 : o, lanes], half
                )
                conv_out[m, at : at + half, lanes] = conv
                act_s[m, at : at + half, lanes] = (conv * sigmoid(conv)).astype(BF)
        return 0

    lax.fori_loop(0, count, step, 0)
    for d, out in enumerate(outs):
        out[...] = act_s[:, pl.ds(pl.multiple_of(bits[BLOCK_AT + d] * sub, sub), sub), :]


def main_kernel(
    plan, bits, a0, a1, a2, a3, c0, c1, c2, c3, weights,
    a_keep, b_keep, a_send, b_send, back_keep, back_send,
    left_s, right_s, q_s, k_s, v_s, u_s,
):
    groups, count, sub, width, factor = plan
    mics = groups * count
    cuts = sub // HALO
    block = mics * HALO
    rows = cuts * block
    cols = width // LANES

    wq, wk, wv, wo = (weights.at[i] for i in range(4))
    for d, (act, cot) in enumerate(((a0, c0), (a1, c1), (a2, c2), (a3, c3))):
        for m in range(count):
            for c in range(cuts):
                part = slice(c * HALO, (c + 1) * HALO)
                at = c * block + (d * count + m) * HALO
                left_s[0, at : at + HALO, :] = act[m, part, :]
                right_s[3, c, d, m] = cot[m, part, :]

    def flat(i):
        return right_s[i].reshape(rows, width)

    def put(i, c, lanes, x):
        right_s[i, c, :, :, :, lanes] = x.astype(BF).reshape(groups, count, HALO, LANES)

    acted = left_s[0]
    q_s[...] = mm(acted, wq[...]).astype(BF)
    k_s[...] = mm(acted, wk[...]).astype(BF)
    v_s[...] = mm(acted, wv[...]).astype(BF)
    u_s[...] = mm(flat(3), wo[...], NT).astype(BF)

    depth = width // HEADS
    per = LANES // depth
    lane = lax.broadcasted_iota(jnp.int32, (block, LANES), 1)
    row_i = lax.broadcasted_iota(jnp.int32, (block, per * block), 0)
    col_i = lax.broadcasted_iota(jnp.int32, (block, per * block), 1)
    same = (row_i % HALO) == (col_i % HALO)

    def by_head(x):
        return jnp.concatenate(
            [jnp.where(lane // depth == h, x, jnp.zeros_like(x)) for h in range(per)], axis=0
        )

    def sums(x):
        return [
            jnp.sum(x[:, h * block : (h + 1) * block], axis=1, keepdims=True) for h in range(per)
        ]

    def each(x, values, op):
        return jnp.concatenate(
            [op(x[:, h * block : (h + 1) * block], values[h]) for h in range(per)], axis=1
        )

    def pick(x):
        out = x[:block]
        for h in range(1, per):
            out = jnp.where(lane // depth == h, x[h * block : (h + 1) * block], out)
        return out

    for c in range(cuts):
        part = slice(c * block, (c + 1) * block)
        for p in range(cols):
            lanes = slice(p * LANES, (p + 1) * LANES)
            q, u = q_s[part, lanes], u_s[part, lanes]
            kc, vc = by_head(k_s[part, lanes]), by_head(v_s[part, lanes])
            e = jnp.where(same, jnp.exp(mm(q, kc, NT) * factor), 0.0)
            w = each(e, [1.0 / x for x in sums(e)], lambda x, s: x * s)
            up = mm(u, vc, NT)
            inner = each(up, sums(w * up), lambda x, s: x - s) * w * factor
            wb, ib = w.astype(BF), inner.astype(BF)
            left_s[1, part, lanes] = mm(wb, vc).astype(BF)
            put(0, c, lanes, mm(ib, kc))
            put(1, c, lanes, pick(mm(ib, q, TN)))
            put(2, c, lanes, pick(mm(wb, u, TN)))

    dacted = mm(flat(0), wq[...], NT) + mm(flat(1), wk[...], NT) + mm(flat(2), wv[...], NT)
    size = cols * width // 8
    core = bits[CORE]
    for out, owner, h in (
        (a_send, 1 - core, 0), (b_send, 1 - core, 1), (a_keep, core, 0), (b_keep, core, 1)
    ):
        i = owner * 2 + h
        first, second, third = ways(bits, h)
        grad = mm(left_s[i // 3], flat(i), TN).astype(BF)
        for piece in range(8):
            rel = ((piece // 4) ^ first) * 4 + ((piece // 2 % 2) ^ second) * 2 + ((piece % 2) ^ third)
            cb, at = piece * size // width, piece * size % width
            out[pl.ds(pl.multiple_of(rel * size, size), size), :] = grad[
                at : at + size, cb * LANES : (cb + 1) * LANES
            ]

    unit = 2 * count * cols * sub
    for d, (out, base) in enumerate(
        ((back_keep, 0), (back_send, 0), (back_keep, unit), (back_send, unit))
    ):
        for m in range(count):
            for c in range(cuts):
                at = c * block + (d * count + m) * HALO
                for kind in range(2):
                    rows_of = left_s[1, at : at + HALO, :] if kind == 0 else dacted[
                        at : at + HALO
                    ].astype(BF)
                    for lc in range(cols):
                        to = base + ((kind * count + m) * cols + lc) * sub + c * HALO
                        out[to : to + HALO, :] = rows_of[:, lc * LANES : (lc + 1) * LANES]


def total(*parts):
    return functools.reduce(lambda x, y: x + y, [x.astype(F32) for x in parts]).astype(BF)


def final_kernel(plan, bits, *refs):
    kinds, first_call, width, norm = plan
    cols = width // LANES
    size = cols * width // 8
    got, refs = refs[: len(kinds)], refs[len(kinds) :]
    if not first_call:
        refs = refs[4:]
    outs, piece_s, sems = refs[:4], refs[4], refs[5]
    core = bits[CORE]
    copies = []
    for n, (own, h, far) in enumerate(kinds):
        owner = core if own else 1 - core
        first, second, third = ways(bits, h)
        for rel in range(4):
            k = 4 * n + rel
            piece_s[k] = got[n][rel * size : (rel + 1) * size, :].astype(F32) * norm
            piece = (first ^ far) * 4 + (second ^ (rel // 2)) * 2 + (third ^ (rel % 2))
            cb, at = piece * size // width, piece * size % width
            rows = pl.ds(pl.multiple_of(at, size), size)
            lanes = pl.ds(pl.multiple_of(cb * LANES, LANES), LANES)
            for which in range(2):
                copy = pltpu.make_async_copy(
                    piece_s.at[k], outs[2 * which + h].at[rows, lanes], sems.at[k]
                )
                copies.append((owner == which, copy))
                pl.when(owner == which)(copy.start)
    for here, copy in copies:
        pl.when(here)(copy.wait)


def tap_grad_kernel(norm, taps, grad):
    for lc, lanes in enumerate(lanes_of(grad.shape[1])):
        grad[:, lanes] = taps[lc * 32 : lc * 32 + 31, :].astype(F32) * norm


def home_chunks(plan, bits, own, core_got, y_got, kind):
    count, sub, cols = plan
    part = count * cols * sub
    for d, (ref, base) in enumerate(
        ((own, 0), (core_got, 0), (y_got, 0), (y_got, 2 * part))
    ):
        to = pl.ds(pl.multiple_of(bits[BLOCK_AT + d] * sub, sub), sub)
        for m in range(count):
            for lc in range(cols):
                at = base + kind * part + (m * cols + lc) * sub
                yield ref[at : at + sub, :], m, to, slice(lc * LANES, (lc + 1) * LANES)


def dconv_kernel(plan, bits, own, core_got, y_got, conv_in, dconv, x_edge, z_edge):
    for dacted, m, to, lanes in home_chunks(plan, bits, own, core_got, y_got, 1):
        conv = conv_in[m, to, lanes]
        sig = sigmoid(conv)
        dconv[m, to, lanes] = dacted.astype(F32) * sig * (1.0 + conv * (1.0 - sig))
    last = dconv.shape[1] - HALO
    odd = bits[X]
    x_edge[...] = dconv[:, pl.ds(pl.multiple_of((1 - odd) * last, HALO), HALO), :].astype(BF)
    z_edge[...] = dconv[:, pl.ds(pl.multiple_of(odd * last, HALO), HALO), :].astype(BF)


def layer_kernel(plan, bits, own, core_got, y_got, frames, weights, layer_out, mix_s):
    for mixed, m, to, lanes in home_chunks(plan, bits, own, core_got, y_got, 0):
        mix_s[m, to, lanes] = mixed
    for m in range(plan[0]):
        proj = mm(mix_s[m], weights[3])
        layer_out[m] = (frames[m].astype(F32) + proj).astype(BF)


def tap_kernel(sub, bits, frames, x_got, z_got, dconv, taps, pad_s):
    count, length, width = frames.shape
    for m in range(count):
        for lanes in lanes_of(width):
            pad_s[m, :, lanes] = padded(bits, frames, x_got, z_got, m, lanes)
    for lc, lanes in enumerate(lanes_of(width)):

        def step(n, accs):
            m = n // (length // sub)
            at = pl.multiple_of(n % (length // sub) * sub, sub)
            x = pad_s[m, pl.ds(at, sub + 2 * HALO), lanes]
            d = dconv[m, pl.ds(at, sub), lanes]
            out = list(accs)
            for r in range(8):
                xr = rolled(x, r)
                for k in range(4):
                    o = 8 * k + r
                    if o == 0:
                        continue
                    prod = xr[8 * k : 8 * k + sub] * d
                    out[o - 1] = out[o - 1] + jnp.sum(prod.reshape(sub // 8, 8, LANES), axis=0)
            return tuple(out)

        zeros = tuple(jnp.zeros((8, LANES), F32) for _ in range(31))
        accs = lax.fori_loop(0, count * (length // sub), step, zeros)
        taps[lc * 32 : lc * 32 + 32, :] = jnp.concatenate(
            [jnp.sum(x, axis=0, keepdims=True) for x in accs] + [jnp.zeros((1, LANES), F32)], axis=0
        ).astype(BF)


def frame_kernel(bits, dconv, x_got, z_got, cot, kern, frame_grad):
    count, length, width = dconv.shape
    half = length // 2

    def step(m, _):
        for lanes in lanes_of(width):
            x = padded(bits, dconv, x_got, z_got, m, lanes)
            for at in (0, half):
                part = slice(at, at + half)
                grad = window(
                    x[at : at + half + 2 * HALO], lambda o: kern[31 - o : 32 - o, lanes], half
                )
                frame_grad[m, part, lanes] = (cot[m, part, lanes].astype(F32) + grad).astype(BF)
        return 0

    lax.fori_loop(0, count, step, 0)


def call(body, outs, scratch, limit, *args, hbm=(), hbm_outs=(), aliases=None):
    spaces = [pltpu.HBM if i in hbm else pltpu.VMEM for i in range(len(args))]
    return pl.pallas_call(
        body,
        out_shape=outs,
        in_specs=[
            pl.BlockSpec(memory_space=pltpu.SMEM if x.dtype == jnp.int32 else space)
            for x, space in zip(args, spaces)
        ],
        out_specs=tuple(
            pl.BlockSpec(memory_space=pltpu.HBM if i in hbm_outs else pltpu.VMEM)
            for i in range(len(outs))
        ),
        scratch_shapes=scratch,
        input_output_aliases=aliases or {},
        compiler_params=pltpu.CompilerParams(vmem_limit_bytes=limit * MIB),
    )(*args)


def shards(frames, cotangent, kernel, w_query, w_key, w_value, w_out):
    groups, blocks = lax.axis_size("mic"), lax.axis_size("tm")
    count, length, width = frames.shape
    sub = length // groups
    cuts = sub // HALO
    cols = width // LANES
    rows = groups * count * sub
    shape = jax.ShapeDtypeStruct

    mic, tm = lax.axis_index("mic"), lax.axis_index("tm")
    over_core, over_y, over_x = blocks, 2 * blocks, 1
    lines = [2**i for i in range(1, blocks.bit_length() - 1)]
    odd = tm % 2
    bits = jnp.stack(
        [mic % 2, mic // 2, odd, tm // 2 % 2, tm // 4 % 2] + [mic ^ d for d in range(4)]
    ).astype(jnp.int32)

    def permute(x, pairs):
        return lax.ppermute(x, ("mic", "tm"), pairs)

    def swap(x, mask):
        return permute(x, [(f, f ^ mask) for f in range(groups * blocks)])

    def swap_edges(x_edge, z_edge):
        pairs = [(m * blocks + t, m * blocks + t + 1)
                 for m in range(groups) for t in range(1, blocks - 1, 2)]
        return swap(x_edge, over_x), permute(z_edge, pairs + [(j, i) for i, j in pairs])

    def spread(parts):
        masks = (0, over_core, over_y, over_core + over_y)
        got = {d: swap(parts[d], masks[d]) for d in (2, 3, 1)}
        return [parts[0], got[1], got[2], got[3]]

    last = length - HALO
    frame_x, frame_z = swap_edges(
        lax.dynamic_slice_in_dim(frames, (1 - odd) * last, HALO, axis=1),
        lax.dynamic_slice_in_dim(frames, odd * last, HALO, axis=1),
    )
    cot_parts = spread(
        [lax.dynamic_slice_in_dim(cotangent, (mic ^ d) * sub, sub, axis=1) for d in range(4)]
    )
    block = shape((count, sub, width), BF)
    wide = shape(frames.shape, F32)
    here = pltpu.VMEM(frames.shape, BF)
    conv, *acted = call(
        functools.partial(conv_kernel, sub), (wide,) + (block,) * 4, [here],
        8, bits, frames, frame_x, frame_z, kernel,
    )
    own_acted, *weights = lax.optimization_barrier(
        (acted[0], w_query, w_key, w_value, w_out)
    )
    weights = jnp.stack(weights)

    factor = 1.0 / math.sqrt(width // HEADS)
    part = width * width // LANES
    unit = 2 * count * cols * sub
    big = pltpu.VMEM((rows, width), BF)

    def flat(n):
        return shape((n, LANES), BF)

    a_keep, b_keep, a_send, b_send, back_keep, back_send = call(
        functools.partial(main_kernel, (groups, count, sub, width, factor)),
        (flat(part),) * 4 + (flat(2 * unit),) * 2,
        [
            pltpu.VMEM((2, rows, width), BF),
            pltpu.VMEM((4, cuts, groups, count, HALO, width), BF),
            big, big, big, big,
        ],
        24, bits, *spread([own_acted] + acted[1:]), *cot_parts, weights,
    )

    def halved(parts, mask):
        n = parts[0].shape[0] // 2
        return [t[:n] for t in parts] + [swap(total(*(t[n:] for t in parts)), mask)]

    def exchanged(x, masks):
        for mask in masks:
            x = total(x, swap(x, mask))
        return x

    def doubled(x, mask):
        return jnp.concatenate([x, swap(x, mask)])

    def after(x, y):
        return lax.optimization_barrier((x, y))[0]

    a = [a_keep, swap(a_send, over_core)]
    b = [b_keep, swap(b_send, over_core)]
    core_got = swap(back_send, over_core)
    y_got = swap(jnp.concatenate([back_keep[unit:], core_got[unit:]]), over_y)
    a = halved(a, over_x)
    b = halved(b, lines[0])
    plan = (count, sub, cols)
    y_got = after(y_got, (a[-1], b[-1]))
    home = (bits, back_keep, core_got, y_got)
    edge = shape((count, HALO, width), BF)
    dconv, x_edge, z_edge = call(
        functools.partial(dconv_kernel, plan), (wide, edge, edge), [], 8, *home, conv
    )
    x_edge, z_edge = swap_edges(x_edge, z_edge)
    a = halved(a, over_y)
    b = halved(b, over_x)
    (taps,) = call(
        functools.partial(tap_kernel, sub), (flat(32 * cols),),
        [pltpu.VMEM((count, length + 2 * HALO, width), F32)],
        8, bits, frames, frame_x, frame_z, after(dconv, a[-1]),
    )
    taps = exchanged(taps, lines)
    a = exchanged(total(*halved(a, lines[1])), lines[:1] + lines[2:])
    b = exchanged(total(*halved(b, over_y)), lines[1:])
    (frame_grad,) = call(
        frame_kernel, (shape(frames.shape, BF),), [], 8,
        bits, after(dconv, a), x_edge, z_edge, cotangent, kernel,
    )
    a = doubled(after(a, (taps, z_edge)), lines[1])
    b = doubled(b, over_y)
    taps = exchanged(taps, [over_x, over_y])
    (layer_out,) = call(
        functools.partial(layer_kernel, plan), (shape(frames.shape, BF),), [here],
        10, *home, after(frames, a), weights,
    )
    a = doubled(a, over_y)
    b = doubled(after(b, taps), over_x)
    taps = exchanged(taps, [over_core])

    norm = 1.0 / math.sqrt(groups * count * blocks * length)
    square = shape((width, width), F32)

    def final(kinds, parts, grads):
        first = 1 + len(parts)
        return call(
            functools.partial(final_kernel, (kinds, not grads, width, norm)), (square,) * 4,
            [
                pltpu.VMEM((4 * len(parts), part // 8, LANES), F32),
                pltpu.SemaphoreType.DMA((4 * len(parts),)),
            ],
            10, bits, *parts, *grads, hbm=range(first, first + len(grads)), hbm_outs=range(4),
            aliases={first + i: i for i in range(len(grads))},
        )

    a_far, b_far = swap(a, over_x), swap(b, lines[0])
    a_other, b_other = swap(a, over_core), swap(b, over_core)
    grads = final(
        ((1, 0, 0), (1, 1, 0), (0, 0, 0), (0, 1, 0)), (a, b, a_other, b_other), ()
    )
    a_far, b_far, taps, frame_grad, layer_out, *grads = lax.optimization_barrier(
        (a_far, b_far, taps, frame_grad, layer_out, *grads)
    )
    a_other, b_other = swap(a_far, over_core), swap(b_far, over_core)
    grads = final(((1, 0, 1), (1, 1, 1)), (a_far, b_far), grads)
    grads = final(((0, 0, 1), (0, 1, 1)), (a_other, b_other), grads)
    (kernel_grad,) = call(
        functools.partial(tap_grad_kernel, norm), (shape((31, width), F32),), [], 4, taps
    )
    return (layer_out, frame_grad, kernel_grad, *grads)


def solution(mesh):
    in_specs = (P("mic", "tm", None), P("mic", "tm", None), P(), P(), P(), P(), P())
    out_specs = (P("mic", "tm", None), P("mic", "tm", None), P(), P(), P(), P(), P())
    return jax.shard_map(shards, mesh=mesh, in_specs=in_specs, out_specs=out_specs, check_vma=False)
```

```python
import functools
import math

import jax
import jax.numpy as jnp
from jax import lax
from jax.experimental import pallas as pl
from jax.experimental.pallas import tpu as pltpu
from jax.sharding import PartitionSpec as P

HEADS = 8
LANES = 128
HALO = 16
NT = (((1,), (1,)), ((), ()))
TN = (((0,), (0,)), ((), ()))
BF = jnp.bfloat16
F32 = jnp.float32
MIB = 1024 * 1024
CORE, Y, X, Z, ZZ, BLOCK_AT = range(6)


def mm(left, right, dims=(((1,), (0,)), ((), ()))):
    return lax.dot_general(left, right, dims, preferred_element_type=F32)


def rolled(x, shift):
    return x if shift == 0 else pltpu.roll(x, x.shape[0] - shift, axis=0)


def window(x, taps, rows):
    acc = None
    for r in range(8):
        xr = rolled(x, r)
        for k in range(4):
            o = 8 * k + r
            if o == 0:
                continue
            term = xr[8 * k : 8 * k + rows] * taps(o)
            acc = term if acc is None else acc + term
    return acc


def ways(bits, half):
    return [bits[i] for i in ((X, Y, ZZ), (Z, X, Y))[half]]


def sigmoid(v):
    return 0.5 * jnp.tanh(0.5 * v) + 0.5


def padded(bits, rows, one, two):
    is_odd = jnp.broadcast_to(bits[X], (HALO, LANES)) == 1
    one, two = one.astype(F32), two.astype(F32)
    return jnp.concatenate(
        [jnp.where(is_odd, one, two), rows.astype(F32), jnp.where(is_odd, two, one)], axis=0
    )


def near_edge(bits):
    return pl.ds(pl.multiple_of(bits[X] * HALO, HALO), HALO)


def padded_frames(bits, frames, x_got, z_got, m, lanes):
    return padded(bits, frames[m, :, lanes], x_got[m, near_edge(bits), lanes], z_got[m, :, lanes])


def lanes_of(width):
    return [slice(at, at + LANES) for at in range(0, width, LANES)]


def conv_kernel(sub, bits, frames, x_got, z_got, kern, conv_out, *refs):
    outs, act_s = refs[:4], refs[4]
    count, length, width = frames.shape
    half = length // 2

    def step(m, _):
        for lanes in lanes_of(width):
            x = padded_frames(bits, frames, x_got, z_got, m, lanes)
            for at in (0, half):
                conv = window(
                    x[at : at + half + 2 * HALO], lambda o: kern[o - 1 : o, lanes], half
                )
                conv_out[m, at : at + half, lanes] = conv
                act_s[m, at : at + half, lanes] = (conv * sigmoid(conv)).astype(BF)
        return 0

    lax.fori_loop(0, count, step, 0)
    for d, out in enumerate(outs):
        out[...] = act_s[:, pl.ds(pl.multiple_of(bits[BLOCK_AT + d] * sub, sub), sub), :]


def main_kernel(
    plan, bits, a0, a1, a2, a3, c0, c1, c2, c3, weights,
    a_keep, b_keep, a_send, b_send, back_keep, back_send,
    left_s, right_s, q_s, k_s, v_s, u_s,
):
    groups, count, sub, width, factor = plan
    mics = groups * count
    cuts = sub // HALO
    block = mics * HALO
    rows = cuts * block
    cols = width // LANES

    wq, wk, wv, wo = (weights.at[i] for i in range(4))
    for d, (act, cot) in enumerate(((a0, c0), (a1, c1), (a2, c2), (a3, c3))):
        for m in range(count):
            for c in range(cuts):
                part = slice(c * HALO, (c + 1) * HALO)
                at = c * block + (d * count + m) * HALO
                left_s[0, at : at + HALO, :] = act[m, part, :]
                right_s[3, c, d, m] = cot[m, part, :]

    def flat(i):
        return right_s[i].reshape(rows, width)

    def put(i, c, lanes, x):
        right_s[i, c, :, :, :, lanes] = x.astype(BF).reshape(groups, count, HALO, LANES)

    acted = left_s[0]
    q_s[...] = mm(acted, wq[...]).astype(BF)
    k_s[...] = mm(acted, wk[...]).astype(BF)
    v_s[...] = mm(acted, wv[...]).astype(BF)
    u_s[...] = mm(flat(3), wo[...], NT).astype(BF)

    depth = width // HEADS
    per = LANES // depth
    lane = lax.broadcasted_iota(jnp.int32, (block, LANES), 1)
    row_i = lax.broadcasted_iota(jnp.int32, (block, per * block), 0)
    col_i = lax.broadcasted_iota(jnp.int32, (block, per * block), 1)
    same = (row_i % HALO) == (col_i % HALO)

    def by_head(x):
        return jnp.concatenate(
            [jnp.where(lane // depth == h, x, jnp.zeros_like(x)) for h in range(per)], axis=0
        )

    def sums(x):
        return [
            jnp.sum(x[:, h * block : (h + 1) * block], axis=1, keepdims=True) for h in range(per)
        ]

    def each(x, values, op):
        return jnp.concatenate(
            [op(x[:, h * block : (h + 1) * block], values[h]) for h in range(per)], axis=1
        )

    def pick(x):
        out = x[:block]
        for h in range(1, per):
            out = jnp.where(lane // depth == h, x[h * block : (h + 1) * block], out)
        return out

    for c in range(cuts):
        part = slice(c * block, (c + 1) * block)
        for p in range(cols):
            lanes = slice(p * LANES, (p + 1) * LANES)
            q, u = q_s[part, lanes], u_s[part, lanes]
            kc, vc = by_head(k_s[part, lanes]), by_head(v_s[part, lanes])
            e = jnp.where(same, jnp.exp(mm(q, kc, NT) * factor), 0.0)
            w = each(e, [1.0 / x for x in sums(e)], lambda x, s: x * s)
            up = mm(u, vc, NT)
            inner = each(up, sums(w * up), lambda x, s: x - s) * w * factor
            wb, ib = w.astype(BF), inner.astype(BF)
            left_s[1, part, lanes] = mm(wb, vc).astype(BF)
            put(0, c, lanes, mm(ib, kc))
            put(1, c, lanes, pick(mm(ib, q, TN)))
            put(2, c, lanes, pick(mm(wb, u, TN)))

    dacted = mm(flat(0), wq[...], NT) + mm(flat(1), wk[...], NT) + mm(flat(2), wv[...], NT)
    size = cols * width // 8
    core = bits[CORE]
    for out, owner, h in (
        (a_send, 1 - core, 0), (b_send, 1 - core, 1), (a_keep, core, 0), (b_keep, core, 1)
    ):
        i = owner * 2 + h
        first, second, third = ways(bits, h)
        grad = mm(left_s[i // 3], flat(i), TN).astype(BF)
        for piece in range(8):
            rel = ((piece // 4) ^ first) * 4 + ((piece // 2 % 2) ^ second) * 2 + ((piece % 2) ^ third)
            cb, at = piece * size // width, piece * size % width
            out[pl.ds(pl.multiple_of(rel * size, size), size), :] = grad[
                at : at + size, cb * LANES : (cb + 1) * LANES
            ]

    unit = 2 * count * cols * sub
    for d, (out, base) in enumerate(
        ((back_keep, 0), (back_send, 0), (back_keep, unit), (back_send, unit))
    ):
        for m in range(count):
            for c in range(cuts):
                at = c * block + (d * count + m) * HALO
                for kind in range(2):
                    rows_of = left_s[1, at : at + HALO, :] if kind == 0 else dacted[
                        at : at + HALO
                    ].astype(BF)
                    for lc in range(cols):
                        to = base + ((kind * count + m) * cols + lc) * sub + c * HALO
                        out[to : to + HALO, :] = rows_of[:, lc * LANES : (lc + 1) * LANES]


def total(*parts):
    return functools.reduce(lambda x, y: x + y, [x.astype(F32) for x in parts]).astype(BF)


def final_kernel(plan, bits, *refs):
    kinds, first_call, width, norm = plan
    cols = width // LANES
    size = cols * width // 8
    got, refs = refs[: len(kinds)], refs[len(kinds) :]
    if first_call:
        taps, *outs, tap_grad, piece_s, sems = refs
        for lc, lanes in enumerate(lanes_of(width)):
            tap_grad[:, lanes] = taps[lc * 32 : lc * 32 + 31, :].astype(F32) * norm
    else:
        outs, piece_s, sems = refs[4:8], refs[8], refs[9]
    core = bits[CORE]
    copies = []
    for n, (own, h, far) in enumerate(kinds):
        owner = core if own else 1 - core
        first, second, third = ways(bits, h)
        for rel in range(4):
            k = 4 * n + rel
            piece_s[k] = got[n][rel * size : (rel + 1) * size, :].astype(F32) * norm
            piece = (first ^ far) * 4 + (second ^ (rel // 2)) * 2 + (third ^ (rel % 2))
            cb, at = piece * size // width, piece * size % width
            rows = pl.ds(pl.multiple_of(at, size), size)
            lanes = pl.ds(pl.multiple_of(cb * LANES, LANES), LANES)
            for which in range(2):
                copy = pltpu.make_async_copy(
                    piece_s.at[k], outs[2 * which + h].at[rows, lanes], sems.at[k]
                )
                copies.append((owner == which, copy))
                pl.when(owner == which)(copy.start)
    for here, copy in copies:
        pl.when(here)(copy.wait)


def home_chunks(plan, bits, own, core_got, y_got, kind):
    count, sub, cols = plan
    part = count * cols * sub
    for d, (ref, base) in enumerate(
        ((own, 0), (core_got, 0), (y_got, 0), (y_got, 2 * part))
    ):
        to = pl.ds(pl.multiple_of(bits[BLOCK_AT + d] * sub, sub), sub)
        for m in range(count):
            for lc in range(cols):
                at = base + kind * part + (m * cols + lc) * sub
                yield ref[at : at + sub, :], m, to, slice(lc * LANES, (lc + 1) * LANES)


def dconv_kernel(plan, bits, own, core_got, y_got, conv_in, dconv, edges):
    for dacted, m, to, lanes in home_chunks(plan, bits, own, core_got, y_got, 1):
        conv = conv_in[m, to, lanes]
        sig = sigmoid(conv)
        dconv[m, to, lanes] = dacted.astype(F32) * sig * (1.0 + conv * (1.0 - sig))
    count, length, width = dconv.shape
    for m in range(count):
        for lc, lanes in enumerate(lanes_of(width)):
            at = (m * plan[2] + lc) * 2 * HALO
            edges[at : at + HALO, :] = dconv[m, :HALO, lanes].astype(BF)
            edges[at + HALO : at + 2 * HALO, :] = dconv[m, length - HALO :, lanes].astype(BF)


def layer_kernel(plan, bits, own, core_got, y_got, frames, weights, layer_out, mix_s):
    for mixed, m, to, lanes in home_chunks(plan, bits, own, core_got, y_got, 0):
        mix_s[m, to, lanes] = mixed
    for m in range(plan[0]):
        proj = mm(mix_s[m], weights[3])
        layer_out[m] = (frames[m].astype(F32) + proj).astype(BF)


def tap_kernel(sub, bits, frames, x_got, z_got, dconv, taps, pad_s):
    count, length, width = frames.shape
    for m in range(count):
        for lanes in lanes_of(width):
            pad_s[m, :, lanes] = padded_frames(bits, frames, x_got, z_got, m, lanes)
    for lc, lanes in enumerate(lanes_of(width)):

        def step(n, accs):
            m = n // (length // sub)
            at = pl.multiple_of(n % (length // sub) * sub, sub)
            x = pad_s[m, pl.ds(at, sub + 2 * HALO), lanes]
            d = dconv[m, pl.ds(at, sub), lanes]
            out = list(accs)
            for r in range(8):
                xr = rolled(x, r)
                for k in range(4):
                    o = 8 * k + r
                    if o == 0:
                        continue
                    prod = xr[8 * k : 8 * k + sub] * d
                    out[o - 1] = out[o - 1] + jnp.sum(prod.reshape(sub // 8, 8, LANES), axis=0)
            return tuple(out)

        zeros = tuple(jnp.zeros((8, LANES), F32) for _ in range(31))
        accs = lax.fori_loop(0, count * (length // sub), step, zeros)
        taps[lc * 32 : lc * 32 + 32, :] = jnp.concatenate(
            [jnp.sum(x, axis=0, keepdims=True) for x in accs] + [jnp.zeros((1, LANES), F32)], axis=0
        ).astype(BF)


def frame_kernel(bits, dconv, x_got, z_got, cot, kern, frame_grad):
    count, length, width = dconv.shape
    half = length // 2

    def step(m, _):
        for lc, lanes in enumerate(lanes_of(width)):
            n = m * (width // LANES) + lc
            x_rows = pl.ds(pl.multiple_of((2 * n + bits[X]) * HALO, HALO), HALO)
            z_rows = pl.ds(pl.multiple_of(n * HALO, HALO), HALO)
            x = padded(bits, dconv[m, :, lanes], x_got[x_rows, :], z_got[z_rows, :])
            for at in (0, half):
                part = slice(at, at + half)
                grad = window(
                    x[at : at + half + 2 * HALO], lambda o: kern[31 - o : 32 - o, lanes], half
                )
                frame_grad[m, part, lanes] = (cot[m, part, lanes].astype(F32) + grad).astype(BF)
        return 0

    lax.fori_loop(0, count, step, 0)


def call(body, outs, scratch, limit, *args, hbm=(), hbm_outs=(), aliases=None):
    spaces = [pltpu.HBM if i in hbm else pltpu.VMEM for i in range(len(args))]
    return pl.pallas_call(
        body,
        out_shape=outs,
        in_specs=[
            pl.BlockSpec(memory_space=pltpu.SMEM if x.dtype == jnp.int32 else space)
            for x, space in zip(args, spaces)
        ],
        out_specs=tuple(
            pl.BlockSpec(memory_space=pltpu.HBM if i in hbm_outs else pltpu.VMEM)
            for i in range(len(outs))
        ),
        scratch_shapes=scratch,
        input_output_aliases=aliases or {},
        compiler_params=pltpu.CompilerParams(vmem_limit_bytes=limit * MIB),
    )(*args)


def shards(frames, cotangent, kernel, w_query, w_key, w_value, w_out):
    groups, blocks = lax.axis_size("mic"), lax.axis_size("tm")
    count, length, width = frames.shape
    sub = length // groups
    cuts = sub // HALO
    cols = width // LANES
    rows = groups * count * sub
    shape = jax.ShapeDtypeStruct

    mic, tm = lax.axis_index("mic"), lax.axis_index("tm")
    over_core, over_y, over_x = blocks, 2 * blocks, 1
    lines = [2**i for i in range(1, blocks.bit_length() - 1)]
    odd = tm % 2
    bits = jnp.stack(
        [mic % 2, mic // 2, odd, tm // 2 % 2, tm // 4 % 2] + [mic ^ d for d in range(4)]
    ).astype(jnp.int32)

    def permute(x, pairs):
        return lax.ppermute(x, ("mic", "tm"), pairs)

    def swap(x, mask):
        return permute(x, [(f, f ^ mask) for f in range(groups * blocks)])

    def passed_on(x, axis):
        x = lax.dynamic_slice_in_dim(x, (1 - odd) * HALO, HALO, axis=axis)
        pairs = [(t, t + 2) if t % 2 == 0 else (t + 2, t) for t in range(blocks - 2)]
        return permute(
            x, [(m * blocks + i, m * blocks + j) for m in range(groups) for i, j in pairs]
        )

    def spread(parts):
        masks = (0, over_core, over_y, over_core + over_y)
        got = {d: swap(parts[d], masks[d]) for d in (2, 3, 1)}
        return [parts[0], got[1], got[2], got[3]]

    frame_x = swap(
        jnp.concatenate([frames[:, :HALO], frames[:, length - HALO :]], axis=1), over_x
    )
    frame_z = passed_on(frame_x, 1)
    cot_parts = spread(
        [lax.dynamic_slice_in_dim(cotangent, (mic ^ d) * sub, sub, axis=1) for d in range(4)]
    )
    block = shape((count, sub, width), BF)
    wide = shape(frames.shape, F32)
    here = pltpu.VMEM(frames.shape, BF)
    conv, *acted = call(
        functools.partial(conv_kernel, sub), (wide,) + (block,) * 4, [here],
        8, bits, frames, frame_x, frame_z, kernel,
    )
    own_acted, *weights = lax.optimization_barrier(
        (acted[0], w_query, w_key, w_value, w_out)
    )
    weights = jnp.stack(weights)

    factor = 1.0 / math.sqrt(width // HEADS)
    part = width * width // LANES
    unit = 2 * count * cols * sub
    big = pltpu.VMEM((rows, width), BF)

    def flat(n):
        return shape((n, LANES), BF)

    a_keep, b_keep, a_send, b_send, back_keep, back_send = call(
        functools.partial(main_kernel, (groups, count, sub, width, factor)),
        (flat(part),) * 4 + (flat(2 * unit),) * 2,
        [
            pltpu.VMEM((2, rows, width), BF),
            pltpu.VMEM((4, cuts, groups, count, HALO, width), BF),
            big, big, big, big,
        ],
        24, bits, *spread([own_acted] + acted[1:]), *cot_parts, weights,
    )

    def halved(parts, mask):
        n = parts[0].shape[0] // 2
        return [t[:n] for t in parts] + [swap(total(*(t[n:] for t in parts)), mask)]

    def exchanged(x, masks):
        for mask in masks:
            x = total(x, swap(x, mask))
        return x

    def doubled(x, mask):
        return jnp.concatenate([x, swap(x, mask)])

    def after(x, y):
        return lax.optimization_barrier((x, y))[0]

    a = [a_keep, swap(a_send, over_core)]
    b = [b_keep, swap(b_send, over_core)]
    core_got = swap(back_send, over_core)
    y_got = swap(jnp.concatenate([back_keep[unit:], core_got[unit:]]), over_y)
    a = halved(a, over_x)
    b = halved(b, lines[0])
    plan = (count, sub, cols)
    y_got = after(y_got, (a[-1], b[-1]))
    home = (bits, back_keep, core_got, y_got)
    dconv, edges = call(
        functools.partial(dconv_kernel, plan), (wide, flat(2 * count * cols * HALO)), [], 8,
        *home, conv,
    )
    a = halved(a, over_y)
    b = halved(b, over_x)
    (taps,) = call(
        functools.partial(tap_kernel, sub), (flat(32 * cols),),
        [pltpu.VMEM((count, length + 2 * HALO, width), F32)],
        8, bits, frames, frame_x, frame_z, after(dconv, a[-1]),
    )
    n = taps.shape[0]
    got = swap(jnp.concatenate([taps, edges]), over_x)
    taps, x_edge = total(taps, got[:n]), got[n:]
    z_edge = passed_on(x_edge.reshape(count * cols, 2 * HALO, LANES), 1).reshape(-1, LANES)
    k = a[0].shape[0] // 2
    got = swap(jnp.concatenate([total(*(t[k:] for t in a)), taps]), lines[1])
    a = total(*(t[:k] for t in a), got[:k])
    taps = total(taps, got[k:])
    a = exchanged(jnp.concatenate([a, taps]), lines[:1] + lines[2:])
    a, taps = a[:k], a[k:]
    b = exchanged(total(*halved(b, over_y)), lines[1:])
    a = doubled(after(a, z_edge), lines[1])
    got = swap(jnp.concatenate([b, taps]), over_y)
    k = b.shape[0]
    b, taps = jnp.concatenate([b, got[:k]]), total(taps, got[k:])
    (frame_grad,) = call(
        frame_kernel, (shape(frames.shape, BF),), [], 8,
        bits, after(dconv, a), x_edge, z_edge, cotangent, kernel,
    )
    (layer_out,) = call(
        functools.partial(layer_kernel, plan), (shape(frames.shape, BF),), [here],
        10, *home, after(frames, a), weights,
    )
    a = doubled(a, over_y)
    b = doubled(b, over_x)

    norm = 1.0 / math.sqrt(groups * count * blocks * length)
    square = shape((width, width), F32)

    def final(kinds, parts, grads, taps=()):
        first = 1 + len(parts)
        return call(
            functools.partial(final_kernel, (kinds, not grads, width, norm)),
            (square,) * 4 + (shape((31, width), F32),) * len(taps),
            [
                pltpu.VMEM((4 * len(kinds), part // 8, LANES), F32),
                pltpu.SemaphoreType.DMA((4 * len(kinds),)),
            ],
            10, bits, *parts, *taps, *grads, hbm=range(first, first + len(grads)),
            hbm_outs=range(4), aliases={first + i: i for i in range(len(grads))},
        )

    a_far, b_far = swap(a, over_x), swap(b, lines[0])
    a_other, b_other = after((jnp.concatenate([a, taps]), b), frame_grad)
    a_other, b_other = swap(a_other, over_core), swap(b_other, over_core)
    k = a.shape[0]
    taps = total(taps, a_other[k:])
    *grads, kernel_grad = final(
        ((1, 0, 0), (1, 1, 0), (0, 0, 0), (0, 1, 0)), (a, b, a_other, b_other), (), (taps,)
    )
    a_far, b_far, frame_grad, layer_out, *grads = lax.optimization_barrier(
        (a_far, b_far, frame_grad, layer_out, *grads)
    )
    a_other, b_other = swap(a_far, over_core), swap(b_far, over_core)
    grads = final(((1, 0, 1), (1, 1, 1)), (a_far, b_far), grads)
    grads = final(((0, 0, 1), (0, 1, 1)), (a_other, b_other), grads)
    return (layer_out, frame_grad, kernel_grad, *grads)


def solution(mesh):
    in_specs = (P("mic", "tm", None), P("mic", "tm", None), P(), P(), P(), P(), P())
    out_specs = (P("mic", "tm", None), P("mic", "tm", None), P(), P(), P(), P(), P())
    return jax.shard_map(shards, mesh=mesh, in_specs=in_specs, out_specs=out_specs, check_vma=False)
```

```python
import functools
import math

import jax
import jax.numpy as jnp
from jax import lax
from jax.experimental import pallas as pl
from jax.experimental.pallas import tpu as pltpu
from jax.sharding import PartitionSpec as P

HEADS = 8
LANES = 128
HALO = 16
NT = (((1,), (1,)), ((), ()))
TN = (((0,), (0,)), ((), ()))
BF = jnp.bfloat16
F32 = jnp.float32
MIB = 1024 * 1024
CORE, Y, X, Z, ZZ, BLOCK_AT = range(6)


def mm(left, right, dims=(((1,), (0,)), ((), ()))):
    return lax.dot_general(left, right, dims, preferred_element_type=F32)


def rolled(x, shift):
    return x if shift == 0 else pltpu.roll(x, x.shape[0] - shift, axis=0)


def window(x, taps, rows):
    acc = None
    for r in range(8):
        xr = rolled(x, r)
        for k in range(4):
            o = 8 * k + r
            if o == 0:
                continue
            term = xr[8 * k : 8 * k + rows] * taps(o)
            acc = term if acc is None else acc + term
    return acc


def ways(bits, half):
    return [bits[i] for i in ((X, Y, ZZ), (Z, X, Y))[half]]


def sigmoid(v):
    return 0.5 * jnp.tanh(0.5 * v) + 0.5


def padded(bits, rows, one, two):
    is_odd = jnp.broadcast_to(bits[X], (HALO, LANES)) == 1
    one, two = one.astype(F32), two.astype(F32)
    return jnp.concatenate(
        [jnp.where(is_odd, one, two), rows.astype(F32), jnp.where(is_odd, two, one)], axis=0
    )


def padded_frames(bits, frames, x_got, z_got, m, lanes):
    return padded(bits, frames[m, :, lanes], x_got[m, :, lanes], z_got[m, :, lanes])


def lanes_of(width):
    return [slice(at, at + LANES) for at in range(0, width, LANES)]


def conv_kernel(sub, bits, frames, x_got, z_got, kern, conv_out, *refs):
    outs, act_s = refs[:4], refs[4]
    count, length, width = conv_out.shape
    half = length // 2

    def step(m, _):
        for lanes in lanes_of(width):
            x = padded_frames(bits, frames, x_got, z_got, m, lanes)
            for at in (0, half):
                conv = window(
                    x[at : at + half + 2 * HALO], lambda o: kern[o - 1 : o, lanes], half
                )
                conv_out[m, at : at + half, lanes] = conv
                act_s[m, at : at + half, lanes] = (conv * sigmoid(conv)).astype(BF)
        return 0

    lax.fori_loop(0, count, step, 0)
    for d, out in enumerate(outs):
        out[...] = act_s[:, pl.ds(pl.multiple_of(bits[BLOCK_AT + d] * sub, sub), sub), :]


def main_kernel(
    plan, bits, a0, a1, a2, a3, c0, c1, c2, c3, weights,
    a_keep, b_keep, a_send, b_send, back_keep, back_send,
    left_s, right_s, q_s, k_s, v_s, u_s,
):
    groups, count, sub, width, factor = plan
    mics = groups * count
    cuts = sub // HALO
    block = mics * HALO
    rows = cuts * block
    cols = width // LANES

    wq, wk, wv, wo = (weights.at[i] for i in range(4))
    for d, (act, cot) in enumerate(((a0, c0), (a1, c1), (a2, c2), (a3, c3))):
        for m in range(count):
            for c in range(cuts):
                part = slice(c * HALO, (c + 1) * HALO)
                at = c * block + (d * count + m) * HALO
                left_s[0, at : at + HALO, :] = act[m, part, :]
                right_s[3, c, d, m] = cot[m, part, :]

    def flat(i):
        return right_s[i].reshape(rows, width)

    def put(i, c, lanes, x):
        right_s[i, c, :, :, :, lanes] = x.astype(BF).reshape(groups, count, HALO, LANES)

    acted = left_s[0]
    q_s[...] = mm(acted, wq[...]).astype(BF)
    k_s[...] = mm(acted, wk[...]).astype(BF)
    v_s[...] = mm(acted, wv[...]).astype(BF)
    u_s[...] = mm(flat(3), wo[...], NT).astype(BF)

    depth = width // HEADS
    per = LANES // depth
    lane = lax.broadcasted_iota(jnp.int32, (block, LANES), 1)
    row_i = lax.broadcasted_iota(jnp.int32, (block, per * block), 0)
    col_i = lax.broadcasted_iota(jnp.int32, (block, per * block), 1)
    same = (row_i % HALO) == (col_i % HALO)

    def by_head(x):
        return jnp.concatenate(
            [jnp.where(lane // depth == h, x, jnp.zeros_like(x)) for h in range(per)], axis=0
        )

    def sums(x):
        return [
            jnp.sum(x[:, h * block : (h + 1) * block], axis=1, keepdims=True) for h in range(per)
        ]

    def each(x, values, op):
        return jnp.concatenate(
            [op(x[:, h * block : (h + 1) * block], values[h]) for h in range(per)], axis=1
        )

    def pick(x):
        out = x[:block]
        for h in range(1, per):
            out = jnp.where(lane // depth == h, x[h * block : (h + 1) * block], out)
        return out

    for c in range(cuts):
        part = slice(c * block, (c + 1) * block)
        for p in range(cols):
            lanes = slice(p * LANES, (p + 1) * LANES)
            q, u = q_s[part, lanes], u_s[part, lanes]
            kc, vc = by_head(k_s[part, lanes]), by_head(v_s[part, lanes])
            e = jnp.where(same, jnp.exp(mm(q, kc, NT) * factor), 0.0)
            w = each(e, [1.0 / x for x in sums(e)], lambda x, s: x * s)
            up = mm(u, vc, NT)
            inner = each(up, sums(w * up), lambda x, s: x - s) * w * factor
            wb, ib = w.astype(BF), inner.astype(BF)
            left_s[1, part, lanes] = mm(wb, vc).astype(BF)
            put(0, c, lanes, mm(ib, kc))
            put(1, c, lanes, pick(mm(ib, q, TN)))
            put(2, c, lanes, pick(mm(wb, u, TN)))

    dacted = mm(flat(0), wq[...], NT) + mm(flat(1), wk[...], NT) + mm(flat(2), wv[...], NT)
    size = cols * width // 8
    core = bits[CORE]
    for out, owner, h in (
        (a_send, 1 - core, 0), (b_send, 1 - core, 1), (a_keep, core, 0), (b_keep, core, 1)
    ):
        i = owner * 2 + h
        first, second, third = ways(bits, h)
        grad = mm(left_s[i // 3], flat(i), TN).astype(BF)
        for piece in range(8):
            rel = ((piece // 4) ^ first) * 4 + ((piece // 2 % 2) ^ second) * 2 + ((piece % 2) ^ third)
            cb, at = piece * size // width, piece * size % width
            out[pl.ds(pl.multiple_of(rel * size, size), size), :] = grad[
                at : at + size, cb * LANES : (cb + 1) * LANES
            ]

    unit = 2 * count * cols * sub
    for d, (out, base) in enumerate(
        ((back_keep, 0), (back_send, 0), (back_keep, unit), (back_send, unit))
    ):
        for m in range(count):
            for c in range(cuts):
                at = c * block + (d * count + m) * HALO
                for kind in range(2):
                    rows_of = left_s[1, at : at + HALO, :] if kind == 0 else dacted[
                        at : at + HALO
                    ].astype(BF)
                    for lc in range(cols):
                        to = base + ((kind * count + m) * cols + lc) * sub + c * HALO
                        out[to : to + HALO, :] = rows_of[:, lc * LANES : (lc + 1) * LANES]


def total(*parts):
    return functools.reduce(lambda x, y: x + y, [x.astype(F32) for x in parts]).astype(BF)


def final_kernel(plan, bits, *refs):
    kinds, first_call, with_taps, width, norm = plan
    cols = width // LANES
    size = cols * width // 8
    got, refs = refs[: len(kinds)], refs[len(kinds) :]
    if with_taps:
        taps, refs, tap_grad = refs[0], refs[1:-3] + refs[-2:], refs[-3]
        for lc, lanes in enumerate(lanes_of(width)):
            tap_grad[:, lanes] = taps[lc * 32 : lc * 32 + 31, :].astype(F32) * norm
    *outs, piece_s, sems = refs if first_call else refs[4:]
    core = bits[CORE]
    copies = []
    for n, (own, h, far) in enumerate(kinds):
        owner = core if own else 1 - core
        first, second, third = ways(bits, h)
        for rel in range(4):
            k = 4 * n + rel
            piece_s[k] = got[n][rel * size : (rel + 1) * size, :].astype(F32) * norm
            piece = (first ^ far) * 4 + (second ^ (rel // 2)) * 2 + (third ^ (rel % 2))
            cb, at = piece * size // width, piece * size % width
            rows = pl.ds(pl.multiple_of(at, size), size)
            lanes = pl.ds(pl.multiple_of(cb * LANES, LANES), LANES)
            for which in range(2):
                copy = pltpu.make_async_copy(
                    piece_s.at[k], outs[2 * which + h].at[rows, lanes], sems.at[k]
                )
                copies.append((owner == which, copy))
                pl.when(owner == which)(copy.start)
    for here, copy in copies:
        pl.when(here)(copy.wait)


def home_chunks(plan, bits, own, core_got, y_got, kind):
    count, sub, cols = plan
    part = count * cols * sub
    for d, (ref, base) in enumerate(
        ((own, 0), (core_got, 0), (y_got, 0), (y_got, 2 * part))
    ):
        to = pl.ds(pl.multiple_of(bits[BLOCK_AT + d] * sub, sub), sub)
        for m in range(count):
            for lc in range(cols):
                at = base + kind * part + (m * cols + lc) * sub
                yield ref[at : at + sub, :], m, to, slice(lc * LANES, (lc + 1) * LANES)


def dconv_kernel(plan, bits, own, core_got, y_got, conv_in, dconv, x_edge, z_edge):
    for dacted, m, to, lanes in home_chunks(plan, bits, own, core_got, y_got, 1):
        conv = conv_in[m, to, lanes]
        sig = sigmoid(conv)
        dconv[m, to, lanes] = dacted.astype(F32) * sig * (1.0 + conv * (1.0 - sig))
    count, length, width = dconv.shape
    odd, last = bits[X], length - HALO
    for m in range(count):
        for lc, lanes in enumerate(lanes_of(width)):
            at = (m * plan[2] + lc) * HALO
            x_rows = pl.ds(pl.multiple_of((1 - odd) * last, HALO), HALO)
            z_rows = pl.ds(pl.multiple_of(odd * last, HALO), HALO)
            x_edge[at : at + HALO, :] = dconv[m, x_rows, lanes].astype(BF)
            z_edge[at : at + HALO, :] = dconv[m, z_rows, lanes].astype(BF)


def layer_kernel(plan, bits, own, core_got, y_got, frames, weights, layer_out, mix_s):
    for mixed, m, to, lanes in home_chunks(plan, bits, own, core_got, y_got, 0):
        mix_s[m, to, lanes] = mixed
    for m in range(plan[0]):
        proj = mm(mix_s[m], weights[3])
        layer_out[m] = (frames[m].astype(F32) + proj).astype(BF)


def tap_kernel(sub, bits, frames, x_got, z_got, dconv, taps, pad_s):
    count, length, width = dconv.shape
    for m in range(count):
        for lanes in lanes_of(width):
            pad_s[m, :, lanes] = padded_frames(bits, frames, x_got, z_got, m, lanes)
    for lc, lanes in enumerate(lanes_of(width)):

        def step(n, accs):
            m = n // (length // sub)
            at = pl.multiple_of(n % (length // sub) * sub, sub)
            x = pad_s[m, pl.ds(at, sub + 2 * HALO), lanes]
            d = dconv[m, pl.ds(at, sub), lanes]
            out = list(accs)
            for r in range(8):
                xr = rolled(x, r)
                for k in range(4):
                    o = 8 * k + r
                    if o == 0:
                        continue
                    prod = xr[8 * k : 8 * k + sub] * d
                    out[o - 1] = out[o - 1] + jnp.sum(prod.reshape(sub // 8, 8, LANES), axis=0)
            return tuple(out)

        zeros = tuple(jnp.zeros((8, LANES), F32) for _ in range(31))
        accs = lax.fori_loop(0, count * (length // sub), step, zeros)
        taps[lc * 32 : lc * 32 + 32, :] = jnp.concatenate(
            [jnp.sum(x, axis=0, keepdims=True) for x in accs] + [jnp.zeros((1, LANES), F32)], axis=0
        ).astype(BF)


def frame_kernel(bits, dconv, x_got, z_got, both, kern, frame_grad):
    count, length, width = dconv.shape
    half = length // 2

    def step(m, _):
        for lc, lanes in enumerate(lanes_of(width)):
            n = m * (width // LANES) + lc
            rows = pl.ds(pl.multiple_of(n * HALO, HALO), HALO)
            x = padded(bits, dconv[m, :, lanes], x_got[rows, :], z_got[rows, :])
            for at in (0, half):
                part = slice(at, at + half)
                grad = window(
                    x[at : at + half + 2 * HALO], lambda o: kern[31 - o : 32 - o, lanes], half
                )
                frame_grad[m, part, lanes] = (
                    both[count + m, part, lanes].astype(F32) + grad
                ).astype(BF)
        return 0

    lax.fori_loop(0, count, step, 0)


def call(body, outs, scratch, limit, *args, hbm=(), hbm_outs=(), aliases=None):
    spaces = [pltpu.HBM if i in hbm else pltpu.VMEM for i in range(len(args))]
    return pl.pallas_call(
        body,
        out_shape=outs,
        in_specs=[
            pl.BlockSpec(memory_space=pltpu.SMEM if x.dtype == jnp.int32 else space)
            for x, space in zip(args, spaces)
        ],
        out_specs=tuple(
            pl.BlockSpec(memory_space=pltpu.HBM if i in hbm_outs else pltpu.VMEM)
            for i in range(len(outs))
        ),
        scratch_shapes=scratch,
        input_output_aliases=aliases or {},
        compiler_params=pltpu.CompilerParams(vmem_limit_bytes=limit * MIB),
    )(*args)


def shards(frames, cotangent, kernel, w_query, w_key, w_value, w_out):
    groups, blocks = lax.axis_size("mic"), lax.axis_size("tm")
    count, length, width = frames.shape
    sub = length // groups
    cuts = sub // HALO
    cols = width // LANES
    rows = groups * count * sub
    shape = jax.ShapeDtypeStruct

    mic, tm = lax.axis_index("mic"), lax.axis_index("tm")
    over_core, over_y, over_x = blocks, 2 * blocks, 1
    lines = [2**i for i in range(1, blocks.bit_length() - 1)]
    odd = tm % 2
    bits = jnp.stack(
        [mic % 2, mic // 2, odd, tm // 2 % 2, tm // 4 % 2] + [mic ^ d for d in range(4)]
    ).astype(jnp.int32)

    def permute(x, pairs):
        return lax.ppermute(x, ("mic", "tm"), pairs)

    def swap(x, mask):
        return permute(x, [(f, f ^ mask) for f in range(groups * blocks)])

    def swap_beyond(x):
        pairs = [(m * blocks + t, m * blocks + t + 1)
                 for m in range(groups) for t in range(1, blocks - 1, 2)]
        return permute(x, pairs + [(j, i) for i, j in pairs])

    def spread(parts):
        masks = (0, over_core, over_y, over_core + over_y)
        got = {d: swap(parts[d], masks[d]) for d in (2, 3, 1)}
        return [parts[0], got[1], got[2], got[3]]

    last = length - HALO
    frame_x = swap(lax.dynamic_slice_in_dim(frames, (1 - odd) * last, HALO, axis=1), over_x)
    frame_z = swap_beyond(lax.dynamic_slice_in_dim(frames, odd * last, HALO, axis=1))
    both = jnp.concatenate([frames, cotangent])
    taps_in = jnp.pad(kernel, ((0, 1), (0, 0)))
    cot_parts = spread(
        [
            lax.dynamic_slice(both, (count, (mic ^ d) * sub, 0), (count, sub, width))
            for d in range(4)
        ]
    )
    block = shape((count, sub, width), BF)
    wide = shape(frames.shape, F32)
    here = pltpu.VMEM(frames.shape, BF)
    conv, *acted = call(
        functools.partial(conv_kernel, sub), (wide,) + (block,) * 4, [here],
        8, bits, both, frame_x, frame_z, taps_in,
    )
    own_acted, *weights = lax.optimization_barrier(
        (acted[0], w_query, w_key, w_value, w_out)
    )
    weights = jnp.stack(weights)

    factor = 1.0 / math.sqrt(width // HEADS)
    part = width * width // LANES
    unit = 2 * count * cols * sub
    big = pltpu.VMEM((rows, width), BF)

    def flat(n):
        return shape((n, LANES), BF)

    a_keep, b_keep, a_send, b_send, back_keep, back_send = call(
        functools.partial(main_kernel, (groups, count, sub, width, factor)),
        (flat(part),) * 4 + (flat(2 * unit),) * 2,
        [
            pltpu.VMEM((2, rows, width), BF),
            pltpu.VMEM((4, cuts, groups, count, HALO, width), BF),
            big, big, big, big,
        ],
        24, bits, *spread([own_acted] + acted[1:]), *cot_parts, weights,
    )

    def halved(parts, mask):
        n = parts[0].shape[0] // 2
        return [t[:n] for t in parts] + [swap(total(*(t[n:] for t in parts)), mask)]

    def exchanged(x, masks):
        for mask in masks:
            x = total(x, swap(x, mask))
        return x

    def doubled(x, mask):
        return jnp.concatenate([x, swap(x, mask)])

    def after(x, y):
        return lax.optimization_barrier((x, y))[0]

    a = [a_keep, swap(a_send, over_core)]
    b = [b_keep, swap(b_send, over_core)]
    core_got = swap(back_send, over_core)
    y_got = swap(jnp.concatenate([back_keep[unit:], core_got[unit:]]), over_y)
    a = halved(a, over_x)
    b = halved(b, lines[0])
    plan = (count, sub, cols)
    y_got = after(y_got, (a[-1], b[-1]))
    home = (bits, back_keep, core_got, y_got)
    edge = flat(count * cols * HALO)
    dconv, x_edge, z_edge = call(
        functools.partial(dconv_kernel, plan), (wide, edge, edge), [], 8, *home, conv
    )
    a = halved(a, over_y)
    b = halved(b, over_x)
    a = halved(a, lines[1])
    (taps,) = call(
        functools.partial(tap_kernel, sub), (flat(32 * cols),),
        [pltpu.VMEM((count, length + 2 * HALO, width), F32)],
        8, bits, both, frame_x, frame_z, after(dconv, a[-1]),
    )
    n = taps.shape[0]
    got = swap(jnp.concatenate([taps, x_edge]), over_x)
    taps, x_edge = total(taps, got[:n]), got[n:]

    def doubled_with(x, taps, mask):
        got = swap(jnp.concatenate([x, taps]), mask)
        return jnp.concatenate([x, got[: x.shape[0]]]), total(taps, got[x.shape[0] :])

    a = exchanged(total(*a), lines[:1] + lines[2:])
    b = exchanged(total(*halved(b, over_y)), lines[1:])
    z_edge = swap_beyond(after(z_edge, a))
    a, taps = doubled_with(a, taps, lines[1])
    for mask in lines[2:]:
        taps = total(taps, swap(taps, mask))
    b = doubled(b, over_y)
    (layer_out,) = call(
        functools.partial(layer_kernel, plan), (shape(frames.shape, BF),), [here],
        10, *home, after(both, a), weights,
    )
    a, taps = doubled_with(a, taps, over_y)
    b = doubled(b, over_x)

    norm = 1.0 / math.sqrt(groups * count * blocks * length)
    square = shape((width, width), F32)

    def final(kinds, parts, grads, taps=()):
        first = 1 + len(parts) + len(taps)
        return call(
            functools.partial(final_kernel, (kinds, not grads, bool(taps), width, norm)),
            (square,) * 4 + (shape((31, width), F32),) * len(taps),
            [
                pltpu.VMEM((4 * len(kinds), part // 8, LANES), F32),
                pltpu.SemaphoreType.DMA((4 * len(kinds),)),
            ],
            10, bits, *parts, *taps, *grads, hbm=range(first, first + len(grads)),
            hbm_outs=range(4), aliases={first + i: i for i in range(len(grads))},
        )

    a_far, b_far = swap(a, over_x), swap(jnp.concatenate([b, taps]), lines[0])
    (frame_grad,) = call(
        frame_kernel, (shape(frames.shape, BF),), [], 8,
        bits, after(dconv, (a, b)), x_edge, z_edge, both, taps_in,
    )
    a_other, b_other = after((a, b), frame_grad)
    a_other, b_other = swap(a_other, over_core), swap(b_other, over_core)
    grads = final(((1, 0, 0), (1, 1, 0), (0, 0, 0), (0, 1, 0)), (a, b, a_other, b_other), ())
    a_far, b_far, frame_grad, layer_out, *grads = lax.optimization_barrier(
        (a_far, b_far, frame_grad, layer_out, *grads)
    )
    k = b.shape[0]
    taps = total(taps, b_far[k:])
    a_other = swap(a_far, over_core)
    b_other = swap(jnp.concatenate([b_far[:k], taps]), over_core)
    taps = total(taps, b_other[k:])
    grads = final(((1, 0, 1), (1, 1, 1)), (a_far, b_far), grads)
    *grads, kernel_grad = final(((0, 0, 1), (0, 1, 1)), (a_other, b_other), grads, (taps,))
    return (layer_out, frame_grad, kernel_grad, *grads)


def solution(mesh):
    in_specs = (P("mic", "tm", None), P("mic", "tm", None), P(), P(), P(), P(), P())
    out_specs = (P("mic", "tm", None), P("mic", "tm", None), P(), P(), P(), P(), P())
    return jax.shard_map(shards, mesh=mesh, in_specs=in_specs, out_specs=out_specs, check_vma=False)
```

```python
import functools
import math

import jax
import jax.numpy as jnp
from jax import lax
from jax.experimental import pallas as pl
from jax.experimental.pallas import tpu as pltpu
from jax.sharding import PartitionSpec as P

HEADS = 8
LANES = 128
HALO = 16
NT = (((1,), (1,)), ((), ()))
TN = (((0,), (0,)), ((), ()))
BF = jnp.bfloat16
F32 = jnp.float32
MIB = 1024 * 1024
CORE, Y, X, Z, ZZ, BLOCK_AT = range(6)


def mm(left, right, dims=(((1,), (0,)), ((), ()))):
    return lax.dot_general(left, right, dims, preferred_element_type=F32)


def rolled(x, shift):
    return x if shift == 0 else pltpu.roll(x, x.shape[0] - shift, axis=0)


def window(x, taps, rows):
    acc = None
    for r in range(8):
        xr = rolled(x, r)
        for k in range(4):
            o = 8 * k + r
            if o == 0:
                continue
            term = xr[8 * k : 8 * k + rows] * taps(o)
            acc = term if acc is None else acc + term
    return acc


def ways(bits, half):
    return [bits[i] for i in ((X, Y, ZZ), (Z, X, Y))[half]]


def sigmoid(v):
    return 0.5 * jnp.tanh(0.5 * v) + 0.5


def padded(bits, rows, one, two):
    is_odd = jnp.broadcast_to(bits[X], (HALO, LANES)) == 1
    one, two = one.astype(F32), two.astype(F32)
    return jnp.concatenate(
        [jnp.where(is_odd, one, two), rows.astype(F32), jnp.where(is_odd, two, one)], axis=0
    )


def padded_frames(bits, frames, x_got, z_got, m, lanes):
    return padded(bits, frames[m, :, lanes], x_got[m, :, lanes], z_got[m, :, lanes])


def lanes_of(width):
    return [slice(at, at + LANES) for at in range(0, width, LANES)]


def conv_kernel(sub, bits, frames, x_got, z_got, kern, conv_out, *refs):
    outs, act_s = refs[:4], refs[4]
    count, length, width = conv_out.shape
    half = length // 2

    def step(m, _):
        for lanes in lanes_of(width):
            x = padded_frames(bits, frames, x_got, z_got, m, lanes)
            for at in (0, half):
                conv = window(
                    x[at : at + half + 2 * HALO], lambda o: kern[o - 1 : o, lanes], half
                )
                conv_out[m, at : at + half, lanes] = conv
                act_s[m, at : at + half, lanes] = (conv * sigmoid(conv)).astype(BF)
        return 0

    lax.fori_loop(0, count, step, 0)
    for d, out in enumerate(outs):
        out[...] = act_s[:, pl.ds(pl.multiple_of(bits[BLOCK_AT + d] * sub, sub), sub), :]


def main_kernel(
    plan, bits, a0, a1, a2, a3, c0, c1, c2, c3, weights,
    a_keep, b_keep, a_send, b_send, back_keep, back_send,
    left_s, right_s, q_s, k_s, v_s, u_s,
):
    groups, count, sub, width, factor = plan
    mics = groups * count
    cuts = sub // HALO
    block = mics * HALO
    rows = cuts * block
    cols = width // LANES

    wq, wk, wv, wo = (weights.at[i] for i in range(4))
    for d, (act, cot) in enumerate(((a0, c0), (a1, c1), (a2, c2), (a3, c3))):
        for m in range(count):
            for c in range(cuts):
                part = slice(c * HALO, (c + 1) * HALO)
                at = c * block + (d * count + m) * HALO
                left_s[0, at : at + HALO, :] = act[m, part, :]
                right_s[3, c, d, m] = cot[m, part, :]

    def flat(i):
        return right_s[i].reshape(rows, width)

    def put(i, c, lanes, x):
        right_s[i, c, :, :, :, lanes] = x.astype(BF).reshape(groups, count, HALO, LANES)

    acted = left_s[0]
    q_s[...] = mm(acted, wq[...]).astype(BF)
    k_s[...] = mm(acted, wk[...]).astype(BF)
    v_s[...] = mm(acted, wv[...]).astype(BF)
    u_s[...] = mm(flat(3), wo[...], NT).astype(BF)

    depth = width // HEADS
    per = LANES // depth
    lane = lax.broadcasted_iota(jnp.int32, (block, LANES), 1)
    row_i = lax.broadcasted_iota(jnp.int32, (block, per * block), 0)
    col_i = lax.broadcasted_iota(jnp.int32, (block, per * block), 1)
    same = (row_i % HALO) == (col_i % HALO)

    def by_head(x):
        return jnp.concatenate(
            [jnp.where(lane // depth == h, x, jnp.zeros_like(x)) for h in range(per)], axis=0
        )

    def sums(x):
        return [
            jnp.sum(x[:, h * block : (h + 1) * block], axis=1, keepdims=True) for h in range(per)
        ]

    def each(x, values, op):
        return jnp.concatenate(
            [op(x[:, h * block : (h + 1) * block], values[h]) for h in range(per)], axis=1
        )

    def pick(x):
        out = x[:block]
        for h in range(1, per):
            out = jnp.where(lane // depth == h, x[h * block : (h + 1) * block], out)
        return out

    for c in range(cuts):
        part = slice(c * block, (c + 1) * block)
        for p in range(cols):
            lanes = slice(p * LANES, (p + 1) * LANES)
            q, u = q_s[part, lanes], u_s[part, lanes]
            kc, vc = by_head(k_s[part, lanes]), by_head(v_s[part, lanes])
            e = jnp.where(same, jnp.exp(mm(q, kc, NT) * factor), 0.0)
            w = each(e, [1.0 / x for x in sums(e)], lambda x, s: x * s)
            up = mm(u, vc, NT)
            inner = each(up, sums(w * up), lambda x, s: x - s) * w * factor
            wb, ib = w.astype(BF), inner.astype(BF)
            left_s[1, part, lanes] = mm(wb, vc).astype(BF)
            put(0, c, lanes, mm(ib, kc))
            put(1, c, lanes, pick(mm(ib, q, TN)))
            put(2, c, lanes, pick(mm(wb, u, TN)))

    dacted = mm(flat(0), wq[...], NT) + mm(flat(1), wk[...], NT) + mm(flat(2), wv[...], NT)
    size = cols * width // 8
    core = bits[CORE]
    for out, owner, h in (
        (a_send, 1 - core, 0), (b_send, 1 - core, 1), (a_keep, core, 0), (b_keep, core, 1)
    ):
        i = owner * 2 + h
        first, second, third = ways(bits, h)
        grad = mm(left_s[i // 3], flat(i), TN).astype(BF)
        for piece in range(8):
            rel = ((piece // 4) ^ first) * 4 + ((piece // 2 % 2) ^ second) * 2 + ((piece % 2) ^ third)
            cb, at = piece * size // width, piece * size % width
            out[pl.ds(pl.multiple_of(rel * size, size), size), :] = grad[
                at : at + size, cb * LANES : (cb + 1) * LANES
            ]

    unit = 2 * count * cols * sub
    for d, (out, base) in enumerate(
        ((back_keep, 0), (back_send, 0), (back_keep, unit), (back_send, unit))
    ):
        for m in range(count):
            for c in range(cuts):
                at = c * block + (d * count + m) * HALO
                for kind in range(2):
                    rows_of = left_s[1, at : at + HALO, :] if kind == 0 else dacted[
                        at : at + HALO
                    ].astype(BF)
                    for lc in range(cols):
                        to = base + ((kind * count + m) * cols + lc) * sub + c * HALO
                        out[to : to + HALO, :] = rows_of[:, lc * LANES : (lc + 1) * LANES]


def total(*parts):
    return functools.reduce(lambda x, y: x + y, [x.astype(F32) for x in parts]).astype(BF)


def final_kernel(plan, bits, *refs):
    kinds, first_call, with_taps, width, norm = plan
    cols = width // LANES
    size = cols * width // 8
    got, refs = refs[: len(kinds)], refs[len(kinds) :]
    if with_taps:
        taps, refs, tap_grad = refs[0], refs[1:-3] + refs[-2:], refs[-3]
        for lc, lanes in enumerate(lanes_of(width)):
            tap_grad[:, lanes] = taps[lc * 32 : lc * 32 + 31, :].astype(F32) * norm
    *outs, piece_s, sems = refs if first_call else refs[4:]
    core = bits[CORE]
    copies = []
    for n, (own, h, far) in enumerate(kinds):
        owner = core if own else 1 - core
        first, second, third = ways(bits, h)
        for rel in range(4):
            k = 4 * n + rel
            piece_s[k] = got[n][rel * size : (rel + 1) * size, :].astype(F32) * norm
            piece = (first ^ far) * 4 + (second ^ (rel // 2)) * 2 + (third ^ (rel % 2))
            cb, at = piece * size // width, piece * size % width
            rows = pl.ds(pl.multiple_of(at, size), size)
            lanes = pl.ds(pl.multiple_of(cb * LANES, LANES), LANES)
            for which in range(2):
                copy = pltpu.make_async_copy(
                    piece_s.at[k], outs[2 * which + h].at[rows, lanes], sems.at[k]
                )
                copies.append((owner == which, copy))
                pl.when(owner == which)(copy.start)
    for here, copy in copies:
        pl.when(here)(copy.wait)


def home_chunks(plan, bits, own, core_got, y_got, kind):
    count, sub, cols = plan
    part = count * cols * sub
    for d, (ref, base) in enumerate(
        ((own, 0), (core_got, 0), (y_got, 0), (y_got, 2 * part))
    ):
        to = pl.ds(pl.multiple_of(bits[BLOCK_AT + d] * sub, sub), sub)
        for m in range(count):
            for lc in range(cols):
                at = base + kind * part + (m * cols + lc) * sub
                yield ref[at : at + sub, :], m, to, slice(lc * LANES, (lc + 1) * LANES)


def dconv_kernel(plan, bits, own, core_got, y_got, conv_in, dconv, first_edge, last_edge):
    for dacted, m, to, lanes in home_chunks(plan, bits, own, core_got, y_got, 1):
        conv = conv_in[m, to, lanes]
        sig = sigmoid(conv)
        dconv[m, to, lanes] = dacted.astype(F32) * sig * (1.0 + conv * (1.0 - sig))
    count, length, width = dconv.shape
    last = length - HALO
    for m in range(count):
        for lc, lanes in enumerate(lanes_of(width)):
            at = (m * plan[2] + lc) * HALO
            first_edge[at : at + HALO, :] = dconv[m, :HALO, lanes].astype(BF)
            last_edge[at : at + HALO, :] = dconv[m, last:, lanes].astype(BF)


def layer_kernel(plan, bits, own, core_got, y_got, frames, weights, layer_out, mix_s):
    for mixed, m, to, lanes in home_chunks(plan, bits, own, core_got, y_got, 0):
        mix_s[m, to, lanes] = mixed
    for m in range(plan[0]):
        proj = mm(mix_s[m], weights[3])
        layer_out[m] = (frames[m].astype(F32) + proj).astype(BF)


def tap_kernel(sub, bits, frames, x_got, z_got, dconv, taps, pad_s):
    count, length, width = dconv.shape
    for m in range(count):
        for lanes in lanes_of(width):
            pad_s[m, :, lanes] = padded_frames(bits, frames, x_got, z_got, m, lanes)
    for lc, lanes in enumerate(lanes_of(width)):

        def step(n, accs):
            m = n // (length // sub)
            at = pl.multiple_of(n % (length // sub) * sub, sub)
            x = pad_s[m, pl.ds(at, sub + 2 * HALO), lanes]
            d = dconv[m, pl.ds(at, sub), lanes]
            out = list(accs)
            for r in range(8):
                xr = rolled(x, r)
                for k in range(4):
                    o = 8 * k + r
                    if o == 0:
                        continue
                    prod = xr[8 * k : 8 * k + sub] * d
                    out[o - 1] = out[o - 1] + jnp.sum(prod.reshape(sub // 8, 8, LANES), axis=0)
            return tuple(out)

        zeros = tuple(jnp.zeros((8, LANES), F32) for _ in range(31))
        accs = lax.fori_loop(0, count * (length // sub), step, zeros)
        taps[lc * 32 : lc * 32 + 32, :] = jnp.concatenate(
            [jnp.sum(x, axis=0, keepdims=True) for x in accs] + [jnp.zeros((1, LANES), F32)], axis=0
        ).astype(BF)


def frame_kernel(bits, dconv, x_got, z_got, other_got, both, kern, frame_grad):
    count, length, width = dconv.shape
    half = length // 2
    n_edge = z_got.shape[0]
    by_z = jnp.broadcast_to(bits[X] ^ bits[Z], (HALO, LANES)) == 1

    def step(m, _):
        for lc, lanes in enumerate(lanes_of(width)):
            at = (m * (width // LANES) + lc) * HALO
            rows = pl.ds(pl.multiple_of(at, HALO), HALO)
            x_rows = pl.ds(pl.multiple_of(bits[X] * n_edge + at, HALO), HALO)
            two = jnp.where(by_z, z_got[rows, :].astype(F32), other_got[rows, :].astype(F32))
            x = padded(bits, dconv[m, :, lanes], x_got[x_rows, :], two)
            for at in (0, half):
                part = slice(at, at + half)
                grad = window(
                    x[at : at + half + 2 * HALO], lambda o: kern[31 - o : 32 - o, lanes], half
                )
                frame_grad[m, part, lanes] = (
                    both[count + m, part, lanes].astype(F32) + grad
                ).astype(BF)
        return 0

    lax.fori_loop(0, count, step, 0)


def call(body, outs, scratch, limit, *args, hbm=(), hbm_outs=(), aliases=None):
    spaces = [pltpu.HBM if i in hbm else pltpu.VMEM for i in range(len(args))]
    return pl.pallas_call(
        body,
        out_shape=outs,
        in_specs=[
            pl.BlockSpec(memory_space=pltpu.SMEM if x.dtype == jnp.int32 else space)
            for x, space in zip(args, spaces)
        ],
        out_specs=tuple(
            pl.BlockSpec(memory_space=pltpu.HBM if i in hbm_outs else pltpu.VMEM)
            for i in range(len(outs))
        ),
        scratch_shapes=scratch,
        input_output_aliases=aliases or {},
        compiler_params=pltpu.CompilerParams(vmem_limit_bytes=limit * MIB),
    )(*args)


def shards(frames, cotangent, kernel, w_query, w_key, w_value, w_out):
    groups, blocks = lax.axis_size("mic"), lax.axis_size("tm")
    count, length, width = frames.shape
    sub = length // groups
    cuts = sub // HALO
    cols = width // LANES
    rows = groups * count * sub
    shape = jax.ShapeDtypeStruct

    mic, tm = lax.axis_index("mic"), lax.axis_index("tm")
    over_core, over_y, over_x = blocks, 2 * blocks, 1
    lines = [2**i for i in range(1, blocks.bit_length() - 1)]
    odd = tm % 2
    bits = jnp.stack(
        [mic % 2, mic // 2, odd, tm // 2 % 2, tm // 4 % 2] + [mic ^ d for d in range(4)]
    ).astype(jnp.int32)

    def permute(x, pairs):
        return lax.ppermute(x, ("mic", "tm"), pairs)

    def swap(x, mask):
        return permute(x, [(f, f ^ mask) for f in range(groups * blocks)])

    def swap_beyond(x):
        pairs = [(m * blocks + t, m * blocks + t + 1)
                 for m in range(groups) for t in range(1, blocks - 1, 2)]
        return permute(x, pairs + [(j, i) for i, j in pairs])

    def spread(parts):
        masks = (0, over_core, over_y, over_core + over_y)
        got = {d: swap(parts[d], masks[d]) for d in (2, 3, 1)}
        return [parts[0], got[1], got[2], got[3]]

    last = length - HALO
    frame_x = swap(lax.dynamic_slice_in_dim(frames, (1 - odd) * last, HALO, axis=1), over_x)
    frame_z = swap_beyond(lax.dynamic_slice_in_dim(frames, odd * last, HALO, axis=1))
    both = jnp.concatenate([frames, cotangent])
    taps_in = jnp.pad(kernel, ((0, 1), (0, 0)))
    cot_parts = spread(
        [
            lax.dynamic_slice(both, (count, (mic ^ d) * sub, 0), (count, sub, width))
            for d in range(4)
        ]
    )
    block = shape((count, sub, width), BF)
    wide = shape(frames.shape, F32)
    here = pltpu.VMEM(frames.shape, BF)
    conv, *acted = call(
        functools.partial(conv_kernel, sub), (wide,) + (block,) * 4, [here],
        8, bits, both, frame_x, frame_z, taps_in,
    )
    own_acted, *weights = lax.optimization_barrier(
        (acted[0], w_query, w_key, w_value, w_out)
    )
    weights = jnp.stack(weights)

    factor = 1.0 / math.sqrt(width // HEADS)
    part = width * width // LANES
    unit = 2 * count * cols * sub
    big = pltpu.VMEM((rows, width), BF)

    def flat(n):
        return shape((n, LANES), BF)

    a_keep, b_keep, a_send, b_send, back_keep, back_send = call(
        functools.partial(main_kernel, (groups, count, sub, width, factor)),
        (flat(part),) * 4 + (flat(2 * unit),) * 2,
        [
            pltpu.VMEM((2, rows, width), BF),
            pltpu.VMEM((4, cuts, groups, count, HALO, width), BF),
            big, big, big, big,
        ],
        24, bits, *spread([own_acted] + acted[1:]), *cot_parts, weights,
    )

    def halved(parts, mask):
        n = parts[0].shape[0] // 2
        return [t[:n] for t in parts] + [swap(total(*(t[n:] for t in parts)), mask)]

    def exchanged(x, masks):
        for mask in masks:
            x = total(x, swap(x, mask))
        return x

    def doubled(x, mask):
        return jnp.concatenate([x, swap(x, mask)])

    def after(x, y):
        return lax.optimization_barrier((x, y))[0]

    a = [a_keep, swap(a_send, over_core)]
    b = [b_keep, swap(b_send, over_core)]
    core_got = swap(back_send, over_core)
    y_got = swap(jnp.concatenate([back_keep[unit:], core_got[unit:]]), over_y)
    a = halved(a, over_x)
    b = halved(b, lines[0])
    plan = (count, sub, cols)
    y_got = after(y_got, (a[-1], b[-1]))
    home = (bits, back_keep, core_got, y_got)
    edge = flat(count * cols * HALO)
    dconv, *edges = call(
        functools.partial(dconv_kernel, plan), (wide, edge, edge), [], 8, *home, conv
    )
    a = halved(a, over_y)
    b = halved(b, over_x)
    a = halved(a, lines[1])
    (taps,) = call(
        functools.partial(tap_kernel, sub), (flat(32 * cols),),
        [pltpu.VMEM((count, length + 2 * HALO, width), F32)],
        8, bits, both, frame_x, frame_z, after(dconv, a[-1]),
    )
    n = taps.shape[0]
    got = swap(jnp.concatenate([taps, *edges]), over_x)
    taps, x_got = total(taps, got[:n]), got[n:]
    passed = lax.dynamic_slice_in_dim(x_got, (1 - odd) * edge.shape[0], edge.shape[0], axis=0)
    a = exchanged(total(*a), lines[:1] + lines[2:])
    b = exchanged(total(*halved(b, over_y)), lines[1:])
    taps = exchanged(taps, lines[1:])
    passed = after(passed, a)
    pairs = [(m * blocks + t, m * blocks + t + 2)
             for m in range(groups) for t in range(2, blocks - 2) if t // 2 % 2]
    z_got = swap(passed, lines[0])
    other_got = permute(passed, pairs + [(j, i) for i, j in pairs])
    a = doubled(a, lines[1])
    b = doubled(b, over_y)
    (layer_out,) = call(
        functools.partial(layer_kernel, plan), (shape(frames.shape, BF),), [here],
        10, *home, after(both, a), weights,
    )
    got = swap(jnp.concatenate([a, taps]), over_y)
    n = a.shape[0]
    a, taps = jnp.concatenate([a, got[:n]]), total(taps, got[n:])
    b = doubled(b, over_x)

    norm = 1.0 / math.sqrt(groups * count * blocks * length)
    square = shape((width, width), F32)

    def final(kinds, parts, grads, taps=()):
        first = 1 + len(parts) + len(taps)
        return call(
            functools.partial(final_kernel, (kinds, not grads, bool(taps), width, norm)),
            (square,) * 4 + (shape((31, width), F32),) * len(taps),
            [
                pltpu.VMEM((4 * len(kinds), part // 8, LANES), F32),
                pltpu.SemaphoreType.DMA((4 * len(kinds),)),
            ],
            10, bits, *parts, *taps, *grads, hbm=range(first, first + len(grads)),
            hbm_outs=range(4), aliases={first + i: i for i in range(len(grads))},
        )

    a_far, b_far = swap(a, over_x), swap(jnp.concatenate([b, taps]), lines[0])
    a_other, b_other = swap(a, over_core), swap(b, over_core)
    (frame_grad,) = call(
        frame_kernel, (shape(frames.shape, BF),), [], 8,
        bits, after(dconv, (a_other, b_other)), x_got, z_got, other_got, both, taps_in,
    )
    grads = final(((1, 0, 0), (1, 1, 0), (0, 0, 0), (0, 1, 0)), (a, b, a_other, b_other), ())
    a_far, b_far, frame_grad, layer_out, *grads = lax.optimization_barrier(
        (a_far, b_far, frame_grad, layer_out, *grads)
    )
    k = b.shape[0]
    taps = total(taps, b_far[k:])
    a_other = swap(a_far, over_core)
    b_other = swap(jnp.concatenate([b_far[:k], taps]), over_core)
    taps = total(taps, b_other[k:])
    grads = final(((1, 0, 1), (1, 1, 1)), (a_far, b_far), grads)
    *grads, kernel_grad = final(((0, 0, 1), (0, 1, 1)), (a_other, b_other), grads, (taps,))
    return (layer_out, frame_grad, kernel_grad, *grads)


def solution(mesh):
    in_specs = (P("mic", "tm", None), P("mic", "tm", None), P(), P(), P(), P(), P())
    out_specs = (P("mic", "tm", None), P("mic", "tm", None), P(), P(), P(), P(), P())
    return jax.shard_map(shards, mesh=mesh, in_specs=in_specs, out_specs=out_specs, check_vma=False)
```

```python
import functools
import math

import jax
import jax.numpy as jnp
from jax import lax
from jax.experimental import pallas as pl
from jax.experimental.pallas import tpu as pltpu
from jax.sharding import PartitionSpec as P

HEADS = 8
LANES = 128
HALO = 16
NT = (((1,), (1,)), ((), ()))
TN = (((0,), (0,)), ((), ()))
BF = jnp.bfloat16
F32 = jnp.float32
MIB = 1024 * 1024
CORE, X, OWN, OTHER, BLOCK_AT = 0, 1, 2, 5, 8


def mm(left, right, dims=(((1,), (0,)), ((), ()))):
    return lax.dot_general(left, right, dims, preferred_element_type=F32)


def rolled(x, shift):
    return x if shift == 0 else pltpu.roll(x, x.shape[0] - shift, axis=0)


def window(x, taps, rows):
    acc = None
    for r in range(8):
        xr = rolled(x, r)
        for k in range(4):
            o = 8 * k + r
            if o == 0:
                continue
            term = xr[8 * k : 8 * k + rows] * taps(o)
            acc = term if acc is None else acc + term
    return acc


def ways(bits, own):
    return [bits[(OWN if own else OTHER) + i] for i in range(3)]


def sigmoid(v):
    return 0.5 * jnp.tanh(0.5 * v) + 0.5


def padded(bits, rows, one, two):
    is_odd = jnp.broadcast_to(bits[X], (HALO, LANES)) == 1
    one, two = one.astype(F32), two.astype(F32)
    return jnp.concatenate(
        [jnp.where(is_odd, one, two), rows.astype(F32), jnp.where(is_odd, two, one)], axis=0
    )


def padded_frames(bits, frames, x_got, z_got, m, lanes):
    return padded(bits, frames[m, :, lanes], x_got[m, :, lanes], z_got[m, :, lanes])


def lanes_of(width):
    return [slice(at, at + LANES) for at in range(0, width, LANES)]


def conv_kernel(sub, bits, frames, x_got, z_got, kern, conv_out, *refs):
    outs, act_s = refs[:4], refs[4]
    count, length, width = conv_out.shape
    half = length // 2

    def step(m, _):
        for lanes in lanes_of(width):
            x = padded_frames(bits, frames, x_got, z_got, m, lanes)
            for at in (0, half):
                conv = window(
                    x[at : at + half + 2 * HALO], lambda o: kern[o - 1 : o, lanes], half
                )
                conv_out[m, at : at + half, lanes] = conv
                act_s[m, at : at + half, lanes] = (conv * sigmoid(conv)).astype(BF)
        return 0

    lax.fori_loop(0, count, step, 0)
    for d, out in enumerate(outs):
        out[...] = act_s[:, pl.ds(pl.multiple_of(bits[BLOCK_AT + d] * sub, sub), sub), :]


def main_kernel(
    plan, bits, c0, c1, c2, c3, a0, a1, a2, a3, weights,
    a_keep, b_keep, a_send, b_send, back_keep, back_send,
    left_s, right_s, q_s, k_s, v_s, u_s,
):
    groups, count, sub, width, factor = plan
    mics = groups * count
    cuts = sub // HALO
    block = mics * HALO
    rows = cuts * block
    cols = width // LANES

    wq, wk, wv, wo = (weights.at[i] for i in range(4))
    for d, (act, cot) in enumerate(((a0, c0), (a1, c1), (a2, c2), (a3, c3))):
        for m in range(count):
            for c in range(cuts):
                part = slice(c * HALO, (c + 1) * HALO)
                at = c * block + (d * count + m) * HALO
                left_s[0, at : at + HALO, :] = act[m, part, :]
                right_s[3, c, d, m] = cot[m, part, :]

    def flat(i):
        return right_s[i].reshape(rows, width)

    def put(i, c, lanes, x):
        right_s[i, c, :, :, :, lanes] = x.astype(BF).reshape(groups, count, HALO, LANES)

    acted = left_s[0]
    q_s[...] = mm(acted, wq[...]).astype(BF)
    k_s[...] = mm(acted, wk[...]).astype(BF)
    v_s[...] = mm(acted, wv[...]).astype(BF)
    u_s[...] = mm(flat(3), wo[...], NT).astype(BF)

    depth = width // HEADS
    per = LANES // depth
    lane = lax.broadcasted_iota(jnp.int32, (block, LANES), 1)
    row_i = lax.broadcasted_iota(jnp.int32, (block, per * block), 0)
    col_i = lax.broadcasted_iota(jnp.int32, (block, per * block), 1)
    same = (row_i % HALO) == (col_i % HALO)

    def by_head(x):
        return jnp.concatenate(
            [jnp.where(lane // depth == h, x, jnp.zeros_like(x)) for h in range(per)], axis=0
        )

    def sums(x):
        return [
            jnp.sum(x[:, h * block : (h + 1) * block], axis=1, keepdims=True) for h in range(per)
        ]

    def each(x, values, op):
        return jnp.concatenate(
            [op(x[:, h * block : (h + 1) * block], values[h]) for h in range(per)], axis=1
        )

    def pick(x):
        out = x[:block]
        for h in range(1, per):
            out = jnp.where(lane // depth == h, x[h * block : (h + 1) * block], out)
        return out

    for c in range(cuts):
        part = slice(c * block, (c + 1) * block)
        for p in range(cols):
            lanes = slice(p * LANES, (p + 1) * LANES)
            q, u = q_s[part, lanes], u_s[part, lanes]
            kc, vc = by_head(k_s[part, lanes]), by_head(v_s[part, lanes])
            e = jnp.where(same, jnp.exp(mm(q, kc, NT) * factor), 0.0)
            w = each(e, [1.0 / x for x in sums(e)], lambda x, s: x * s)
            up = mm(u, vc, NT)
            inner = each(up, sums(w * up), lambda x, s: x - s) * w * factor
            wb, ib = w.astype(BF), inner.astype(BF)
            left_s[1, part, lanes] = mm(wb, vc).astype(BF)
            put(0, c, lanes, mm(ib, kc))
            put(1, c, lanes, pick(mm(ib, q, TN)))
            put(2, c, lanes, pick(mm(wb, u, TN)))

    dacted = mm(flat(0), wq[...], NT) + mm(flat(1), wk[...], NT) + mm(flat(2), wv[...], NT)
    size = cols * width // 8
    core = bits[CORE]
    for out, owner, h in (
        (a_send, 1 - core, 0), (b_send, 1 - core, 1), (a_keep, core, 0), (b_keep, core, 1)
    ):
        i = owner * 2 + h
        first, second, third = ways(bits, out is a_keep or out is b_keep)
        grad = mm(left_s[i // 3], flat(i), TN).astype(BF)
        for piece in range(8):
            rel = ((piece // 4) ^ first) * 4 + ((piece // 2 % 2) ^ second) * 2 + ((piece % 2) ^ third)
            cb, at = piece * size // width, piece * size % width
            out[pl.ds(pl.multiple_of(rel * size, size), size), :] = grad[
                at : at + size, cb * LANES : (cb + 1) * LANES
            ]

    unit = 2 * count * cols * sub
    for d, (out, base) in enumerate(
        ((back_keep, 0), (back_send, 0), (back_keep, unit), (back_send, unit))
    ):
        for m in range(count):
            for c in range(cuts):
                at = c * block + (d * count + m) * HALO
                for kind in range(2):
                    rows_of = left_s[1, at : at + HALO, :] if kind == 0 else dacted[
                        at : at + HALO
                    ].astype(BF)
                    for lc in range(cols):
                        to = base + ((kind * count + m) * cols + lc) * sub + c * HALO
                        out[to : to + HALO, :] = rows_of[:, lc * LANES : (lc + 1) * LANES]


def total(*parts):
    return functools.reduce(lambda x, y: x + y, [x.astype(F32) for x in parts]).astype(BF)


def final_kernel(plan, bits, *refs):
    kinds, first_call, with_taps, width, norm = plan
    cols = width // LANES
    size = cols * width // 8
    got, refs = refs[: len(kinds)], refs[len(kinds) :]
    if with_taps:
        taps, refs, tap_grad = refs[0], refs[1:-3] + refs[-2:], refs[-3]
        for lc, lanes in enumerate(lanes_of(width)):
            tap_grad[:, lanes] = taps[lc * 32 : lc * 32 + 31, :].astype(F32) * norm
    *outs, piece_s, sems = refs if first_call else refs[4:]
    core = bits[CORE]
    copies = []
    for n, (own, h, far) in enumerate(kinds):
        owner = core if own else 1 - core
        first, second, third = ways(bits, own)
        for rel in range(4):
            k = 4 * n + rel
            piece_s[k] = got[n][rel * size : (rel + 1) * size, :].astype(F32) * norm
            piece = (first ^ far) * 4 + (second ^ (rel // 2)) * 2 + (third ^ (rel % 2))
            cb, at = piece * size // width, piece * size % width
            rows = pl.ds(pl.multiple_of(at, size), size)
            lanes = pl.ds(pl.multiple_of(cb * LANES, LANES), LANES)
            for which in range(2):
                copy = pltpu.make_async_copy(
                    piece_s.at[k], outs[2 * which + h].at[rows, lanes], sems.at[k]
                )
                copies.append((owner == which, copy))
                pl.when(owner == which)(copy.start)
    for here, copy in copies:
        pl.when(here)(copy.wait)


def home_chunks(plan, bits, own, core_got, y_got, kind):
    count, sub, cols = plan
    part = count * cols * sub
    for d, (ref, base) in enumerate(
        ((own, 0), (core_got, 0), (y_got, 0), (y_got, 2 * part))
    ):
        to = pl.ds(pl.multiple_of(bits[BLOCK_AT + d] * sub, sub), sub)
        for m in range(count):
            for lc in range(cols):
                at = base + kind * part + (m * cols + lc) * sub
                yield ref[at : at + sub, :], m, to, slice(lc * LANES, (lc + 1) * LANES)


def dconv_kernel(plan, bits, own, core_got, y_got, conv_in, dconv, x_edge, z_edge):
    for dacted, m, to, lanes in home_chunks(plan, bits, own, core_got, y_got, 1):
        conv = conv_in[m, to, lanes]
        sig = sigmoid(conv)
        dconv[m, to, lanes] = dacted.astype(F32) * sig * (1.0 + conv * (1.0 - sig))
    count, length, width = dconv.shape
    odd, last = bits[X], length - HALO
    for m in range(count):
        for lc, lanes in enumerate(lanes_of(width)):
            at = (m * plan[2] + lc) * HALO
            x_rows = pl.ds(pl.multiple_of((1 - odd) * last, HALO), HALO)
            z_rows = pl.ds(pl.multiple_of(odd * last, HALO), HALO)
            x_edge[at : at + HALO, :] = dconv[m, x_rows, lanes].astype(BF)
            z_edge[at : at + HALO, :] = dconv[m, z_rows, lanes].astype(BF)


def layer_kernel(plan, bits, own, core_got, y_got, frames, weights, layer_out, mix_s):
    for mixed, m, to, lanes in home_chunks(plan, bits, own, core_got, y_got, 0):
        mix_s[m, to, lanes] = mixed
    for m in range(plan[0]):
        proj = mm(mix_s[m], weights[3])
        layer_out[m] = (frames[m].astype(F32) + proj).astype(BF)


def tap_kernel(sub, bits, frames, x_got, z_got, dconv, taps, pad_s):
    count, length, width = dconv.shape
    for m in range(count):
        for lanes in lanes_of(width):
            pad_s[m, :, lanes] = padded_frames(bits, frames, x_got, z_got, m, lanes)
    for lc, lanes in enumerate(lanes_of(width)):

        def step(n, accs):
            m = n // (length // sub)
            at = pl.multiple_of(n % (length // sub) * sub, sub)
            x = pad_s[m, pl.ds(at, sub + 2 * HALO), lanes]
            d = dconv[m, pl.ds(at, sub), lanes]
            out = list(accs)
            for r in range(8):
                xr = rolled(x, r)
                for k in range(4):
                    o = 8 * k + r
                    if o == 0:
                        continue
                    prod = xr[8 * k : 8 * k + sub] * d
                    out[o - 1] = out[o - 1] + jnp.sum(prod.reshape(sub // 8, 8, LANES), axis=0)
            return tuple(out)

        zeros = tuple(jnp.zeros((8, LANES), F32) for _ in range(31))
        accs = lax.fori_loop(0, count * (length // sub), step, zeros)
        taps[lc * 32 : lc * 32 + 32, :] = jnp.concatenate(
            [jnp.sum(x, axis=0, keepdims=True) for x in accs] + [jnp.zeros((1, LANES), F32)], axis=0
        ).astype(BF)


def frame_kernel(bits, dconv, x_got, z_got, cot, kern, frame_grad):
    count, length, width = dconv.shape
    half = length // 2

    def step(m, _):
        for lc, lanes in enumerate(lanes_of(width)):
            rows = pl.ds(pl.multiple_of((m * (width // LANES) + lc) * HALO, HALO), HALO)
            x = padded(bits, dconv[m, :, lanes], x_got[rows, :], z_got[rows, :])
            for at in (0, half):
                part = slice(at, at + half)
                grad = window(
                    x[at : at + half + 2 * HALO], lambda o: kern[31 - o : 32 - o, lanes], half
                )
                frame_grad[m, part, lanes] = (cot[m, part, lanes].astype(F32) + grad).astype(BF)
        return 0

    lax.fori_loop(0, count, step, 0)


def call(body, outs, scratch, limit, *args, hbm=(), hbm_outs=(), aliases=None):
    spaces = [pltpu.HBM if i in hbm else pltpu.VMEM for i in range(len(args))]
    return pl.pallas_call(
        body,
        out_shape=outs,
        in_specs=[
            pl.BlockSpec(memory_space=pltpu.SMEM if x.dtype == jnp.int32 else space)
            for x, space in zip(args, spaces)
        ],
        out_specs=tuple(
            pl.BlockSpec(memory_space=pltpu.HBM if i in hbm_outs else pltpu.VMEM)
            for i in range(len(outs))
        ),
        scratch_shapes=scratch,
        input_output_aliases=aliases or {},
        compiler_params=pltpu.CompilerParams(vmem_limit_bytes=limit * MIB),
    )(*args)


def shards(frames, cotangent, kernel, w_query, w_key, w_value, w_out):
    groups, blocks = lax.axis_size("mic"), lax.axis_size("tm")
    count, length, width = frames.shape
    sub = length // groups
    cuts = sub // HALO
    cols = width // LANES
    rows = groups * count * sub
    shape = jax.ShapeDtypeStruct

    mic, tm = lax.axis_index("mic"), lax.axis_index("tm")
    over_core, over_y, over_x = blocks, 2 * blocks, 1
    lines = [2**i for i in range(1, blocks.bit_length() - 1)]
    core, odd = mic % 2, tm % 2
    axes = [(over_x, lines[0]), (over_y, over_x), (lines[1], over_y)]
    whole_axes = [(lines[0], lines[1])] + [(m, m) for m in lines[2:]]
    flat_at = mic * blocks + tm

    def bit(mask):
        return (flat_at // mask) % 2

    own = [jnp.where(core == 0, bit(i), bit(j)) for i, j in axes]
    other = [jnp.where(core == 0, bit(j), bit(i)) for i, j in axes]
    bits = jnp.stack([core, odd] + own + other + [mic ^ d for d in range(4)]).astype(jnp.int32)

    def permute(x, pairs):
        return lax.ppermute(x, ("mic", "tm"), pairs)

    def swap(x, even, odd=None):
        masks = (even, even if odd is None else odd)
        return permute(x, [(f, f ^ masks[f // blocks % 2]) for f in range(groups * blocks)])

    def swap_beyond(x):
        pairs = [(m * blocks + t, m * blocks + t + 1)
                 for m in range(groups) for t in range(1, blocks - 1, 2)]
        return permute(x, pairs + [(j, i) for i, j in pairs])

    def spread(parts):
        masks = (0, over_core, over_y, over_core + over_y)
        got = {d: swap(parts[d], masks[d]) for d in (2, 3, 1)}
        return [parts[0], got[1], got[2], got[3]]

    last = length - HALO
    frame_x = swap(lax.dynamic_slice_in_dim(frames, (1 - odd) * last, HALO, axis=1), over_x)
    frame_z = swap_beyond(lax.dynamic_slice_in_dim(frames, odd * last, HALO, axis=1))
    block = shape((count, sub, width), BF)
    wide = shape(frames.shape, F32)
    here = pltpu.VMEM(frames.shape, BF)
    conv, *acted = call(
        functools.partial(conv_kernel, sub), (wide,) + (block,) * 4, [here],
        8, bits, frames, frame_x, frame_z, kernel,
    )
    own_acted, cot_late, *weights = lax.optimization_barrier(
        (acted[0], cotangent, w_query, w_key, w_value, w_out)
    )
    weights = jnp.stack(weights)
    cot_parts = spread(
        [lax.dynamic_slice_in_dim(cot_late, (mic ^ d) * sub, sub, axis=1) for d in range(4)]
    )

    factor = 1.0 / math.sqrt(width // HEADS)
    part = width * width // LANES
    unit = 2 * count * cols * sub
    big = pltpu.VMEM((rows, width), BF)

    def flat(n):
        return shape((n, LANES), BF)

    a_keep, b_keep, a_send, b_send, back_keep, back_send = call(
        functools.partial(main_kernel, (groups, count, sub, width, factor)),
        (flat(part),) * 4 + (flat(2 * unit),) * 2,
        [
            pltpu.VMEM((2, rows, width), BF),
            pltpu.VMEM((4, cuts, groups, count, HALO, width), BF),
            big, big, big, big,
        ],
        24, bits, *cot_parts, *spread([own_acted] + acted[1:]), weights,
    )

    def halved(parts, pair):
        n = parts[0].shape[0] // 2
        return [t[:n] for t in parts] + [swap(total(*(t[n:] for t in parts)), *pair)]

    def exchanged(x, pairs):
        for pair in pairs:
            x = total(x, swap(x, *pair))
        return x

    def doubled(x, pair):
        return jnp.concatenate([x, swap(x, *pair)])

    def doubled_with(x, taps, pair):
        got = swap(jnp.concatenate([x, taps]), *pair)
        return jnp.concatenate([x, got[: x.shape[0]]]), total(taps, got[x.shape[0] :])

    def after(x, y):
        return lax.optimization_barrier((x, y))[0]

    a = [a_keep, swap(a_send, over_core)]
    b = [b_keep, swap(b_send, over_core)]
    core_got = swap(back_send, over_core)
    y_got = swap(jnp.concatenate([back_keep[unit:], core_got[unit:]]), over_y)
    a = halved(a, axes[0])
    b = halved(b, axes[0])
    plan = (count, sub, cols)
    y_got = after(y_got, (a[-1], b[-1]))
    home = (bits, back_keep, core_got, y_got)
    edge = flat(count * cols * HALO)
    dconv, x_edge, z_edge = call(
        functools.partial(dconv_kernel, plan), (wide, edge, edge), [], 8, *home, conv
    )
    a = halved(a, axes[1])
    b = halved(b, axes[1])
    (taps,) = call(
        functools.partial(tap_kernel, sub), (flat(32 * cols),),
        [pltpu.VMEM((count, length + 2 * HALO, width), F32)],
        8, bits, frames, frame_x, frame_z, after(dconv, a[-1]),
    )
    taps = exchanged(taps, whole_axes)
    x_got = swap(x_edge, over_x)
    a = exchanged(total(*halved(a, axes[2])), whole_axes)
    b = exchanged(total(*halved(b, axes[2])), whole_axes)
    z_got = swap_beyond(after(z_edge, (x_got, a)))
    a = doubled(after(a, x_got), axes[2])
    b, taps = doubled_with(b, taps, axes[2])
    a = doubled(after(a, z_got), axes[1])
    b, taps = doubled_with(b, taps, axes[1])

    norm = 1.0 / math.sqrt(groups * count * blocks * length)
    square = shape((width, width), F32)

    def final(kinds, parts, grads, taps=()):
        first = 1 + len(parts) + len(taps)
        return call(
            functools.partial(final_kernel, (kinds, not grads, bool(taps), width, norm)),
            (square,) * 4 + (shape((31, width), F32),) * len(taps),
            [
                pltpu.VMEM((4 * len(kinds), part // 8, LANES), F32),
                pltpu.SemaphoreType.DMA((4 * len(kinds),)),
            ],
            10, bits, *parts, *taps, *grads, hbm=range(first, first + len(grads)),
            hbm_outs=range(4), aliases={first + i: i for i in range(len(grads))},
        )

    a_far, b_far = swap(a, *axes[0]), swap(jnp.concatenate([b, taps]), *axes[0])
    a_other, b_other = swap(a, over_core), swap(b, over_core)
    (frame_grad,) = call(
        frame_kernel, (shape(frames.shape, BF),), [], 8,
        bits, after(dconv, a), x_got, z_got, cotangent, kernel,
    )
    (layer_out,) = call(
        functools.partial(layer_kernel, plan), (shape(frames.shape, BF),), [here],
        10, *home, after(frames, a), weights,
    )
    grads = final(((1, 0, 0), (1, 1, 0), (0, 0, 0), (0, 1, 0)), (a, b, a_other, b_other), ())
    a_far, b_far, frame_grad, layer_out, *grads = lax.optimization_barrier(
        (a_far, b_far, frame_grad, layer_out, *grads)
    )
    k = b.shape[0]
    taps = total(taps, b_far[k:])
    a_other = swap(a_far, over_core)
    b_other = swap(jnp.concatenate([b_far[:k], taps]), over_core)
    taps = total(taps, b_other[k:])
    grads = final(((1, 0, 1), (1, 1, 1)), (a_far, b_far), grads)
    *grads, kernel_grad = final(((0, 0, 1), (0, 1, 1)), (a_other, b_other), grads, (taps,))
    return (layer_out, frame_grad, kernel_grad, *grads)


def solution(mesh):
    in_specs = (P("mic", "tm", None), P("mic", "tm", None), P(), P(), P(), P(), P())
    out_specs = (P("mic", "tm", None), P("mic", "tm", None), P(), P(), P(), P(), P())
    return jax.shard_map(shards, mesh=mesh, in_specs=in_specs, out_specs=out_specs, check_vma=False)
```

```python
import functools
import math

import jax
import jax.numpy as jnp
from jax import lax
from jax.experimental import pallas as pl
from jax.experimental.pallas import tpu as pltpu
from jax.sharding import PartitionSpec as P

HEADS = 8
LANES = 128
HALO = 16
NT = (((1,), (1,)), ((), ()))
TN = (((0,), (0,)), ((), ()))
BF = jnp.bfloat16
F32 = jnp.float32
MIB = 1024 * 1024
CORE, Y, X, Z, ZZ, ODD, SKIP, BLOCK_AT = range(8)


def mm(left, right, dims=(((1,), (0,)), ((), ()))):
    return lax.dot_general(left, right, dims, preferred_element_type=F32)


def rolled(x, shift):
    return x if shift == 0 else pltpu.roll(x, x.shape[0] - shift, axis=0)


def window(x, taps, rows):
    acc = None
    for r in range(8):
        xr = rolled(x, r)
        for k in range(4):
            o = 8 * k + r
            if o == 0:
                continue
            term = xr[8 * k : 8 * k + rows] * taps(o)
            acc = term if acc is None else acc + term
    return acc


def ways(bits, half):
    return [bits[i] for i in ((X, Y, Z), (Z, X, ZZ))[half]]


def sigmoid(v):
    return 0.5 * jnp.tanh(0.5 * v) + 0.5


def edge_kernel(sub, bits, f0, f1, f2, f3, near, side):
    odd = bits[ODD]
    for d, f in enumerate((f0, f1, f2, f3)):
        last = sub - HALO
        near[d] = f[:, pl.ds(pl.multiple_of((1 - odd) * last, HALO), HALO), :]
        side[d] = f[:, pl.ds(pl.multiple_of(odd * last, HALO), HALO), :]


def frames_window(bits, frames, near, side, a, m, lanes):
    is_odd = jnp.broadcast_to(bits[ODD], (HALO, LANES)) == 1
    one = near[a ^ 1, m, :, lanes].astype(F32)
    two = side[a ^ bits[SKIP], m, :, lanes].astype(F32)
    return jnp.concatenate(
        [
            jnp.where(is_odd, one, two),
            frames[a, m, :, lanes].astype(F32),
            jnp.where(is_odd, two, one),
        ],
        axis=0,
    )


def conv_kernel(plan, bits, f0, f1, f2, f3, near, side, kern, frames, conv_out, acted_out):
    groups, count, sub, width = plan
    mics = groups * count
    cuts = sub // HALO
    for d, f in enumerate((f0, f1, f2, f3)):
        frames[d] = f[...]

    def conv_step(n, _):
        a, m = n // count, n % count
        for lc in range(width // LANES):
            lanes = slice(lc * LANES, (lc + 1) * LANES)
            x = frames_window(bits, frames, near, side, a, m, lanes)
            conv = window(x, lambda o: kern[o - 1 : o, lanes], sub)
            acted = (conv * sigmoid(conv)).astype(BF)
            for c in range(cuts):
                at = pl.multiple_of((c * mics + n) * HALO, HALO)
                conv_out[pl.ds(at, HALO), lanes] = conv[c * HALO : (c + 1) * HALO]
                acted_out[pl.ds(at, HALO), lanes] = acted[c * HALO : (c + 1) * HALO]
        return 0

    lax.fori_loop(0, mics, conv_step, 0)


def main_kernel(
    plan, bits, frames, conv_in, acted_in, c0, c1, c2, c3, near, side, weights,
    a_keep, b_keep, a_send, b_send, back_keep, back_send,
    left_s, right_s, q_s, k_s, v_s, u_s, dconv_s, tap_s,
):
    groups, count, sub, width, factor = plan
    mics = groups * count
    cuts = sub // HALO
    block = mics * HALO
    rows = cuts * block
    cols = width // LANES

    wq, wk, wv, wo = (weights.at[i] for i in range(4))
    left_s[0] = acted_in[...]
    for d, cot in enumerate((c0, c1, c2, c3)):
        for m in range(count):
            for c in range(cuts):
                right_s[3, c, d, m] = cot[m, c * HALO : (c + 1) * HALO, :]

    def flat(i):
        return right_s[i].reshape(rows, width)

    def put(i, c, lanes, x):
        right_s[i, c, :, :, :, lanes] = x.astype(BF).reshape(groups, count, HALO, LANES)

    acted = left_s[0]
    q_s[...] = mm(acted, wq[...]).astype(BF)
    k_s[...] = mm(acted, wk[...]).astype(BF)
    v_s[...] = mm(acted, wv[...]).astype(BF)
    u_s[...] = mm(flat(3), wo[...], NT).astype(BF)

    depth = width // HEADS
    per = LANES // depth
    lane = lax.broadcasted_iota(jnp.int32, (block, LANES), 1)
    row_i = lax.broadcasted_iota(jnp.int32, (block, per * block), 0)
    col_i = lax.broadcasted_iota(jnp.int32, (block, per * block), 1)
    same = (row_i % HALO) == (col_i % HALO)

    def by_head(x):
        return jnp.concatenate(
            [jnp.where(lane // depth == h, x, jnp.zeros_like(x)) for h in range(per)], axis=0
        )

    def sums(x):
        return [
            jnp.sum(x[:, h * block : (h + 1) * block], axis=1, keepdims=True) for h in range(per)
        ]

    def each(x, values, op):
        return jnp.concatenate(
            [op(x[:, h * block : (h + 1) * block], values[h]) for h in range(per)], axis=1
        )

    def pick(x):
        out = x[:block]
        for h in range(1, per):
            out = jnp.where(lane // depth == h, x[h * block : (h + 1) * block], out)
        return out

    for c in range(cuts):
        part = slice(c * block, (c + 1) * block)
        for p in range(cols):
            lanes = slice(p * LANES, (p + 1) * LANES)
            q, u = q_s[part, lanes], u_s[part, lanes]
            kc, vc = by_head(k_s[part, lanes]), by_head(v_s[part, lanes])
            e = jnp.where(same, jnp.exp(mm(q, kc, NT) * factor), 0.0)
            w = each(e, [1.0 / x for x in sums(e)], lambda x, s: x * s)
            up = mm(u, vc, NT)
            inner = each(up, sums(w * up), lambda x, s: x - s) * w * factor
            wb, ib = w.astype(BF), inner.astype(BF)
            left_s[1, part, lanes] = mm(wb, vc).astype(BF)
            put(0, c, lanes, mm(ib, kc))
            put(1, c, lanes, pick(mm(ib, q, TN)))
            put(2, c, lanes, pick(mm(wb, u, TN)))

    dacted = mm(flat(0), wq[...], NT) + mm(flat(1), wk[...], NT) + mm(flat(2), wv[...], NT)
    conv = conv_in[...]
    sig = sigmoid(conv)
    dconv_s[...] = dacted * sig * (1.0 + conv * (1.0 - sig))

    for lc in range(cols):
        lanes = slice(lc * LANES, (lc + 1) * LANES)

        def tap_step(n, accs):
            a, m = n // count, n % count
            x = frames_window(bits, frames, near, side, a, m, lanes)
            d = jnp.concatenate(
                [
                    dconv_s[pl.ds(pl.multiple_of(c * block + n * HALO, HALO), HALO), lanes]
                    for c in range(cuts)
                ],
                axis=0,
            )
            out = list(accs)
            for r in range(8):
                xr = rolled(x, r)
                for k in range(4):
                    o = 8 * k + r
                    if o == 0:
                        continue
                    prod = xr[8 * k : 8 * k + sub] * d
                    out[o - 1] = out[o - 1] + jnp.sum(prod.reshape(sub // 8, 8, LANES), axis=0)
            return tuple(out)

        accs = lax.fori_loop(0, mics, tap_step, tuple(jnp.zeros((8, LANES), F32) for _ in range(31)))
        tap_s[lc * 32 : lc * 32 + 32, :] = jnp.concatenate(
            [jnp.sum(x, axis=0, keepdims=True) for x in accs] + [jnp.zeros((1, LANES), F32)], axis=0
        )

    tap_s[cols * 32 :, :] = jnp.zeros((HALO, LANES), F32)
    size = cols * width // 8
    core = bits[CORE]
    for out, owner, h in (
        (a_send, 1 - core, 0), (b_send, 1 - core, 1), (a_keep, core, 0), (b_keep, core, 1)
    ):
        i = owner * 2 + h
        span = size + HALO * (1 - h)
        first, second, third = ways(bits, h)
        grad = mm(left_s[i // 3], flat(i), TN).astype(BF)
        for piece in range(8):
            cb, at = piece * size // width, piece * size % width
            rel = ((piece // 4) ^ first) * 4 + ((piece // 2 % 2) ^ second) * 2 + ((piece % 2) ^ third)
            start = pl.multiple_of(rel * span, HALO)
            out[pl.ds(start, size), :] = grad[at : at + size, cb * LANES : (cb + 1) * LANES]
            if h == 0:
                tail = tap_s[pl.ds(pl.multiple_of((owner * 8 + piece) * 8, 8), HALO), :]
                out[pl.ds(pl.multiple_of(start + size, HALO), HALO), :] = tail.astype(BF)

    proj = mm(left_s[1], wo[...])
    unit = 2 * count * cols * sub
    for d, (out, base) in enumerate(
        ((back_keep, 0), (back_send, 0), (back_keep, unit), (back_send, unit))
    ):
        for m in range(count):
            for c in range(cuts):
                at = c * block + (d * count + m) * HALO
                part = slice(c * HALO, (c + 1) * HALO)
                layer = (frames[d, m, part, :].astype(F32) + proj[at : at + HALO]).astype(BF)
                dconv = dconv_s[at : at + HALO, :].astype(BF)
                for lc in range(cols):
                    for kind, value in enumerate((layer, dconv)):
                        to = base + ((kind * count + m) * cols + lc) * sub + c * HALO
                        out[to : to + HALO, :] = value[:, lc * LANES : (lc + 1) * LANES]


def total(*parts):
    return functools.reduce(lambda x, y: x + y, [x.astype(F32) for x in parts]).astype(BF)


def final_kernel(plan, bits, *refs):
    kinds, first_call, with_taps, width, norm = plan
    cols = width // LANES
    size = cols * width // 8
    span = size + HALO
    core = bits[CORE]

    def piece_of(h, far, rel):
        first, second, third = ways(bits, h)
        return (first ^ far) * 4 + (second ^ (rel // 2)) * 2 + (third ^ (rel % 2))

    got, refs = refs[: len(kinds)], refs[len(kinds) :]
    if with_taps:
        tap_refs, refs, tap_grad, tap_s = refs[:4], refs[4:-4] + refs[-3:-1], refs[-4], refs[-1]
        for n, ref in enumerate(tap_refs):
            owner = core if n < 2 else 1 - core
            for rel in range(4):
                at = rel * span + size
                tap_s[owner * 8 + piece_of(0, n % 2, rel)] = ref[at : at + HALO, :].astype(F32) * norm
        for g in range(16):
            lc, j = g // 4, g % 4 * 8
            kept = min(8, 31 - j)
            tap_grad[j : j + kept, lc * LANES : (lc + 1) * LANES] = tap_s[g, 0:kept]
    *outs, piece_s, sems = refs if first_call else refs[4:]
    copies = []
    for n, (own, h, far) in enumerate(kinds):
        owner = core if own else 1 - core
        for rel in range(4):
            k = 4 * n + rel
            at = rel * (size + HALO * (1 - h))
            piece_s[k] = got[n][at : at + size, :].astype(F32) * norm
            piece = piece_of(h, far, rel)
            cb, at = piece * size // width, piece * size % width
            rows = pl.ds(pl.multiple_of(at, size), size)
            lanes = pl.ds(pl.multiple_of(cb * LANES, LANES), LANES)
            for which in range(2):
                copy = pltpu.make_async_copy(
                    piece_s.at[k], outs[2 * which + h].at[rows, lanes], sems.at[k]
                )
                copies.append((owner == which, copy))
                pl.when(owner == which)(copy.start)
    for here, copy in copies:
        pl.when(here)(copy.wait)


def home_kernel(plan, bits, own, core_got, y_got, layer_out, dconv, x_edge, z_edge):
    count, sub, cols = plan
    unit = 2 * count * cols * sub
    odd = bits[X]
    last = 3 * sub + sub - HALO
    for d, (ref, base) in enumerate(
        ((own, 0), (core_got, 0), (y_got, 0), (y_got, unit))
    ):
        to = pl.ds(pl.multiple_of(bits[BLOCK_AT + d] * sub, sub), sub)
        for m in range(count):
            for lc in range(cols):
                at = base + (m * cols + lc) * sub
                layer_out[m, to, lc * LANES : (lc + 1) * LANES] = ref[at : at + sub, :]
                at += count * cols * sub
                dconv[m, lc, to, :] = ref[at : at + sub, :]
    for m in range(count):
        for lc in range(cols):
            at = (m * cols + lc) * HALO
            x_rows = pl.ds(pl.multiple_of((1 - odd) * last, HALO), HALO)
            z_rows = pl.ds(pl.multiple_of(odd * last, HALO), HALO)
            x_edge[at : at + HALO, :] = dconv[m, lc, x_rows, :]
            z_edge[at : at + HALO, :] = dconv[m, lc, z_rows, :]


def frame_kernel(plan, bits, dconv, x_got, z_got, cot, kern, frame_grad):
    count, cols, x_at, length = plan
    is_odd = jnp.broadcast_to(bits[X], (HALO, LANES)) == 1

    def step(m, _):
        for lc in range(cols):
            lanes = slice(lc * LANES, (lc + 1) * LANES)
            at = pl.multiple_of((m * cols + lc) * HALO, HALO)
            one = x_got[pl.ds(pl.multiple_of(x_at + at, HALO), HALO), :].astype(F32)
            two = z_got[pl.ds(at, HALO), :].astype(F32)
            x = jnp.concatenate(
                [
                    jnp.where(is_odd, one, two),
                    dconv[m, lc].astype(F32),
                    jnp.where(is_odd, two, one),
                ],
                axis=0,
            )
            grad = window(x, lambda o: kern[31 - o : 32 - o, lanes], length)
            frame_grad[m, :, lanes] = (cot[m, :, lanes].astype(F32) + grad).astype(BF)
        return 0

    lax.fori_loop(0, count, step, 0)


def call(body, outs, scratch, limit, *args, hbm=(), hbm_outs=(), aliases=None):
    spaces = [pltpu.HBM if i in hbm else pltpu.VMEM for i in range(len(args))]
    return pl.pallas_call(
        body,
        out_shape=outs,
        in_specs=[
            pl.BlockSpec(memory_space=pltpu.SMEM if x.dtype == jnp.int32 else space)
            for x, space in zip(args, spaces)
        ],
        out_specs=tuple(
            pl.BlockSpec(memory_space=pltpu.HBM if i in hbm_outs else pltpu.VMEM)
            for i in range(len(outs))
        ),
        scratch_shapes=scratch,
        input_output_aliases=aliases or {},
        compiler_params=pltpu.CompilerParams(vmem_limit_bytes=limit * MIB),
    )(*args)


def shards(frames, cotangent, kernel, w_query, w_key, w_value, w_out):
    groups, blocks = lax.axis_size("mic"), lax.axis_size("tm")
    count, length, width = frames.shape
    sub = length // groups
    cuts = sub // HALO
    cols = width // LANES
    rows = groups * count * sub
    shape = jax.ShapeDtypeStruct

    mic, tm = lax.axis_index("mic"), lax.axis_index("tm")
    over_core, over_y, over_x, over_z = blocks, 2 * blocks, 1, 2

    def order(a):
        return (a ^ (a >> 1)) ^ (3 * (tm % 2))

    mine = order(mic)
    bits = jnp.stack(
        [mic % 2, mic // 2, tm % 2, tm // 2 % 2, tm // 4 % 2, mine % 2, 2 * ((mine + 1) // 2 % 2)]
        + [order(mic ^ d) for d in range(4)]
    ).astype(jnp.int32)

    def permute(x, pairs):
        return lax.ppermute(x, ("mic", "tm"), pairs)

    def swap(x, mask):
        return permute(x, [(f, f ^ mask) for f in range(groups * blocks)])

    def both(pairs):
        return pairs + [(j, i) for i, j in pairs]

    masks = (0, over_core, over_y, over_core + over_y)

    def scattered(x):
        parts = [
            lax.dynamic_slice_in_dim(x, order(mic ^ d) * sub, sub, axis=1) for d in range(4)
        ]
        got = {d: swap(parts[d], masks[d]) for d in (2, 3, 1)}
        return [parts[0], got[1], got[2], got[3]]

    f, c = scattered(frames), scattered(cotangent)
    weights = jnp.stack([w_query, w_key, w_value, w_out])
    edge = shape((groups, count, HALO, width), BF)
    near, side = call(functools.partial(edge_kernel, sub), (edge, edge), [], 8, bits, *f)
    near, side, weights = lax.optimization_barrier((near, side, weights))
    near = swap(near, over_core)
    side = permute(
        side,
        both([(blocks + t, 3 * blocks + t) for t in range(blocks)])
        + both([((2 - 2 * (t % 2)) * blocks + t, (2 - 2 * (t % 2)) * blocks + t + 1)
                for t in range(blocks - 1)]),
    )

    factor = 1.0 / math.sqrt(width // HEADS)
    size = width * width // LANES // 8
    span = size + HALO
    unit = 2 * count * cols * sub
    big = pltpu.VMEM((rows, width), BF)
    wide = pltpu.VMEM((rows, width), F32)

    def flat(n):
        return shape((n, LANES), BF)

    moved = shape((groups, count, sub, width), BF)
    placed, conv, acted = call(
        functools.partial(conv_kernel, (groups, count, sub, width)),
        (moved, shape((rows, width), F32), shape((rows, width), BF)),
        [], 8, bits, *f, near, side, kernel,
    )
    a_keep, b_keep, a_send, b_send, back_keep, back_send = call(
        functools.partial(main_kernel, (groups, count, sub, width, factor)),
        (flat(8 * span), flat(8 * size)) * 2 + (flat(2 * unit),) * 2,
        [
            pltpu.VMEM((2, rows, width), BF),
            pltpu.VMEM((4, cuts, groups, count, HALO, width), BF),
            big, big, big, big, wide,
            pltpu.VMEM((32 * cols + HALO, LANES), F32),
        ],
        24, bits, placed, conv, acted, *c, near, side, weights,
    )

    lines = [2**i for i in range(1, blocks.bit_length() - 1)]

    def after(x, y):
        return lax.optimization_barrier((x, y))[0]

    def halved(parts, mask):
        n = parts[0].shape[0] // 2
        return [t[:n] for t in parts] + [swap(total(*(t[n:] for t in parts)), mask)]

    def exchanged(parts, masks):
        mine = total(*parts)
        for mask in masks:
            mine = total(mine, swap(mine, mask))
        return mine

    def doubled(x, mask):
        return jnp.concatenate([x, swap(x, mask)])

    a = [a_keep, swap(a_send, over_core)]
    b = [b_keep, swap(b_send, over_core)]
    core_got = swap(back_send, over_core)
    a = halved(a, over_x)
    b = halved(b, lines[0])
    y_got = swap(jnp.concatenate([back_keep[unit:], core_got[unit:]]), over_y)
    edge = flat(count * cols * HALO)
    layer_out, dconv, x_edge, z_edge = call(
        functools.partial(home_kernel, (count, sub, cols)),
        (shape(frames.shape, BF), shape((count, cols, length, LANES), BF), edge, edge),
        [], 8, bits, back_keep, core_got, y_got,
    )
    a = halved(a, over_y)
    b = halved(b, over_x)
    a = halved(a, lines[0])
    b = halved(b, lines[1])
    a = exchanged(a, lines[1:])
    b = exchanged(b, [over_y] + lines[2:])
    x_got = swap(x_edge, over_x)
    z_got = permute(
        after(z_edge, a),
        both([(m * blocks + t, m * blocks + t + 1)
              for m in range(groups) for t in range(1, blocks - 1, 2)]),
    )
    a = doubled(a, lines[0])
    b = doubled(b, lines[1])
    a = doubled(after(a, x_got), over_y)
    b = doubled(after(b, z_got), over_x)

    norm = 1.0 / math.sqrt(groups * count * blocks * length)
    square = shape((width, width), F32)

    def final(kinds, parts, grads, taps=()):
        first = 1 + len(parts) + len(taps)
        scratch = [
            pltpu.VMEM((4 * len(kinds), size, LANES), F32),
            pltpu.SemaphoreType.DMA((4 * len(kinds),)),
        ]
        return call(
            functools.partial(final_kernel, (kinds, not grads, bool(taps), width, norm)),
            (square,) * 4 + (shape((31, width), F32),) * bool(taps),
            scratch + [pltpu.VMEM((16, HALO, LANES), F32)] * bool(taps),
            10, bits, *parts, *taps, *grads, hbm=range(first, first + len(grads)),
            hbm_outs=range(4), aliases={first + i: i for i in range(len(grads))},
        )

    a_far, b_far = swap(a, over_x), swap(b, lines[0])
    a_other, b_other = swap(a, over_core), swap(b, over_core)
    (frame_grad,) = call(
        functools.partial(frame_kernel, (count, cols, 0, length)),
        (shape(frames.shape, BF),), [], 8,
        bits, after(dconv, a), x_got, z_got, cotangent, kernel,
    )
    grads = final(((1, 0, 0), (1, 1, 0), (0, 0, 0), (0, 1, 0)), (a, b, a_other, b_other), ())
    a_far, b_far, frame_grad, *grads = lax.optimization_barrier(
        (a_far, b_far, frame_grad, *grads)
    )
    taps = (a, a_far, a_other)
    a_other, b_other = swap(a_far, over_core), swap(b_far, over_core)
    grads = final(((1, 0, 1), (1, 1, 1)), (a_far, b_far), grads)
    *grads, kernel_grad = final(
        ((0, 0, 1), (0, 1, 1)), (a_other, b_other), grads, (*taps, a_other)
    )
    return (layer_out, frame_grad, kernel_grad, *grads)


def solution(mesh):
    in_specs = (P("mic", "tm", None), P("mic", "tm", None), P(), P(), P(), P(), P())
    out_specs = (P("mic", "tm", None), P("mic", "tm", None), P(), P(), P(), P(), P())
    return jax.shard_map(shards, mesh=mesh, in_specs=in_specs, out_specs=out_specs, check_vma=False)
```

```python
import functools
import math

import jax
import jax.numpy as jnp
from jax import lax
from jax.experimental import pallas as pl
from jax.experimental.pallas import tpu as pltpu
from jax.sharding import PartitionSpec as P

HEADS = 8
LANES = 128
HALO = 16
NT = (((1,), (1,)), ((), ()))
TN = (((0,), (0,)), ((), ()))
BF = jnp.bfloat16
F32 = jnp.float32
MIB = 1024 * 1024
CORE, Y, X, Z, ZZ, ODD, SKIP, BLOCK_AT = range(8)


def mm(left, right, dims=(((1,), (0,)), ((), ()))):
    return lax.dot_general(left, right, dims, preferred_element_type=F32)


def rolled(x, shift):
    return x if shift == 0 else pltpu.roll(x, x.shape[0] - shift, axis=0)


def window(x, taps, rows):
    acc = None
    for r in range(8):
        xr = rolled(x, r)
        for k in range(4):
            o = 8 * k + r
            if o == 0:
                continue
            term = xr[8 * k : 8 * k + rows] * taps(o)
            acc = term if acc is None else acc + term
    return acc


def ways(bits, half):
    return [bits[i] for i in ((X, Y, Z), (Z, X, ZZ))[half]]


def sigmoid(v):
    return 0.5 * jnp.tanh(0.5 * v) + 0.5


def edge_kernel(sub, bits, f0, pair, f2, f3, near, side):
    odd = bits[ODD]
    for d, f in enumerate((f0, pair.at[0], f2, f3)):
        last = sub - HALO
        near[d] = f[:, pl.ds(pl.multiple_of((1 - odd) * last, HALO), HALO), :]
        side[d] = f[:, pl.ds(pl.multiple_of(odd * last, HALO), HALO), :]


def frames_window(bits, frames, near, side, a, m, lanes):
    is_odd = jnp.broadcast_to(bits[ODD], (HALO, LANES)) == 1
    one = near[a ^ 1, m, :, lanes].astype(F32)
    two = side[a ^ bits[SKIP], m, :, lanes].astype(F32)
    return jnp.concatenate(
        [
            jnp.where(is_odd, one, two),
            frames[a, m, :, lanes].astype(F32),
            jnp.where(is_odd, two, one),
        ],
        axis=0,
    )


def conv_kernel(plan, bits, f0, pair, f2, f3, near, side, kern, frames, conv_out, acted_out):
    groups, count, sub, width = plan
    mics = groups * count
    cuts = sub // HALO
    for d, f in enumerate((f0, pair.at[0], f2, f3)):
        frames[d] = f[...]

    def conv_step(n, _):
        a, m = n // count, n % count
        for lc in range(width // LANES):
            lanes = slice(lc * LANES, (lc + 1) * LANES)
            x = frames_window(bits, frames, near, side, a, m, lanes)
            conv = window(x, lambda o: kern[o - 1 : o, lanes], sub)
            acted = (conv * sigmoid(conv)).astype(BF)
            for c in range(cuts):
                at = pl.multiple_of((c * mics + n) * HALO, HALO)
                conv_out[pl.ds(at, HALO), lanes] = conv[c * HALO : (c + 1) * HALO]
                acted_out[pl.ds(at, HALO), lanes] = acted[c * HALO : (c + 1) * HALO]
        return 0

    lax.fori_loop(0, mics, conv_step, 0)


def main_kernel(
    plan, bits, frames, conv_in, acted_in, c0, pair, c2, c3, near, side, weights,
    a_keep, b_keep, a_send, b_send, back_keep, back_send,
    left_s, turned_s, right_s, q_s, k_s, v_s, u_s, dconv_s, tap_s,
):
    groups, count, sub, width, factor = plan
    mics = groups * count
    cuts = sub // HALO
    block = mics * HALO
    rows = cuts * block
    cols = width // LANES

    wq, wk, wv, wo = (weights.at[i] for i in range(4))
    left_s[0] = acted_in[...]
    for d, cot in enumerate((c0, pair.at[1], c2, c3)):
        for m in range(count):
            for c in range(cuts):
                right_s[3, c, d, m] = cot[m, c * HALO : (c + 1) * HALO, :]

    def flat(i):
        return right_s[i].reshape(rows, width)

    def put(i, c, lanes, x):
        right_s[i, c, :, :, :, lanes] = x.astype(BF).reshape(groups, count, HALO, LANES)

    acted = left_s[0]
    q_s[...] = mm(acted, wq[...]).astype(BF)
    k_s[...] = mm(acted, wk[...]).astype(BF)
    v_s[...] = mm(acted, wv[...]).astype(BF)
    u_s[...] = mm(flat(3), wo[...], NT).astype(BF)
    turned_s[0] = acted.T

    depth = width // HEADS
    per = LANES // depth
    lane = lax.broadcasted_iota(jnp.int32, (block, LANES), 1)
    row_i = lax.broadcasted_iota(jnp.int32, (block, per * block), 0)
    col_i = lax.broadcasted_iota(jnp.int32, (block, per * block), 1)
    same = (row_i % HALO) == (col_i % HALO)

    def by_head(x):
        return jnp.concatenate(
            [jnp.where(lane // depth == h, x, jnp.zeros_like(x)) for h in range(per)], axis=0
        )

    def sums(x):
        return [
            jnp.sum(x[:, h * block : (h + 1) * block], axis=1, keepdims=True) for h in range(per)
        ]

    def each(x, values, op):
        return jnp.concatenate(
            [op(x[:, h * block : (h + 1) * block], values[h]) for h in range(per)], axis=1
        )

    def pick(x):
        out = x[:block]
        for h in range(1, per):
            out = jnp.where(lane // depth == h, x[h * block : (h + 1) * block], out)
        return out

    for c in range(cuts):
        part = slice(c * block, (c + 1) * block)
        for p in range(cols):
            lanes = slice(p * LANES, (p + 1) * LANES)
            q, u = q_s[part, lanes], u_s[part, lanes]
            kc, vc = by_head(k_s[part, lanes]), by_head(v_s[part, lanes])
            e = jnp.where(same, jnp.exp(mm(q, kc, NT) * factor), 0.0)
            w = each(e, [1.0 / x for x in sums(e)], lambda x, s: x * s)
            up = mm(u, vc, NT)
            inner = each(up, sums(w * up), lambda x, s: x - s) * w * factor
            wb, ib = w.astype(BF), inner.astype(BF)
            left_s[1, part, lanes] = mm(wb, vc).astype(BF)
            put(0, c, lanes, mm(ib, kc))
            put(1, c, lanes, pick(mm(ib, q, TN)))
            put(2, c, lanes, pick(mm(wb, u, TN)))

    turned_s[1] = left_s[1].T
    dacted = mm(flat(0), wq[...], NT) + mm(flat(1), wk[...], NT) + mm(flat(2), wv[...], NT)
    conv = conv_in[...]
    sig = sigmoid(conv)
    dconv_s[...] = dacted * sig * (1.0 + conv * (1.0 - sig))

    for lc in range(cols):
        lanes = slice(lc * LANES, (lc + 1) * LANES)

        def tap_step(n, accs):
            a, m = n // count, n % count
            x = frames_window(bits, frames, near, side, a, m, lanes)
            d = jnp.concatenate(
                [
                    dconv_s[pl.ds(pl.multiple_of(c * block + n * HALO, HALO), HALO), lanes]
                    for c in range(cuts)
                ],
                axis=0,
            )
            out = list(accs)
            for r in range(8):
                xr = rolled(x, r)
                for k in range(4):
                    o = 8 * k + r
                    if o == 0:
                        continue
                    prod = xr[8 * k : 8 * k + sub] * d
                    out[o - 1] = out[o - 1] + jnp.sum(prod.reshape(sub // 8, 8, LANES), axis=0)
            return tuple(out)

        accs = lax.fori_loop(0, mics, tap_step, tuple(jnp.zeros((8, LANES), F32) for _ in range(31)))
        tap_s[lc * 32 : lc * 32 + 32, :] = jnp.concatenate(
            [jnp.sum(x, axis=0, keepdims=True) for x in accs] + [jnp.zeros((1, LANES), F32)], axis=0
        )

    tap_s[cols * 32 :, :] = jnp.zeros((HALO, LANES), F32)
    size = cols * width // 8
    core = bits[CORE]
    for out, owner, h in (
        (a_send, 1 - core, 0), (b_send, 1 - core, 1), (a_keep, core, 0), (b_keep, core, 1)
    ):
        i = owner * 2 + h
        span = size + HALO * (1 - h)
        first, second, third = ways(bits, h)
        grad = mm(turned_s[i // 3], flat(i)).astype(BF)
        for piece in range(8):
            cb, at = piece * size // width, piece * size % width
            rel = ((piece // 4) ^ first) * 4 + ((piece // 2 % 2) ^ second) * 2 + ((piece % 2) ^ third)
            start = pl.multiple_of(rel * span, HALO)
            out[pl.ds(start, size), :] = grad[at : at + size, cb * LANES : (cb + 1) * LANES]
            if h == 0:
                tail = tap_s[pl.ds(pl.multiple_of((owner * 8 + piece) * 8, 8), HALO), :]
                out[pl.ds(pl.multiple_of(start + size, HALO), HALO), :] = tail.astype(BF)

    proj = mm(left_s[1], wo[...])
    unit = 2 * count * cols * sub
    for d, (out, base) in enumerate(
        ((back_keep, 0), (back_send, 0), (back_keep, unit), (back_send, unit))
    ):
        for m in range(count):
            for c in range(cuts):
                at = c * block + (d * count + m) * HALO
                part = slice(c * HALO, (c + 1) * HALO)
                layer = (frames[d, m, part, :].astype(F32) + proj[at : at + HALO]).astype(BF)
                dconv = dconv_s[at : at + HALO, :].astype(BF)
                for lc in range(cols):
                    for kind, value in enumerate((layer, dconv)):
                        to = base + ((kind * count + m) * cols + lc) * sub + c * HALO
                        out[to : to + HALO, :] = value[:, lc * LANES : (lc + 1) * LANES]


def total(*parts):
    return functools.reduce(lambda x, y: x + y, [x.astype(F32) for x in parts]).astype(BF)


def final_kernel(plan, bits, *refs):
    kinds, first_call, with_taps, width, norm = plan
    cols = width // LANES
    size = cols * width // 8
    span = size + HALO
    core = bits[CORE]

    def piece_of(h, far, rel):
        first, second, third = ways(bits, h)
        return (first ^ far) * 4 + (second ^ (rel // 2)) * 2 + (third ^ (rel % 2))

    got, refs = refs[: len(kinds)], refs[len(kinds) :]
    if with_taps:
        tap_refs, refs, tap_grad, tap_s = refs[:4], refs[4:-4] + refs[-3:-1], refs[-4], refs[-1]
    *outs, piece_s, sems = refs if first_call else refs[4:]
    copies = []
    for n, (own, h, far) in enumerate(kinds):
        owner = core if own else 1 - core
        for rel in range(4):
            k = 4 * n + rel
            at = rel * (size + HALO * (1 - h))
            piece_s[k] = got[n][at : at + size, :].astype(F32) * norm
            piece = piece_of(h, far, rel)
            cb, at = piece * size // width, piece * size % width
            rows = pl.ds(pl.multiple_of(at, size), size)
            lanes = pl.ds(pl.multiple_of(cb * LANES, LANES), LANES)
            for which in range(2):
                copy = pltpu.make_async_copy(
                    piece_s.at[k], outs[2 * which + h].at[rows, lanes], sems.at[k]
                )
                copies.append((owner == which, copy))
                pl.when(owner == which)(copy.start)
    if with_taps:
        for n, ref in enumerate(tap_refs):
            owner = core if n < 2 else 1 - core
            for rel in range(4):
                at = rel * span + size
                tap_s[owner * 8 + piece_of(0, n % 2, rel)] = ref[at : at + HALO, :].astype(F32) * norm
        for g in range(16):
            lc, j = g // 4, g % 4 * 8
            kept = min(8, 31 - j)
            tap_grad[j : j + kept, lc * LANES : (lc + 1) * LANES] = tap_s[g, 0:kept]
    for here, copy in copies:
        pl.when(here)(copy.wait)


def home_kernel(plan, bits, own, core_got, y_got, layer_out, dconv, first_edge, last_edge):
    count, sub, cols = plan
    unit = 2 * count * cols * sub
    last = 4 * sub - HALO
    for d, (ref, base) in enumerate(
        ((own, 0), (core_got, 0), (y_got, 0), (y_got, unit))
    ):
        to = pl.ds(pl.multiple_of(bits[BLOCK_AT + d] * sub, sub), sub)
        for m in range(count):
            for lc in range(cols):
                at = base + (m * cols + lc) * sub
                layer_out[m, to, lc * LANES : (lc + 1) * LANES] = ref[at : at + sub, :]
                at += count * cols * sub
                dconv[m, lc, to, :] = ref[at : at + sub, :]
    for m in range(count):
        for lc in range(cols):
            at = (m * cols + lc) * HALO
            first_edge[at : at + HALO, :] = dconv[m, lc, :HALO, :]
            last_edge[at : at + HALO, :] = dconv[m, lc, last:, :]


def frame_kernel(plan, bits, dconv, x_got, z_got, other_got, cot, kern, frame_grad):
    count, cols, length = plan
    is_odd = jnp.broadcast_to(bits[X], (HALO, LANES)) == 1
    by_z = jnp.broadcast_to(bits[X] ^ bits[Z], (HALO, LANES)) == 1

    def step(m, _):
        for lc in range(cols):
            lanes = slice(lc * LANES, (lc + 1) * LANES)
            at = (m * cols + lc) * HALO
            rows = pl.ds(pl.multiple_of(at, HALO), HALO)
            x_rows = pl.ds(pl.multiple_of(bits[X] * count * cols * HALO + at, HALO), HALO)
            one = x_got[x_rows, :].astype(F32)
            two = jnp.where(by_z, z_got[rows, :].astype(F32), other_got[rows, :].astype(F32))
            x = jnp.concatenate(
                [
                    jnp.where(is_odd, one, two),
                    dconv[m, lc].astype(F32),
                    jnp.where(is_odd, two, one),
                ],
                axis=0,
            )
            grad = window(x, lambda o: kern[31 - o : 32 - o, lanes], length)
            frame_grad[m, :, lanes] = (cot[m, :, lanes].astype(F32) + grad).astype(BF)
        return 0

    lax.fori_loop(0, count, step, 0)


def call(body, outs, scratch, limit, *args, hbm=(), hbm_outs=(), aliases=None):
    spaces = [pltpu.HBM if i in hbm else pltpu.VMEM for i in range(len(args))]
    return pl.pallas_call(
        body,
        out_shape=outs,
        in_specs=[
            pl.BlockSpec(memory_space=pltpu.SMEM if x.dtype == jnp.int32 else space)
            for x, space in zip(args, spaces)
        ],
        out_specs=tuple(
            pl.BlockSpec(memory_space=pltpu.HBM if i in hbm_outs else pltpu.VMEM)
            for i in range(len(outs))
        ),
        scratch_shapes=scratch,
        input_output_aliases=aliases or {},
        compiler_params=pltpu.CompilerParams(vmem_limit_bytes=limit * MIB),
    )(*args)


def shards(frames, cotangent, kernel, w_query, w_key, w_value, w_out):
    groups, blocks = lax.axis_size("mic"), lax.axis_size("tm")
    count, length, width = frames.shape
    sub = length // groups
    cuts = sub // HALO
    cols = width // LANES
    rows = groups * count * sub
    shape = jax.ShapeDtypeStruct

    mic, tm = lax.axis_index("mic"), lax.axis_index("tm")
    over_core, over_y, over_x, over_z = blocks, 2 * blocks, 1, 2

    def order(a):
        return (a ^ (a >> 1)) ^ (3 * (tm % 2))

    mine = order(mic)
    bits = jnp.stack(
        [mic % 2, mic // 2, tm % 2, tm // 2 % 2, tm // 4 % 2, mine % 2, 2 * ((mine + 1) // 2 % 2)]
        + [order(mic ^ d) for d in range(4)]
    ).astype(jnp.int32)

    def permute(x, pairs):
        return lax.ppermute(x, ("mic", "tm"), pairs)

    def swap(x, mask):
        return permute(x, [(f, f ^ mask) for f in range(groups * blocks)])

    def both(pairs):
        return pairs + [(j, i) for i, j in pairs]

    masks = (0, over_core, over_y, over_core + over_y)

    def sub_block(x, d):
        return lax.dynamic_slice_in_dim(x, order(mic ^ d) * sub, sub, axis=1)

    f, c = [[sub_block(x, d) for d in range(4)] for x in (frames, cotangent)]
    f[2], f[3] = (swap(f[d], masks[d]) for d in (2, 3))
    near_pair = swap(jnp.stack([f[1], c[1]]), masks[1])
    c[2], c[3] = (swap(c[d], masks[d]) for d in (2, 3))
    weights = jnp.stack([w_query, w_key, w_value, w_out])
    edge = shape((groups, count, HALO, width), BF)
    near, side = call(functools.partial(edge_kernel, sub), (edge, edge), [], 8, bits, f[0], near_pair, f[2], f[3])
    near, side, weights = lax.optimization_barrier((near, side, weights))
    near = swap(near, over_core)
    side = permute(
        side,
        both([(blocks + t, 3 * blocks + t) for t in range(blocks)])
        + both([((2 - 2 * (t % 2)) * blocks + t, (2 - 2 * (t % 2)) * blocks + t + 1)
                for t in range(blocks - 1)]),
    )

    factor = 1.0 / math.sqrt(width // HEADS)
    size = width * width // LANES // 8
    span = size + HALO
    unit = 2 * count * cols * sub
    big = pltpu.VMEM((rows, width), BF)
    wide = pltpu.VMEM((rows, width), F32)

    def flat(n):
        return shape((n, LANES), BF)

    moved = shape((groups, count, sub, width), BF)
    placed, conv, acted = call(
        functools.partial(conv_kernel, (groups, count, sub, width)),
        (moved, shape((rows, width), F32), shape((rows, width), BF)),
        [], 8, bits, f[0], near_pair, f[2], f[3], near, side, kernel,
    )
    a_keep, b_keep, a_send, b_send, back_keep, back_send = call(
        functools.partial(main_kernel, (groups, count, sub, width, factor)),
        (flat(8 * span), flat(8 * size)) * 2 + (flat(2 * unit),) * 2,
        [
            pltpu.VMEM((2, rows, width), BF),
            pltpu.VMEM((2, width, rows), BF),
            pltpu.VMEM((4, cuts, groups, count, HALO, width), BF),
            big, big, big, big, wide,
            pltpu.VMEM((32 * cols + HALO, LANES), F32),
        ],
        24, bits, placed, conv, acted, c[0], near_pair, c[2], c[3], near, side, weights,
    )

    lines = [2**i for i in range(1, blocks.bit_length() - 1)]

    def after(x, y):
        return lax.optimization_barrier((x, y))[0]

    def halved(parts, mask):
        n = parts[0].shape[0] // 2
        return [t[:n] for t in parts] + [swap(total(*(t[n:] for t in parts)), mask)]

    def exchanged(parts, masks):
        mine = total(*parts)
        for mask in masks:
            mine = total(mine, swap(mine, mask))
        return mine

    def doubled(x, mask):
        return jnp.concatenate([x, swap(x, mask)])

    a = [a_keep, swap(a_send, over_core)]
    b = [b_keep, swap(b_send, over_core)]
    core_got = swap(back_send, over_core)
    a = halved(a, over_x)
    b = halved(b, lines[0])
    y_got = swap(jnp.concatenate([back_keep[unit:], core_got[unit:]]), over_y)
    y_got = after(y_got, (a[-1], b[-1]))
    edge = flat(count * cols * HALO)
    layer_out, dconv, *edges = call(
        functools.partial(home_kernel, (count, sub, cols)),
        (shape(frames.shape, BF), shape((count, cols, length, LANES), BF), edge, edge),
        [], 8, bits, back_keep, core_got, y_got,
    )
    x_got = swap(jnp.concatenate(edges), over_x)
    n_edge = edge.shape[0]
    passed = lax.dynamic_slice_in_dim(x_got, (1 - tm % 2) * n_edge, n_edge, axis=0)
    a = halved(a, over_y)
    b = halved(b, over_x)
    got = swap(jnp.concatenate([total(*(t[span:] for t in a)), passed]), lines[0])
    a, z_got = [t[:span] for t in a] + [got[:span]], got[span:]
    b = halved(b, lines[1])
    a = exchanged(a, lines[1:])
    b = exchanged(b, [over_y] + lines[2:])
    other_got = permute(
        after(passed, a),
        both([(m * blocks + t, m * blocks + t + 2)
              for m in range(groups) for t in range(2, blocks - 2) if t // 2 % 2]),
    )
    a = doubled(a, lines[0])
    b = doubled(b, lines[1])
    a = doubled(a, over_y)
    b = doubled(after(b, other_got), over_x)

    norm = 1.0 / math.sqrt(groups * count * blocks * length)
    square = shape((width, width), F32)

    def final(kinds, parts, grads, taps=()):
        first = 1 + len(parts) + len(taps)
        scratch = [
            pltpu.VMEM((4 * len(kinds), size, LANES), F32),
            pltpu.SemaphoreType.DMA((4 * len(kinds),)),
        ]
        return call(
            functools.partial(final_kernel, (kinds, not grads, bool(taps), width, norm)),
            (square,) * 4 + (shape((31, width), F32),) * bool(taps),
            scratch + [pltpu.VMEM((16, HALO, LANES), F32)] * bool(taps),
            10, bits, *parts, *taps, *grads, hbm=range(first, first + len(grads)),
            hbm_outs=range(4), aliases={first + i: i for i in range(len(grads))},
        )

    a_far, b_far = swap(a, over_x), swap(b, lines[0])
    a_other, b_other = swap(a, over_core), swap(b, over_core)
    (frame_grad,) = call(
        functools.partial(frame_kernel, (count, cols, length)),
        (shape(frames.shape, BF),), [], 8,
        bits, after(dconv, a), x_got, z_got, other_got, cotangent, kernel,
    )
    grads = final(((1, 0, 0), (1, 1, 0), (0, 0, 0), (0, 1, 0)), (a, b, a_other, b_other), ())
    a_far, b_far, frame_grad, *grads = lax.optimization_barrier(
        (a_far, b_far, frame_grad, *grads)
    )
    taps = (a, a_far, a_other)
    a_other, b_other = swap(a_far, over_core), swap(b_far, over_core)
    grads = final(((1, 0, 1), (1, 1, 1)), (a_far, b_far), grads)
    *grads, kernel_grad = final(
        ((0, 0, 1), (0, 1, 1)), (a_other, b_other), grads, (*taps, a_other)
    )
    return (layer_out, frame_grad, kernel_grad, *grads)


def solution(mesh):
    in_specs = (P("mic", "tm", None), P("mic", "tm", None), P(), P(), P(), P(), P())
    out_specs = (P("mic", "tm", None), P("mic", "tm", None), P(), P(), P(), P(), P())
    return jax.shard_map(shards, mesh=mesh, in_specs=in_specs, out_specs=out_specs, check_vma=False)
```

```python
import functools
import math

import jax
import jax.numpy as jnp
from jax import lax
from jax.experimental import pallas as pl
from jax.experimental.pallas import tpu as pltpu
from jax.sharding import PartitionSpec as P

HEADS = 8
LANES = 128
HALO = 16
NT = (((1,), (1,)), ((), ()))
TN = (((0,), (0,)), ((), ()))
BF = jnp.bfloat16
F32 = jnp.float32
MIB = 1024 * 1024
CORE, Y, X, Z, ZZ, ODD, SKIP, BLOCK_AT = range(8)


def mm(left, right, dims=(((1,), (0,)), ((), ()))):
    return lax.dot_general(left, right, dims, preferred_element_type=F32)


def rolled(x, shift):
    return x if shift == 0 else pltpu.roll(x, x.shape[0] - shift, axis=0)


def window(x, taps, rows):
    acc = None
    for r in range(8):
        xr = rolled(x, r)
        for k in range(4):
            o = 8 * k + r
            if o == 0:
                continue
            term = xr[8 * k : 8 * k + rows] * taps(o)
            acc = term if acc is None else acc + term
    return acc


def ways(bits, half):
    return [bits[i] for i in ((X, Y, Z), (Z, X, ZZ))[half]]


def sigmoid(v):
    return 0.5 * jnp.tanh(0.5 * v) + 0.5


def edge_kernel(sub, bits, f0, f1, f2, f3, near, side):
    odd = bits[ODD]
    for d, f in enumerate((f0, f1, f2, f3)):
        last = sub - HALO
        near[d] = f[:, pl.ds(pl.multiple_of((1 - odd) * last, HALO), HALO), :]
        side[d] = f[:, pl.ds(pl.multiple_of(odd * last, HALO), HALO), :]


def frames_window(bits, frames, near, side, a, m, lanes):
    is_odd = jnp.broadcast_to(bits[ODD], (HALO, LANES)) == 1
    one = near[a ^ 1, m, :, lanes].astype(F32)
    two = side[a ^ bits[SKIP], m, :, lanes].astype(F32)
    return jnp.concatenate(
        [
            jnp.where(is_odd, one, two),
            frames[a, m, :, lanes].astype(F32),
            jnp.where(is_odd, two, one),
        ],
        axis=0,
    )


def conv_kernel(plan, bits, f0, f1, f2, f3, near, side, kern, frames, conv_out, acted_out):
    groups, count, sub, width = plan
    mics = groups * count
    cuts = sub // HALO
    for d, f in enumerate((f0, f1, f2, f3)):
        frames[d] = f[...]

    def conv_step(n, _):
        a, m = n // count, n % count
        for lc in range(width // LANES):
            lanes = slice(lc * LANES, (lc + 1) * LANES)
            x = frames_window(bits, frames, near, side, a, m, lanes)
            conv = window(x, lambda o: kern[o - 1 : o, lanes], sub)
            acted = (conv * sigmoid(conv)).astype(BF)
            for c in range(cuts):
                at = pl.multiple_of((c * mics + n) * HALO, HALO)
                conv_out[pl.ds(at, HALO), lanes] = conv[c * HALO : (c + 1) * HALO]
                acted_out[pl.ds(at, HALO), lanes] = acted[c * HALO : (c + 1) * HALO]
        return 0

    lax.fori_loop(0, mics, conv_step, 0)


def main_kernel(
    plan, bits, frames, conv_in, acted_in, c0, c1, c2, c3, near, side, weights,
    a_keep, b_keep, a_send, b_send, back_keep, back_send,
    left_s, turned_s, right_s, q_s, k_s, v_s, u_s, dconv_s, tap_s,
):
    groups, count, sub, width, factor = plan
    mics = groups * count
    cuts = sub // HALO
    block = mics * HALO
    rows = cuts * block
    cols = width // LANES

    wq, wk, wv, wo = (weights.at[i] for i in range(4))
    left_s[0] = acted_in[...]
    for d, cot in enumerate((c0, c1, c2, c3)):
        for m in range(count):
            for c in range(cuts):
                right_s[3, c, d, m] = cot[m, c * HALO : (c + 1) * HALO, :]

    def flat(i):
        return right_s[i].reshape(rows, width)

    def put(i, c, lanes, x):
        right_s[i, c, :, :, :, lanes] = x.astype(BF).reshape(groups, count, HALO, LANES)

    acted = left_s[0]
    q_s[...] = mm(acted, wq[...]).astype(BF)
    k_s[...] = mm(acted, wk[...]).astype(BF)
    v_s[...] = mm(acted, wv[...]).astype(BF)
    u_s[...] = mm(flat(3), wo[...], NT).astype(BF)
    turned_s[0] = acted.T

    depth = width // HEADS
    per = LANES // depth
    lane = lax.broadcasted_iota(jnp.int32, (block, LANES), 1)
    row_i = lax.broadcasted_iota(jnp.int32, (block, per * block), 0)
    col_i = lax.broadcasted_iota(jnp.int32, (block, per * block), 1)
    same = (row_i % HALO) == (col_i % HALO)

    def by_head(x):
        return jnp.concatenate(
            [jnp.where(lane // depth == h, x, jnp.zeros_like(x)) for h in range(per)], axis=0
        )

    def sums(x):
        return [
            jnp.sum(x[:, h * block : (h + 1) * block], axis=1, keepdims=True) for h in range(per)
        ]

    def each(x, values, op):
        return jnp.concatenate(
            [op(x[:, h * block : (h + 1) * block], values[h]) for h in range(per)], axis=1
        )

    def pick(x):
        out = x[:block]
        for h in range(1, per):
            out = jnp.where(lane // depth == h, x[h * block : (h + 1) * block], out)
        return out

    for c in range(cuts):
        part = slice(c * block, (c + 1) * block)
        for p in range(cols):
            lanes = slice(p * LANES, (p + 1) * LANES)
            q, u = q_s[part, lanes], u_s[part, lanes]
            kc, vc = by_head(k_s[part, lanes]), by_head(v_s[part, lanes])
            e = jnp.where(same, jnp.exp(mm(q, kc, NT) * factor), 0.0)
            w = each(e, [1.0 / x for x in sums(e)], lambda x, s: x * s)
            up = mm(u, vc, NT)
            inner = each(up, sums(w * up), lambda x, s: x - s) * w * factor
            wb, ib = w.astype(BF), inner.astype(BF)
            left_s[1, part, lanes] = mm(wb, vc).astype(BF)
            put(0, c, lanes, mm(ib, kc))
            put(1, c, lanes, pick(mm(ib, q, TN)))
            put(2, c, lanes, pick(mm(wb, u, TN)))

    turned_s[1] = left_s[1].T
    dacted = mm(flat(0), wq[...], NT) + mm(flat(1), wk[...], NT) + mm(flat(2), wv[...], NT)
    conv = conv_in[...]
    sig = sigmoid(conv)
    dconv_s[...] = dacted * sig * (1.0 + conv * (1.0 - sig))

    for lc in range(cols):
        lanes = slice(lc * LANES, (lc + 1) * LANES)

        def tap_step(n, accs):
            a, m = n // count, n % count
            x = frames_window(bits, frames, near, side, a, m, lanes)
            d = jnp.concatenate(
                [
                    dconv_s[pl.ds(pl.multiple_of(c * block + n * HALO, HALO), HALO), lanes]
                    for c in range(cuts)
                ],
                axis=0,
            )
            out = list(accs)
            for r in range(8):
                xr = rolled(x, r)
                for k in range(4):
                    o = 8 * k + r
                    if o == 0:
                        continue
                    prod = xr[8 * k : 8 * k + sub] * d
                    out[o - 1] = out[o - 1] + jnp.sum(prod.reshape(sub // 8, 8, LANES), axis=0)
            return tuple(out)

        accs = lax.fori_loop(0, mics, tap_step, tuple(jnp.zeros((8, LANES), F32) for _ in range(31)))
        tap_s[lc * 32 : lc * 32 + 32, :] = jnp.concatenate(
            [jnp.sum(x, axis=0, keepdims=True) for x in accs] + [jnp.zeros((1, LANES), F32)], axis=0
        )

    tap_s[cols * 32 :, :] = jnp.zeros((HALO, LANES), F32)
    size = cols * width // 8
    core = bits[CORE]
    for out, owner, h in (
        (a_send, 1 - core, 0), (b_send, 1 - core, 1), (a_keep, core, 0), (b_keep, core, 1)
    ):
        i = owner * 2 + h
        span = size + HALO * (1 - h)
        first, second, third = ways(bits, h)
        grad = mm(turned_s[i // 3], flat(i)).astype(BF)
        for piece in range(8):
            cb, at = piece * size // width, piece * size % width
            rel = ((piece // 4) ^ first) * 4 + ((piece // 2 % 2) ^ second) * 2 + ((piece % 2) ^ third)
            start = pl.multiple_of(rel * span, HALO)
            out[pl.ds(start, size), :] = grad[at : at + size, cb * LANES : (cb + 1) * LANES]
            if h == 0:
                tail = tap_s[pl.ds(pl.multiple_of((owner * 8 + piece) * 8, 8), HALO), :]
                out[pl.ds(pl.multiple_of(start + size, HALO), HALO), :] = tail.astype(BF)

    proj = mm(left_s[1], wo[...])
    unit = 2 * count * cols * sub
    for d, (out, base) in enumerate(
        ((back_keep, 0), (back_send, 0), (back_keep, unit), (back_send, unit))
    ):
        for m in range(count):
            for c in range(cuts):
                at = c * block + (d * count + m) * HALO
                part = slice(c * HALO, (c + 1) * HALO)
                layer = (frames[d, m, part, :].astype(F32) + proj[at : at + HALO]).astype(BF)
                dconv = dconv_s[at : at + HALO, :].astype(BF)
                for lc in range(cols):
                    for kind, value in enumerate((layer, dconv)):
                        to = base + ((kind * count + m) * cols + lc) * sub + c * HALO
                        out[to : to + HALO, :] = value[:, lc * LANES : (lc + 1) * LANES]


def total(*parts):
    return functools.reduce(lambda x, y: x + y, [x.astype(F32) for x in parts]).astype(BF)


def final_kernel(plan, bits, *refs):
    kinds, first_call, with_taps, width, norm = plan
    cols = width // LANES
    size = cols * width // 8
    span = size + HALO
    core = bits[CORE]

    def piece_of(h, far, rel):
        first, second, third = ways(bits, h)
        return (first ^ far) * 4 + (second ^ (rel // 2)) * 2 + (third ^ (rel % 2))

    got, refs = refs[: len(kinds)], refs[len(kinds) :]
    if with_taps:
        tap_refs, refs, tap_grad, tap_s = refs[:4], refs[4:-4] + refs[-3:-1], refs[-4], refs[-1]
    *outs, piece_s, sems = refs if first_call else refs[4:]
    copies = []
    for n, (own, h, far) in enumerate(kinds):
        owner = core if own else 1 - core
        for rel in range(4):
            k = 4 * n + rel
            at = rel * (size + HALO * (1 - h))
            piece_s[k] = got[n][at : at + size, :].astype(F32) * norm
            piece = piece_of(h, far, rel)
            cb, at = piece * size // width, piece * size % width
            rows = pl.ds(pl.multiple_of(at, size), size)
            lanes = pl.ds(pl.multiple_of(cb * LANES, LANES), LANES)
            for which in range(2):
                copy = pltpu.make_async_copy(
                    piece_s.at[k], outs[2 * which + h].at[rows, lanes], sems.at[k]
                )
                copies.append((owner == which, copy))
                pl.when(owner == which)(copy.start)
    if with_taps:
        for n, ref in enumerate(tap_refs):
            owner = core if n < 2 else 1 - core
            for rel in range(4):
                at = rel * span + size
                tap_s[owner * 8 + piece_of(0, n % 2, rel)] = ref[at : at + HALO, :].astype(F32) * norm
        for g in range(16):
            lc, j = g // 4, g % 4 * 8
            kept = min(8, 31 - j)
            tap_grad[j : j + kept, lc * LANES : (lc + 1) * LANES] = tap_s[g, 0:kept]
    for here, copy in copies:
        pl.when(here)(copy.wait)


def home_kernel(plan, bits, own, core_got, y_got, layer_out, dconv, first_edge, last_edge):
    count, sub, cols = plan
    unit = 2 * count * cols * sub
    last = 4 * sub - HALO
    for d, (ref, base) in enumerate(
        ((own, 0), (core_got, 0), (y_got, 0), (y_got, unit))
    ):
        to = pl.ds(pl.multiple_of(bits[BLOCK_AT + d] * sub, sub), sub)
        for m in range(count):
            for lc in range(cols):
                at = base + (m * cols + lc) * sub
                layer_out[m, to, lc * LANES : (lc + 1) * LANES] = ref[at : at + sub, :]
                at += count * cols * sub
                dconv[m, lc, to, :] = ref[at : at + sub, :]
    for m in range(count):
        for lc in range(cols):
            at = (m * cols + lc) * HALO
            first_edge[at : at + HALO, :] = dconv[m, lc, :HALO, :]
            last_edge[at : at + HALO, :] = dconv[m, lc, last:, :]


def frame_kernel(plan, bits, dconv, x_got, z_got, other_got, cot, kern, frame_grad):
    count, cols, length = plan
    is_odd = jnp.broadcast_to(bits[X], (HALO, LANES)) == 1
    by_z = jnp.broadcast_to(bits[X] ^ bits[Z], (HALO, LANES)) == 1

    def step(m, _):
        for lc in range(cols):
            lanes = slice(lc * LANES, (lc + 1) * LANES)
            at = (m * cols + lc) * HALO
            rows = pl.ds(pl.multiple_of(at, HALO), HALO)
            x_rows = pl.ds(pl.multiple_of(bits[X] * count * cols * HALO + at, HALO), HALO)
            one = x_got[x_rows, :].astype(F32)
            two = jnp.where(by_z, z_got[rows, :].astype(F32), other_got[rows, :].astype(F32))
            x = jnp.concatenate(
                [
                    jnp.where(is_odd, one, two),
                    dconv[m, lc].astype(F32),
                    jnp.where(is_odd, two, one),
                ],
                axis=0,
            )
            grad = window(x, lambda o: kern[31 - o : 32 - o, lanes], length)
            frame_grad[m, :, lanes] = (cot[m, :, lanes].astype(F32) + grad).astype(BF)
        return 0

    lax.fori_loop(0, count, step, 0)


def call(body, outs, scratch, limit, *args, hbm=(), hbm_outs=(), aliases=None):
    spaces = [pltpu.HBM if i in hbm else pltpu.VMEM for i in range(len(args))]
    return pl.pallas_call(
        body,
        out_shape=outs,
        in_specs=[
            pl.BlockSpec(memory_space=pltpu.SMEM if x.dtype == jnp.int32 else space)
            for x, space in zip(args, spaces)
        ],
        out_specs=tuple(
            pl.BlockSpec(memory_space=pltpu.HBM if i in hbm_outs else pltpu.VMEM)
            for i in range(len(outs))
        ),
        scratch_shapes=scratch,
        input_output_aliases=aliases or {},
        compiler_params=pltpu.CompilerParams(vmem_limit_bytes=limit * MIB),
    )(*args)


def shards(frames, cotangent, kernel, w_query, w_key, w_value, w_out):
    groups, blocks = lax.axis_size("mic"), lax.axis_size("tm")
    count, length, width = frames.shape
    sub = length // groups
    cuts = sub // HALO
    cols = width // LANES
    rows = groups * count * sub
    shape = jax.ShapeDtypeStruct

    mic, tm = lax.axis_index("mic"), lax.axis_index("tm")
    over_core, over_y, over_x, over_z = blocks, 2 * blocks, 1, 2

    def order(a):
        return (a ^ (a >> 1)) ^ (3 * (tm % 2))

    mine = order(mic)
    bits = jnp.stack(
        [mic % 2, mic // 2, tm % 2, tm // 2 % 2, tm // 4 % 2, mine % 2, 2 * ((mine + 1) // 2 % 2)]
        + [order(mic ^ d) for d in range(4)]
    ).astype(jnp.int32)

    def permute(x, pairs):
        return lax.ppermute(x, ("mic", "tm"), pairs)

    def swap(x, mask):
        return permute(x, [(f, f ^ mask) for f in range(groups * blocks)])

    def both(pairs):
        return pairs + [(j, i) for i, j in pairs]

    masks = (0, over_core, over_y, over_core + over_y)

    def sub_block(x, d):
        return lax.dynamic_slice_in_dim(x, order(mic ^ d) * sub, sub, axis=1)

    def scattered(x):
        parts = [sub_block(x, d) for d in range(4)]
        got = {d: swap(parts[d], masks[d]) for d in (2, 3, 1)}
        return [parts[0], got[1], got[2], got[3]]

    f, c = scattered(frames), scattered(cotangent)
    weights = jnp.stack([w_query, w_key, w_value, w_out])
    edge = shape((groups, count, HALO, width), BF)
    near, side = call(functools.partial(edge_kernel, sub), (edge, edge), [], 4, bits, *f)
    near, side, weights = lax.optimization_barrier((near, side, weights))
    near = swap(near, over_core)
    side = permute(
        side,
        both([(blocks + t, 3 * blocks + t) for t in range(blocks)])
        + both([((2 - 2 * (t % 2)) * blocks + t, (2 - 2 * (t % 2)) * blocks + t + 1)
                for t in range(blocks - 1)]),
    )

    factor = 1.0 / math.sqrt(width // HEADS)
    size = width * width // LANES // 8
    span = size + HALO
    unit = 2 * count * cols * sub
    big = pltpu.VMEM((rows, width), BF)
    wide = pltpu.VMEM((rows, width), F32)

    def flat(n):
        return shape((n, LANES), BF)

    moved = shape((groups, count, sub, width), BF)
    placed, conv, acted = call(
        functools.partial(conv_kernel, (groups, count, sub, width)),
        (moved, shape((rows, width), F32), shape((rows, width), BF)),
        [], 4, bits, *f, near, side, kernel,
    )
    a_keep, b_keep, a_send, b_send, back_keep, back_send = call(
        functools.partial(main_kernel, (groups, count, sub, width, factor)),
        (flat(8 * span), flat(8 * size)) * 2 + (flat(2 * unit),) * 2,
        [
            pltpu.VMEM((2, rows, width), BF),
            pltpu.VMEM((2, width, rows), BF),
            pltpu.VMEM((4, cuts, groups, count, HALO, width), BF),
            big, big, big, big, wide,
            pltpu.VMEM((32 * cols + HALO, LANES), F32),
        ],
        14, bits, placed, conv, acted, *c, near, side, weights,
    )

    lines = [2**i for i in range(1, blocks.bit_length() - 1)]

    def after(x, y):
        return lax.optimization_barrier((x, y))[0]

    def halved(parts, mask):
        n = parts[0].shape[0] // 2
        return [t[:n] for t in parts] + [swap(total(*(t[n:] for t in parts)), mask)]

    def exchanged(parts, masks):
        mine = total(*parts)
        for mask in masks:
            mine = total(mine, swap(mine, mask))
        return mine

    def doubled(x, mask):
        return jnp.concatenate([x, swap(x, mask)])

    a = [a_keep, swap(a_send, over_core)]
    b = [b_keep, swap(b_send, over_core)]
    core_got = swap(back_send, over_core)
    a = halved(a, over_x)
    b = halved(b, lines[0])
    y_got = swap(jnp.concatenate([back_keep[unit:], core_got[unit:]]), over_y)
    y_got = after(y_got, a[-1])
    edge = flat(count * cols * HALO)
    layer_out, dconv, *edges = call(
        functools.partial(home_kernel, (count, sub, cols)),
        (shape(frames.shape, BF), shape((count, cols, length, LANES), BF), edge, edge),
        [], 4, bits, back_keep, core_got, y_got,
    )
    x_got = swap(jnp.concatenate(edges), over_x)
    n_edge = edge.shape[0]
    passed = lax.dynamic_slice_in_dim(x_got, (1 - tm % 2) * n_edge, n_edge, axis=0)
    a = halved(a, over_y)
    b = halved(b, over_x)
    got = swap(jnp.concatenate([total(*(t[span:] for t in a)), passed]), lines[0])
    a, z_got = [t[:span] for t in a] + [got[:span]], got[span:]
    b = halved(b, lines[1])
    a = exchanged(a, lines[1:])
    b = exchanged(b, [over_y] + lines[2:])
    other_got = permute(
        after(passed, a),
        both([(m * blocks + t, m * blocks + t + 2)
              for m in range(groups) for t in range(2, blocks - 2) if t // 2 % 2]),
    )
    a = doubled(a, lines[0])
    b = doubled(b, lines[1])
    a = doubled(a, over_y)
    b = doubled(after(b, other_got), over_x)

    norm = 1.0 / math.sqrt(groups * count * blocks * length)
    square = shape((width, width), F32)

    def final(kinds, parts, grads, taps=()):
        first = 1 + len(parts) + len(taps)
        scratch = [
            pltpu.VMEM((4 * len(kinds), size, LANES), F32),
            pltpu.SemaphoreType.DMA((4 * len(kinds),)),
        ]
        return call(
            functools.partial(final_kernel, (kinds, not grads, bool(taps), width, norm)),
            (square,) * 4 + (shape((31, width), F32),) * bool(taps),
            scratch + [pltpu.VMEM((16, HALO, LANES), F32)] * bool(taps),
            5, bits, *parts, *taps, *grads, hbm=range(first, first + len(grads)),
            hbm_outs=range(4), aliases={first + i: i for i in range(len(grads))},
        )

    a_far, b_far = swap(a, over_x), swap(b, lines[0])
    a_other, b_other = swap(a, over_core), swap(b, over_core)
    (frame_grad,) = call(
        functools.partial(frame_kernel, (count, cols, length)),
        (shape(frames.shape, BF),), [], 4,
        bits, after(dconv, a), x_got, z_got, other_got, cotangent, kernel,
    )
    grads = final(((1, 0, 0), (1, 1, 0), (0, 0, 0), (0, 1, 0)), (a, b, a_other, b_other), ())
    a_far, b_far, frame_grad, *grads = lax.optimization_barrier(
        (a_far, b_far, frame_grad, *grads)
    )
    taps = (a, a_far, a_other)
    a_other, b_other = swap(a_far, over_core), swap(b_far, over_core)
    grads = final(((1, 0, 1), (1, 1, 1)), (a_far, b_far), grads)
    *grads, kernel_grad = final(
        ((0, 0, 1), (0, 1, 1)), (a_other, b_other), grads, (*taps, a_other)
    )
    return (layer_out, frame_grad, kernel_grad, *grads)


def solution(mesh):
    in_specs = (P("mic", "tm", None), P("mic", "tm", None), P(), P(), P(), P(), P())
    out_specs = (P("mic", "tm", None), P("mic", "tm", None), P(), P(), P(), P(), P())
    return jax.shard_map(shards, mesh=mesh, in_specs=in_specs, out_specs=out_specs, check_vma=False)
```

```python
import functools
import math

import jax
import jax.numpy as jnp
from jax import lax
from jax.experimental import pallas as pl
from jax.experimental.pallas import tpu as pltpu
from jax.sharding import PartitionSpec as P

HEADS = 8
LANES = 128
HALO = 16
NT = (((1,), (1,)), ((), ()))
TN = (((0,), (0,)), ((), ()))
BF = jnp.bfloat16
F32 = jnp.float32
MIB = 1024 * 1024
CORE, Y, X, Z, ZZ, ODD, SKIP, BLOCK_AT = range(8)


def mm(left, right, dims=(((1,), (0,)), ((), ()))):
    return lax.dot_general(left, right, dims, preferred_element_type=F32)


def rolled(x, shift):
    return x if shift == 0 else pltpu.roll(x, x.shape[0] - shift, axis=0)


def window(x, taps, rows):
    acc = None
    for r in range(8):
        xr = rolled(x, r)
        for k in range(4):
            o = 8 * k + r
            if o == 0:
                continue
            term = xr[8 * k : 8 * k + rows] * taps(o)
            acc = term if acc is None else acc + term
    return acc


def ways(bits, half):
    return [bits[i] for i in ((X, Y, Z), (Z, X, ZZ))[half]]


def sigmoid(v):
    return 0.5 * jnp.tanh(0.5 * v) + 0.5


def edge_kernel(sub, bits, f0, f1, f2, f3, near, side):
    odd = bits[ODD]
    for d, f in enumerate((f0, f1, f2, f3)):
        last = sub - HALO
        near[d] = f[:, pl.ds(pl.multiple_of((1 - odd) * last, HALO), HALO), :]
        side[d] = f[:, pl.ds(pl.multiple_of(odd * last, HALO), HALO), :]


def frames_window(bits, frames, near, side, a, m, lanes):
    is_odd = jnp.broadcast_to(bits[ODD], (HALO, LANES)) == 1
    one = near[a ^ 1, m, :, lanes].astype(F32)
    two = side[a ^ bits[SKIP], m, :, lanes].astype(F32)
    return jnp.concatenate(
        [
            jnp.where(is_odd, one, two),
            frames[a, m, :, lanes].astype(F32),
            jnp.where(is_odd, two, one),
        ],
        axis=0,
    )


def conv_kernel(plan, bits, f0, f1, f2, f3, near, side, kern, frames, conv_out, acted_out):
    groups, count, sub, width = plan
    mics = groups * count
    cuts = sub // HALO
    for d, f in enumerate((f0, f1, f2, f3)):
        frames[d] = f[...]

    def conv_step(n, _):
        a, m = n // count, n % count
        for lc in range(width // LANES):
            lanes = slice(lc * LANES, (lc + 1) * LANES)
            x = frames_window(bits, frames, near, side, a, m, lanes)
            conv = window(x, lambda o: kern[o - 1 : o, lanes], sub)
            acted = (conv * sigmoid(conv)).astype(BF)
            for c in range(cuts):
                at = pl.multiple_of((c * mics + n) * HALO, HALO)
                conv_out[pl.ds(at, HALO), lanes] = conv[c * HALO : (c + 1) * HALO]
                acted_out[pl.ds(at, HALO), lanes] = acted[c * HALO : (c + 1) * HALO]
        return 0

    lax.fori_loop(0, mics, conv_step, 0)


def main_kernel(
    plan, bits, frames, conv_in, acted_in, c0, c1, c2, c3, near, side, weights,
    a_keep, b_keep, a_send, b_send, back_keep, back_send,
    left_s, turned_s, right_s, q_s, k_s, v_s, u_s, dconv_s, tap_s,
):
    groups, count, sub, width, factor = plan
    mics = groups * count
    cuts = sub // HALO
    block = mics * HALO
    rows = cuts * block
    cols = width // LANES

    wq, wk, wv, wo = (weights.at[i] for i in range(4))
    left_s[0] = acted_in[...]
    for d, cot in enumerate((c0, c1, c2, c3)):
        for m in range(count):
            for c in range(cuts):
                right_s[3, c, d, m] = cot[m, c * HALO : (c + 1) * HALO, :]

    def flat(i):
        return right_s[i].reshape(rows, width)

    def put(i, c, lanes, x):
        right_s[i, c, :, :, :, lanes] = x.astype(BF).reshape(groups, count, HALO, LANES)

    acted = left_s[0]
    q_s[...] = mm(acted, wq[...]).astype(BF)
    k_s[...] = mm(acted, wk[...]).astype(BF)
    v_s[...] = mm(acted, wv[...]).astype(BF)
    u_s[...] = mm(flat(3), wo[...], NT).astype(BF)
    turned_s[0] = acted.T

    depth = width // HEADS
    per = LANES // depth
    lane = lax.broadcasted_iota(jnp.int32, (block, LANES), 1)
    row_i = lax.broadcasted_iota(jnp.int32, (block, per * block), 0)
    col_i = lax.broadcasted_iota(jnp.int32, (block, per * block), 1)
    same = (row_i % HALO) == (col_i % HALO)

    def by_head(x):
        return jnp.concatenate(
            [jnp.where(lane // depth == h, x, jnp.zeros_like(x)) for h in range(per)], axis=0
        )

    def sums(x):
        return [
            jnp.sum(x[:, h * block : (h + 1) * block], axis=1, keepdims=True) for h in range(per)
        ]

    def each(x, values, op):
        return jnp.concatenate(
            [op(x[:, h * block : (h + 1) * block], values[h]) for h in range(per)], axis=1
        )

    def pick(x):
        out = x[:block]
        for h in range(1, per):
            out = jnp.where(lane // depth == h, x[h * block : (h + 1) * block], out)
        return out

    for c in range(cuts):
        part = slice(c * block, (c + 1) * block)
        for p in range(cols):
            lanes = slice(p * LANES, (p + 1) * LANES)
            q, u = q_s[part, lanes], u_s[part, lanes]
            kc, vc = by_head(k_s[part, lanes]), by_head(v_s[part, lanes])
            e = jnp.where(same, jnp.exp(mm(q, kc, NT) * factor), 0.0)
            w = each(e, [1.0 / x for x in sums(e)], lambda x, s: x * s)
            up = mm(u, vc, NT)
            inner = each(up, sums(w * up), lambda x, s: x - s) * w * factor
            wb, ib = w.astype(BF), inner.astype(BF)
            left_s[1, part, lanes] = mm(wb, vc).astype(BF)
            put(0, c, lanes, mm(ib, kc))
            put(1, c, lanes, pick(mm(ib, q, TN)))
            put(2, c, lanes, pick(mm(wb, u, TN)))

    turned_s[1] = left_s[1].T
    dacted = mm(flat(0), wq[...], NT) + mm(flat(1), wk[...], NT) + mm(flat(2), wv[...], NT)
    conv = conv_in[...]
    sig = sigmoid(conv)
    dconv_s[...] = dacted * sig * (1.0 + conv * (1.0 - sig))

    for lc in range(cols):
        lanes = slice(lc * LANES, (lc + 1) * LANES)

        def tap_step(n, accs):
            a, m = n // count, n % count
            x = frames_window(bits, frames, near, side, a, m, lanes)
            d = jnp.concatenate(
                [
                    dconv_s[pl.ds(pl.multiple_of(c * block + n * HALO, HALO), HALO), lanes]
                    for c in range(cuts)
                ],
                axis=0,
            )
            out = list(accs)
            for r in range(8):
                xr = rolled(x, r)
                for k in range(4):
                    o = 8 * k + r
                    if o == 0:
                        continue
                    prod = xr[8 * k : 8 * k + sub] * d
                    out[o - 1] = out[o - 1] + jnp.sum(prod.reshape(sub // 8, 8, LANES), axis=0)
            return tuple(out)

        accs = lax.fori_loop(0, mics, tap_step, tuple(jnp.zeros((8, LANES), F32) for _ in range(31)))
        tap_s[lc * 32 : lc * 32 + 32, :] = jnp.concatenate(
            [jnp.sum(x, axis=0, keepdims=True) for x in accs] + [jnp.zeros((1, LANES), F32)], axis=0
        )

    tap_s[cols * 32 :, :] = jnp.zeros((HALO, LANES), F32)
    size = cols * width // 8
    core = bits[CORE]
    for out, owner, h in (
        (a_send, 1 - core, 0), (b_send, 1 - core, 1), (a_keep, core, 0), (b_keep, core, 1)
    ):
        i = owner * 2 + h
        span = size + HALO * (1 - h)
        first, second, third = ways(bits, h)
        grad = mm(turned_s[i // 3], flat(i)).astype(BF)
        for piece in range(8):
            cb, at = piece * size // width, piece * size % width
            rel = ((piece // 4) ^ first) * 4 + ((piece // 2 % 2) ^ second) * 2 + ((piece % 2) ^ third)
            start = pl.multiple_of(rel * span, HALO)
            out[pl.ds(start, size), :] = grad[at : at + size, cb * LANES : (cb + 1) * LANES]
            if h == 0:
                tail = tap_s[pl.ds(pl.multiple_of((owner * 8 + piece) * 8, 8), HALO), :]
                out[pl.ds(pl.multiple_of(start + size, HALO), HALO), :] = tail.astype(BF)

    proj = mm(left_s[1], wo[...])
    unit = 2 * count * cols * sub
    for d, (out, base) in enumerate(
        ((back_keep, 0), (back_send, 0), (back_keep, unit), (back_send, unit))
    ):
        for m in range(count):
            for c in range(cuts):
                at = c * block + (d * count + m) * HALO
                part = slice(c * HALO, (c + 1) * HALO)
                layer = (frames[d, m, part, :].astype(F32) + proj[at : at + HALO]).astype(BF)
                dconv = dconv_s[at : at + HALO, :].astype(BF)
                for lc in range(cols):
                    for kind, value in enumerate((layer, dconv)):
                        to = base + ((kind * count + m) * cols + lc) * sub + c * HALO
                        out[to : to + HALO, :] = value[:, lc * LANES : (lc + 1) * LANES]


def total(*parts):
    return functools.reduce(lambda x, y: x + y, [x.astype(F32) for x in parts]).astype(BF)


def final_kernel(plan, bits, *refs):
    kinds, first_call, with_taps, width, norm = plan
    cols = width // LANES
    size = cols * width // 8
    span = size + HALO
    core = bits[CORE]

    def piece_of(h, far, rel):
        first, second, third = ways(bits, h)
        return (first ^ far) * 4 + (second ^ (rel // 2)) * 2 + (third ^ (rel % 2))

    got, refs = refs[: len(kinds)], refs[len(kinds) :]
    if with_taps:
        tap_refs, refs, tap_grad, tap_s = refs[:4], refs[4:-4] + refs[-3:-1], refs[-4], refs[-1]
    *outs, piece_s, sems = refs if first_call else refs[4:]
    copies = []
    for n, (own, h, far) in enumerate(kinds):
        owner = core if own else 1 - core
        for rel in range(4):
            k = 4 * n + rel
            at = rel * (size + HALO * (1 - h))
            piece_s[k] = got[n][at : at + size, :].astype(F32) * norm
            piece = piece_of(h, far, rel)
            cb, at = piece * size // width, piece * size % width
            rows = pl.ds(pl.multiple_of(at, size), size)
            lanes = pl.ds(pl.multiple_of(cb * LANES, LANES), LANES)
            for which in range(2):
                copy = pltpu.make_async_copy(
                    piece_s.at[k], outs[2 * which + h].at[rows, lanes], sems.at[k]
                )
                copies.append((owner == which, copy))
                pl.when(owner == which)(copy.start)
    if with_taps:
        for n, ref in enumerate(tap_refs):
            owner = core if n < 2 else 1 - core
            for rel in range(4):
                at = rel * span + size
                tap_s[owner * 8 + piece_of(0, n % 2, rel)] = ref[at : at + HALO, :].astype(F32) * norm
        for g in range(16):
            lc, j = g // 4, g % 4 * 8
            kept = min(8, 31 - j)
            tap_grad[j : j + kept, lc * LANES : (lc + 1) * LANES] = tap_s[g, 0:kept]
    for here, copy in copies:
        pl.when(here)(copy.wait)


def home_kernel(plan, bits, own, core_got, y_got, layer_out, dconv, first_edge, last_edge):
    count, sub, cols = plan
    unit = 2 * count * cols * sub
    last = 4 * sub - HALO
    for d, (ref, base) in enumerate(
        ((own, 0), (core_got, 0), (y_got, 0), (y_got, unit))
    ):
        to = pl.ds(pl.multiple_of(bits[BLOCK_AT + d] * sub, sub), sub)
        for m in range(count):
            for lc in range(cols):
                at = base + (m * cols + lc) * sub
                layer_out[m, to, lc * LANES : (lc + 1) * LANES] = ref[at : at + sub, :]
                at += count * cols * sub
                dconv[m, lc, to, :] = ref[at : at + sub, :]
    for m in range(count):
        for lc in range(cols):
            at = (m * cols + lc) * HALO
            first_edge[at : at + HALO, :] = dconv[m, lc, :HALO, :]
            last_edge[at : at + HALO, :] = dconv[m, lc, last:, :]


def frame_kernel(plan, bits, dconv, x_got, z_got, other_got, cot, kern, frame_grad):
    count, cols, length = plan
    is_odd = jnp.broadcast_to(bits[X], (HALO, LANES)) == 1
    by_z = jnp.broadcast_to(bits[X] ^ bits[Z], (HALO, LANES)) == 1

    def step(m, _):
        for lc in range(cols):
            lanes = slice(lc * LANES, (lc + 1) * LANES)
            at = (m * cols + lc) * HALO
            rows = pl.ds(pl.multiple_of(at, HALO), HALO)
            x_rows = pl.ds(pl.multiple_of(bits[X] * count * cols * HALO + at, HALO), HALO)
            one = x_got[x_rows, :].astype(F32)
            two = jnp.where(by_z, z_got[rows, :].astype(F32), other_got[rows, :].astype(F32))
            x = jnp.concatenate(
                [
                    jnp.where(is_odd, one, two),
                    dconv[m, lc].astype(F32),
                    jnp.where(is_odd, two, one),
                ],
                axis=0,
            )
            grad = window(x, lambda o: kern[31 - o : 32 - o, lanes], length)
            frame_grad[m, :, lanes] = (cot[m, :, lanes].astype(F32) + grad).astype(BF)
        return 0

    lax.fori_loop(0, count, step, 0)


def call(body, outs, scratch, limit, *args, hbm=(), hbm_outs=(), aliases=None):
    spaces = [pltpu.HBM if i in hbm else pltpu.VMEM for i in range(len(args))]
    return pl.pallas_call(
        body,
        out_shape=outs,
        in_specs=[
            pl.BlockSpec(memory_space=pltpu.SMEM if x.dtype == jnp.int32 else space)
            for x, space in zip(args, spaces)
        ],
        out_specs=tuple(
            pl.BlockSpec(memory_space=pltpu.HBM if i in hbm_outs else pltpu.VMEM)
            for i in range(len(outs))
        ),
        scratch_shapes=scratch,
        input_output_aliases=aliases or {},
        compiler_params=pltpu.CompilerParams(vmem_limit_bytes=limit * MIB),
    )(*args)


def shards(frames, cotangent, kernel, w_query, w_key, w_value, w_out):
    groups, blocks = lax.axis_size("mic"), lax.axis_size("tm")
    count, length, width = frames.shape
    sub = length // groups
    cuts = sub // HALO
    cols = width // LANES
    rows = groups * count * sub
    shape = jax.ShapeDtypeStruct

    mic, tm = lax.axis_index("mic"), lax.axis_index("tm")
    over_core, over_y, over_x, over_z = blocks, 2 * blocks, 1, 2

    def order(a):
        return (a ^ (a >> 1)) ^ (3 * (tm % 2))

    mine = order(mic)
    bits = jnp.stack(
        [mic % 2, mic // 2, tm % 2, tm // 2 % 2, tm // 4 % 2, mine % 2, 2 * ((mine + 1) // 2 % 2)]
        + [order(mic ^ d) for d in range(4)]
    ).astype(jnp.int32)

    def permute(x, pairs):
        return lax.ppermute(x, ("mic", "tm"), pairs)

    def swap(x, mask):
        return permute(x, [(f, f ^ mask) for f in range(groups * blocks)])

    def both(pairs):
        return pairs + [(j, i) for i, j in pairs]

    masks = (0, over_core, over_y, over_core + over_y)

    def sub_block(x, d):
        return lax.dynamic_slice_in_dim(x, order(mic ^ d) * sub, sub, axis=1)

    def scattered(x):
        parts = [sub_block(x, d) for d in range(4)]
        got = {d: swap(parts[d], masks[d]) for d in (2, 3, 1)}
        return [parts[0], got[1], got[2], got[3]]

    f, c = scattered(frames), scattered(cotangent)
    weights = jnp.stack([w_query, w_key, w_value, w_out])
    edge = shape((groups, count, HALO, width), BF)
    near, side = call(functools.partial(edge_kernel, sub), (edge, edge), [], 8, bits, *f)
    near, side, weights = lax.optimization_barrier((near, side, weights))
    near = swap(near, over_core)
    side = permute(
        side,
        both([(blocks + t, 3 * blocks + t) for t in range(blocks)])
        + both([((2 - 2 * (t % 2)) * blocks + t, (2 - 2 * (t % 2)) * blocks + t + 1)
                for t in range(blocks - 1)]),
    )

    factor = 1.0 / math.sqrt(width // HEADS)
    size = width * width // LANES // 8
    span = size + HALO
    unit = 2 * count * cols * sub
    big = pltpu.VMEM((rows, width), BF)
    wide = pltpu.VMEM((rows, width), F32)

    def flat(n):
        return shape((n, LANES), BF)

    moved = shape((groups, count, sub, width), BF)
    placed, conv, acted = call(
        functools.partial(conv_kernel, (groups, count, sub, width)),
        (moved, shape((rows, width), F32), shape((rows, width), BF)),
        [], 8, bits, *f, near, side, kernel,
    )
    a_keep, b_keep, a_send, b_send, back_keep, back_send = call(
        functools.partial(main_kernel, (groups, count, sub, width, factor)),
        (flat(8 * span), flat(8 * size)) * 2 + (flat(2 * unit),) * 2,
        [
            pltpu.VMEM((2, rows, width), BF),
            pltpu.VMEM((2, width, rows), BF),
            pltpu.VMEM((4, cuts, groups, count, HALO, width), BF),
            big, big, big, big, wide,
            pltpu.VMEM((32 * cols + HALO, LANES), F32),
        ],
        24, bits, placed, conv, acted, *c, near, side, weights,
    )

    lines = [2**i for i in range(1, blocks.bit_length() - 1)]

    def after(x, y):
        return lax.optimization_barrier((x, y))[0]

    def kept(parts, n):
        return lax.optimization_barrier(total(*(t[:n] for t in parts)))

    def halved(parts, mask):
        n = parts[0].shape[0] // 2
        return [kept(parts, n), swap(total(*(t[n:] for t in parts)), mask)]

    def exchanged(parts, masks):
        mine = total(*parts)
        for mask in masks:
            mine = total(mine, swap(mine, mask))
        return mine

    def doubled(x, mask):
        return jnp.concatenate([x, swap(x, mask)])

    a = [a_keep, swap(a_send, over_core)]
    b = [b_keep, swap(b_send, over_core)]
    core_got = swap(back_send, over_core)
    a = halved(a, over_x)
    b = halved(b, lines[0])
    y_got = swap(jnp.concatenate([back_keep[unit:], core_got[unit:]]), over_y)
    y_got = after(y_got, b[-1])
    edge = flat(count * cols * HALO)
    layer_out, dconv, *edges = call(
        functools.partial(home_kernel, (count, sub, cols)),
        (shape(frames.shape, BF), shape((count, cols, length, LANES), BF), edge, edge),
        [], 8, bits, back_keep, core_got, y_got,
    )
    x_got = swap(jnp.concatenate(edges), over_x)
    n_edge = edge.shape[0]
    passed = lax.dynamic_slice_in_dim(x_got, (1 - tm % 2) * n_edge, n_edge, axis=0)
    a = halved(a, over_y)
    b = halved(b, over_x)
    got = swap(jnp.concatenate([total(*(t[span:] for t in a)), passed]), lines[0])
    a, z_got = [kept(a, span), got[:span]], got[span:]
    b = halved(b, lines[1])
    a = exchanged(a, lines[1:])
    b = exchanged(b, [over_y] + lines[2:])
    other_got = permute(
        after(passed, a),
        both([(m * blocks + t, m * blocks + t + 2)
              for m in range(groups) for t in range(2, blocks - 2) if t // 2 % 2]),
    )
    a = doubled(a, lines[0])
    b = doubled(b, lines[1])
    a = doubled(a, over_y)
    b = doubled(after(b, other_got), over_x)

    norm = 1.0 / math.sqrt(groups * count * blocks * length)
    square = shape((width, width), F32)

    def final(kinds, parts, grads, taps=()):
        first = 1 + len(parts) + len(taps)
        scratch = [
            pltpu.VMEM((4 * len(kinds), size, LANES), F32),
            pltpu.SemaphoreType.DMA((4 * len(kinds),)),
        ]
        return call(
            functools.partial(final_kernel, (kinds, not grads, bool(taps), width, norm)),
            (square,) * 4 + (shape((31, width), F32),) * bool(taps),
            scratch + [pltpu.VMEM((16, HALO, LANES), F32)] * bool(taps),
            10, bits, *parts, *taps, *grads, hbm=range(first, first + len(grads)),
            hbm_outs=range(4), aliases={first + i: i for i in range(len(grads))},
        )

    a_far, b_far = swap(a, over_x), swap(b, lines[0])
    a_other, b_other = swap(a, over_core), swap(b, over_core)
    (frame_grad,) = call(
        functools.partial(frame_kernel, (count, cols, length)),
        (shape(frames.shape, BF),), [], 8,
        bits, after(dconv, a), x_got, z_got, other_got, cotangent, kernel,
    )
    grads = final(((1, 0, 0), (1, 1, 0), (0, 0, 0), (0, 1, 0)), (a, b, a_other, b_other), ())
    a_far, b_far, frame_grad, *grads = lax.optimization_barrier(
        (a_far, b_far, frame_grad, *grads)
    )
    taps = (a, a_far, a_other)
    a_other, b_other = swap(a_far, over_core), swap(b_far, over_core)
    grads = final(((1, 0, 1), (1, 1, 1)), (a_far, b_far), grads)
    *grads, kernel_grad = final(
        ((0, 0, 1), (0, 1, 1)), (a_other, b_other), grads, (*taps, a_other)
    )
    return (layer_out, frame_grad, kernel_grad, *grads)


def solution(mesh):
    in_specs = (P("mic", "tm", None), P("mic", "tm", None), P(), P(), P(), P(), P())
    out_specs = (P("mic", "tm", None), P("mic", "tm", None), P(), P(), P(), P(), P())
    return jax.shard_map(shards, mesh=mesh, in_specs=in_specs, out_specs=out_specs, check_vma=False)
```

```python
import functools
import math

import jax
import jax.numpy as jnp
from jax import lax
from jax.experimental import pallas as pl
from jax.experimental.pallas import tpu as pltpu
from jax.sharding import PartitionSpec as P

HEADS = 8
LANES = 128
HALO = 16
NT = (((1,), (1,)), ((), ()))
TN = (((0,), (0,)), ((), ()))
BF = jnp.bfloat16
F32 = jnp.float32
MIB = 1024 * 1024
CORE, Y, X, Z, ZZ, ODD, SKIP, BLOCK_AT = range(8)


def mm(left, right, dims=(((1,), (0,)), ((), ()))):
    return lax.dot_general(left, right, dims, preferred_element_type=F32)


def rolled(x, shift):
    return x if shift == 0 else pltpu.roll(x, x.shape[0] - shift, axis=0)


def window(x, taps, rows):
    acc = None
    for r in range(8):
        xr = rolled(x, r)
        for k in range(4):
            o = 8 * k + r
            if o == 0:
                continue
            term = xr[8 * k : 8 * k + rows] * taps(o)
            acc = term if acc is None else acc + term
    return acc


def ways(bits, half):
    return [bits[i] for i in ((X, Y, Z), (Z, X, ZZ))[half]]


def sigmoid(v):
    return 0.5 * jnp.tanh(0.5 * v) + 0.5


def edge_kernel(sub, bits, f0, f1, f2, f3, near, side):
    odd = bits[ODD]
    for d, f in enumerate((f0, f1, f2, f3)):
        last = sub - HALO
        near[d] = f[:, pl.ds(pl.multiple_of((1 - odd) * last, HALO), HALO), :]
        side[d] = f[:, pl.ds(pl.multiple_of(odd * last, HALO), HALO), :]


def frames_window(bits, frames, near, side, a, m, lanes):
    is_odd = jnp.broadcast_to(bits[ODD], (HALO, LANES)) == 1
    one = near[a ^ 1, m, :, lanes].astype(F32)
    two = side[a ^ bits[SKIP], m, :, lanes].astype(F32)
    return jnp.concatenate(
        [
            jnp.where(is_odd, one, two),
            frames[a, m, :, lanes].astype(F32),
            jnp.where(is_odd, two, one),
        ],
        axis=0,
    )


def conv_kernel(plan, bits, f0, f1, f2, f3, near, side, kern, frames, conv_out, acted_out):
    groups, count, sub, width = plan
    mics = groups * count
    cuts = sub // HALO
    for d, f in enumerate((f0, f1, f2, f3)):
        frames[d] = f[...]

    def conv_step(n, _):
        a, m = n // count, n % count
        for lc in range(width // LANES):
            lanes = slice(lc * LANES, (lc + 1) * LANES)
            x = frames_window(bits, frames, near, side, a, m, lanes)
            conv = window(x, lambda o: kern[o - 1 : o, lanes], sub)
            acted = (conv * sigmoid(conv)).astype(BF)
            for c in range(cuts):
                at = pl.multiple_of((c * mics + n) * HALO, HALO)
                conv_out[pl.ds(at, HALO), lanes] = conv[c * HALO : (c + 1) * HALO]
                acted_out[pl.ds(at, HALO), lanes] = acted[c * HALO : (c + 1) * HALO]
        return 0

    lax.fori_loop(0, mics, conv_step, 0)


def main_kernel(
    plan, bits, frames, conv_in, acted_in, c0, c1, c2, c3, weights,
    a_keep, b_keep, a_send, b_send, back_keep, back_send, dconv_s,
    left_s, turned_s, right_s, q_s, k_s, v_s, u_s,
):
    groups, count, sub, width, factor = plan
    mics = groups * count
    cuts = sub // HALO
    block = mics * HALO
    rows = cuts * block
    cols = width // LANES

    wq, wk, wv, wo = (weights.at[i] for i in range(4))
    left_s[0] = acted_in[...]
    for d, cot in enumerate((c0, c1, c2, c3)):
        for m in range(count):
            for c in range(cuts):
                right_s[3, c, d, m] = cot[m, c * HALO : (c + 1) * HALO, :]

    def flat(i):
        return right_s[i].reshape(rows, width)

    def put(i, c, lanes, x):
        right_s[i, c, :, :, :, lanes] = x.astype(BF).reshape(groups, count, HALO, LANES)

    acted = left_s[0]
    q_s[...] = mm(acted, wq[...]).astype(BF)
    k_s[...] = mm(acted, wk[...]).astype(BF)
    v_s[...] = mm(acted, wv[...]).astype(BF)
    u_s[...] = mm(flat(3), wo[...], NT).astype(BF)
    turned_s[0] = acted.T

    depth = width // HEADS
    per = LANES // depth
    lane = lax.broadcasted_iota(jnp.int32, (block, LANES), 1)
    row_i = lax.broadcasted_iota(jnp.int32, (block, per * block), 0)
    col_i = lax.broadcasted_iota(jnp.int32, (block, per * block), 1)
    same = (row_i % HALO) == (col_i % HALO)

    def by_head(x):
        return jnp.concatenate(
            [jnp.where(lane // depth == h, x, jnp.zeros_like(x)) for h in range(per)], axis=0
        )

    def sums(x):
        return [
            jnp.sum(x[:, h * block : (h + 1) * block], axis=1, keepdims=True) for h in range(per)
        ]

    def each(x, values, op):
        return jnp.concatenate(
            [op(x[:, h * block : (h + 1) * block], values[h]) for h in range(per)], axis=1
        )

    def pick(x):
        out = x[:block]
        for h in range(1, per):
            out = jnp.where(lane // depth == h, x[h * block : (h + 1) * block], out)
        return out

    for c in range(cuts):
        part = slice(c * block, (c + 1) * block)
        for p in range(cols):
            lanes = slice(p * LANES, (p + 1) * LANES)
            q, u = q_s[part, lanes], u_s[part, lanes]
            kc, vc = by_head(k_s[part, lanes]), by_head(v_s[part, lanes])
            e = jnp.where(same, jnp.exp(mm(q, kc, NT) * factor), 0.0)
            w = each(e, [1.0 / x for x in sums(e)], lambda x, s: x * s)
            up = mm(u, vc, NT)
            inner = each(up, sums(w * up), lambda x, s: x - s) * w * factor
            wb, ib = w.astype(BF), inner.astype(BF)
            left_s[1, part, lanes] = mm(wb, vc).astype(BF)
            put(0, c, lanes, mm(ib, kc))
            put(1, c, lanes, pick(mm(ib, q, TN)))
            put(2, c, lanes, pick(mm(wb, u, TN)))

    turned_s[1] = left_s[1].T
    dacted = mm(flat(0), wq[...], NT) + mm(flat(1), wk[...], NT) + mm(flat(2), wv[...], NT)
    conv = conv_in[...]
    sig = sigmoid(conv)
    dconv_s[...] = dacted * sig * (1.0 + conv * (1.0 - sig))

    size = cols * width // 8
    core = bits[CORE]
    for out, owner, h in (
        (a_send, 1 - core, 0), (b_send, 1 - core, 1), (a_keep, core, 0), (b_keep, core, 1)
    ):
        i = owner * 2 + h
        span = size + HALO * (1 - h)
        first, second, third = ways(bits, h)
        grad = mm(turned_s[i // 3], flat(i)).astype(BF)
        for piece in range(8):
            cb, at = piece * size // width, piece * size % width
            rel = ((piece // 4) ^ first) * 4 + ((piece // 2 % 2) ^ second) * 2 + ((piece % 2) ^ third)
            start = pl.multiple_of(rel * span, HALO)
            out[pl.ds(start, size), :] = grad[at : at + size, cb * LANES : (cb + 1) * LANES]
            if h == 0:
                out[pl.ds(pl.multiple_of(start + size, HALO), HALO), :] = jnp.zeros(
                    (HALO, LANES), BF
                )

    proj = mm(left_s[1], wo[...])
    unit = 2 * count * cols * sub
    for d, (out, base) in enumerate(
        ((back_keep, 0), (back_send, 0), (back_keep, unit), (back_send, unit))
    ):
        for m in range(count):
            for c in range(cuts):
                at = c * block + (d * count + m) * HALO
                part = slice(c * HALO, (c + 1) * HALO)
                layer = (frames[d, m, part, :].astype(F32) + proj[at : at + HALO]).astype(BF)
                dconv = dconv_s[at : at + HALO, :].astype(BF)
                for lc in range(cols):
                    for kind, value in enumerate((layer, dconv)):
                        to = base + ((kind * count + m) * cols + lc) * sub + c * HALO
                        out[to : to + HALO, :] = value[:, lc * LANES : (lc + 1) * LANES]


def tap_kernel(plan, bits, frames, near, side, dconv_s, keep_in, send_in, keep, send, tap_s):
    groups, count, sub, width = plan
    mics = groups * count
    cuts = sub // HALO
    block = mics * HALO
    cols = width // LANES
    keep[...] = keep_in[...]
    send[...] = send_in[...]
    for lc in range(cols):
        lanes = slice(lc * LANES, (lc + 1) * LANES)

        def tap_step(n, accs):
            a, m = n // count, n % count
            x = frames_window(bits, frames, near, side, a, m, lanes)
            d = jnp.concatenate(
                [
                    dconv_s[pl.ds(pl.multiple_of(c * block + n * HALO, HALO), HALO), lanes]
                    for c in range(cuts)
                ],
                axis=0,
            )
            out = list(accs)
            for r in range(8):
                xr = rolled(x, r)
                for k in range(4):
                    o = 8 * k + r
                    if o == 0:
                        continue
                    prod = xr[8 * k : 8 * k + sub] * d
                    out[o - 1] = out[o - 1] + jnp.sum(prod.reshape(sub // 8, 8, LANES), axis=0)
            return tuple(out)

        accs = lax.fori_loop(0, mics, tap_step, tuple(jnp.zeros((8, LANES), F32) for _ in range(31)))
        tap_s[lc * 32 : lc * 32 + 32, :] = jnp.concatenate(
            [jnp.sum(x, axis=0, keepdims=True) for x in accs] + [jnp.zeros((1, LANES), F32)], axis=0
        )

    tap_s[cols * 32 :, :] = jnp.zeros((HALO, LANES), F32)
    size = cols * width // 8
    span = size + HALO
    core = bits[CORE]
    first, second, third = ways(bits, 0)
    for out, owner in ((send, 1 - core), (keep, core)):
        for piece in range(8):
            rel = ((piece // 4) ^ first) * 4 + ((piece // 2 % 2) ^ second) * 2 + ((piece % 2) ^ third)
            tail = tap_s[pl.ds(pl.multiple_of((owner * 8 + piece) * 8, 8), HALO), :]
            at = pl.multiple_of(rel * span + size, HALO)
            out[pl.ds(at, HALO), :] = tail.astype(BF)


def total(*parts):
    return functools.reduce(lambda x, y: x + y, [x.astype(F32) for x in parts]).astype(BF)


def final_kernel(plan, bits, *refs):
    kinds, first_call, with_taps, width, norm = plan
    cols = width // LANES
    size = cols * width // 8
    span = size + HALO
    core = bits[CORE]

    def piece_of(h, far, rel):
        first, second, third = ways(bits, h)
        return (first ^ far) * 4 + (second ^ (rel // 2)) * 2 + (third ^ (rel % 2))

    got, refs = refs[: len(kinds)], refs[len(kinds) :]
    if with_taps:
        tap_refs, refs, tap_grad, tap_s = refs[:4], refs[4:-4] + refs[-3:-1], refs[-4], refs[-1]
    *outs, piece_s, sems = refs if first_call else refs[4:]
    copies = []
    for n, (own, h, far) in enumerate(kinds):
        owner = core if own else 1 - core
        for rel in range(4):
            k = 4 * n + rel
            at = rel * (size + HALO * (1 - h))
            piece_s[k] = got[n][at : at + size, :].astype(F32) * norm
            piece = piece_of(h, far, rel)
            cb, at = piece * size // width, piece * size % width
            rows = pl.ds(pl.multiple_of(at, size), size)
            lanes = pl.ds(pl.multiple_of(cb * LANES, LANES), LANES)
            for which in range(2):
                copy = pltpu.make_async_copy(
                    piece_s.at[k], outs[2 * which + h].at[rows, lanes], sems.at[k]
                )
                copies.append((owner == which, copy))
                pl.when(owner == which)(copy.start)
    if with_taps:
        for n, ref in enumerate(tap_refs):
            owner = core if n < 2 else 1 - core
            for rel in range(4):
                at = rel * span + size
                tap_s[owner * 8 + piece_of(0, n % 2, rel)] = ref[at : at + HALO, :].astype(F32) * norm
        for g in range(16):
            lc, j = g // 4, g % 4 * 8
            kept = min(8, 31 - j)
            tap_grad[j : j + kept, lc * LANES : (lc + 1) * LANES] = tap_s[g, 0:kept]
    for here, copy in copies:
        pl.when(here)(copy.wait)


def home_kernel(plan, bits, own, core_got, y_got, layer_out, dconv, first_edge, last_edge):
    count, sub, cols = plan
    unit = 2 * count * cols * sub
    last = 4 * sub - HALO
    for d, (ref, base) in enumerate(
        ((own, 0), (core_got, 0), (y_got, 0), (y_got, unit))
    ):
        to = pl.ds(pl.multiple_of(bits[BLOCK_AT + d] * sub, sub), sub)
        for m in range(count):
            for lc in range(cols):
                at = base + (m * cols + lc) * sub
                layer_out[m, to, lc * LANES : (lc + 1) * LANES] = ref[at : at + sub, :]
                at += count * cols * sub
                dconv[m, lc, to, :] = ref[at : at + sub, :]
    for m in range(count):
        for lc in range(cols):
            at = (m * cols + lc) * HALO
            first_edge[at : at + HALO, :] = dconv[m, lc, :HALO, :]
            last_edge[at : at + HALO, :] = dconv[m, lc, last:, :]


def frame_kernel(plan, bits, dconv, x_got, z_got, other_got, cot, kern, frame_grad):
    count, cols, length = plan
    is_odd = jnp.broadcast_to(bits[X], (HALO, LANES)) == 1
    by_z = jnp.broadcast_to(bits[X] ^ bits[Z], (HALO, LANES)) == 1

    def step(m, _):
        for lc in range(cols):
            lanes = slice(lc * LANES, (lc + 1) * LANES)
            at = (m * cols + lc) * HALO
            rows = pl.ds(pl.multiple_of(at, HALO), HALO)
            x_rows = pl.ds(pl.multiple_of(bits[X] * count * cols * HALO + at, HALO), HALO)
            one = x_got[x_rows, :].astype(F32)
            two = jnp.where(by_z, z_got[rows, :].astype(F32), other_got[rows, :].astype(F32))
            x = jnp.concatenate(
                [
                    jnp.where(is_odd, one, two),
                    dconv[m, lc].astype(F32),
                    jnp.where(is_odd, two, one),
                ],
                axis=0,
            )
            grad = window(x, lambda o: kern[31 - o : 32 - o, lanes], length)
            frame_grad[m, :, lanes] = (cot[m, :, lanes].astype(F32) + grad).astype(BF)
        return 0

    lax.fori_loop(0, count, step, 0)


def call(body, outs, scratch, limit, *args, hbm=(), hbm_outs=(), aliases=None):
    spaces = [pltpu.HBM if i in hbm else pltpu.VMEM for i in range(len(args))]
    return pl.pallas_call(
        body,
        out_shape=outs,
        in_specs=[
            pl.BlockSpec(memory_space=pltpu.SMEM if x.dtype == jnp.int32 else space)
            for x, space in zip(args, spaces)
        ],
        out_specs=tuple(
            pl.BlockSpec(memory_space=pltpu.HBM if i in hbm_outs else pltpu.VMEM)
            for i in range(len(outs))
        ),
        scratch_shapes=scratch,
        input_output_aliases=aliases or {},
        compiler_params=pltpu.CompilerParams(vmem_limit_bytes=limit * MIB),
    )(*args)


def shards(frames, cotangent, kernel, w_query, w_key, w_value, w_out):
    groups, blocks = lax.axis_size("mic"), lax.axis_size("tm")
    count, length, width = frames.shape
    sub = length // groups
    cuts = sub // HALO
    cols = width // LANES
    rows = groups * count * sub
    shape = jax.ShapeDtypeStruct

    mic, tm = lax.axis_index("mic"), lax.axis_index("tm")
    over_core, over_y, over_x, over_z = blocks, 2 * blocks, 1, 2

    def order(a):
        return (a ^ (a >> 1)) ^ (3 * (tm % 2))

    mine = order(mic)
    bits = jnp.stack(
        [mic % 2, mic // 2, tm % 2, tm // 2 % 2, tm // 4 % 2, mine % 2, 2 * ((mine + 1) // 2 % 2)]
        + [order(mic ^ d) for d in range(4)]
    ).astype(jnp.int32)

    def permute(x, pairs):
        return lax.ppermute(x, ("mic", "tm"), pairs)

    def swap(x, mask):
        return permute(x, [(f, f ^ mask) for f in range(groups * blocks)])

    def both(pairs):
        return pairs + [(j, i) for i, j in pairs]

    masks = (0, over_core, over_y, over_core + over_y)

    def sub_block(x, d):
        return lax.dynamic_slice_in_dim(x, order(mic ^ d) * sub, sub, axis=1)

    def scattered(x):
        parts = [sub_block(x, d) for d in range(4)]
        got = {d: swap(parts[d], masks[d]) for d in (2, 3, 1)}
        return [parts[0], got[1], got[2], got[3]]

    f, c = scattered(frames), scattered(cotangent)
    weights = jnp.stack([w_query, w_key, w_value, w_out])
    edge = shape((groups, count, HALO, width), BF)
    near, side = call(functools.partial(edge_kernel, sub), (edge, edge), [], 8, bits, *f)
    near, side, weights = lax.optimization_barrier((near, side, weights))
    near = swap(near, over_core)
    side = permute(
        side,
        both([(blocks + t, 3 * blocks + t) for t in range(blocks)])
        + both([((2 - 2 * (t % 2)) * blocks + t, (2 - 2 * (t % 2)) * blocks + t + 1)
                for t in range(blocks - 1)]),
    )

    factor = 1.0 / math.sqrt(width // HEADS)
    size = width * width // LANES // 8
    span = size + HALO
    unit = 2 * count * cols * sub
    big = pltpu.VMEM((rows, width), BF)
    wide = pltpu.VMEM((rows, width), F32)

    def flat(n):
        return shape((n, LANES), BF)

    moved = shape((groups, count, sub, width), BF)
    placed, conv, acted = call(
        functools.partial(conv_kernel, (groups, count, sub, width)),
        (moved, shape((rows, width), F32), shape((rows, width), BF)),
        [], 8, bits, *f, near, side, kernel,
    )
    a_keep, b_keep, a_send, b_send, back_keep, back_send, dconv_here = call(
        functools.partial(main_kernel, (groups, count, sub, width, factor)),
        (flat(8 * span), flat(8 * size)) * 2 + (flat(2 * unit),) * 2 + (shape((rows, width), F32),),
        [
            pltpu.VMEM((2, rows, width), BF),
            pltpu.VMEM((2, width, rows), BF),
            pltpu.VMEM((4, cuts, groups, count, HALO, width), BF),
            big, big, big, big,
        ],
        24, bits, placed, conv, acted, *c, weights,
    )
    a_keep, a_send = call(
        functools.partial(tap_kernel, (groups, count, sub, width)), (flat(8 * span),) * 2,
        [pltpu.VMEM((32 * cols + HALO, LANES), F32)],
        8, bits, placed, near, side, dconv_here, a_keep, a_send,
    )

    lines = [2**i for i in range(1, blocks.bit_length() - 1)]

    def after(x, y):
        return lax.optimization_barrier((x, y))[0]

    def kept(parts, n):
        return lax.optimization_barrier(total(*(t[:n] for t in parts)))

    def halved(parts, mask):
        n = parts[0].shape[0] // 2
        return [kept(parts, n), swap(total(*(t[n:] for t in parts)), mask)]

    def exchanged(parts, masks):
        mine = total(*parts)
        for mask in masks:
            mine = total(mine, swap(mine, mask))
        return mine

    def doubled(x, mask):
        return jnp.concatenate([x, swap(x, mask)])

    a = [a_keep, swap(a_send, over_core)]
    b = [b_keep, swap(b_send, over_core)]
    core_got = swap(back_send, over_core)
    a = halved(a, over_x)
    b = halved(b, lines[0])
    y_got = swap(jnp.concatenate([back_keep[unit:], core_got[unit:]]), over_y)
    y_got = after(y_got, b[-1])
    edge = flat(count * cols * HALO)
    layer_out, dconv, *edges = call(
        functools.partial(home_kernel, (count, sub, cols)),
        (shape(frames.shape, BF), shape((count, cols, length, LANES), BF), edge, edge),
        [], 8, bits, back_keep, core_got, y_got,
    )
    x_got = swap(jnp.concatenate(edges), over_x)
    n_edge = edge.shape[0]
    passed = lax.dynamic_slice_in_dim(x_got, (1 - tm % 2) * n_edge, n_edge, axis=0)
    a = halved(a, over_y)
    b = halved(b, over_x)
    got = swap(jnp.concatenate([total(*(t[span:] for t in a)), passed]), lines[0])
    a, z_got = [kept(a, span), got[:span]], got[span:]
    b = halved(b, lines[1])
    a = exchanged(a, lines[1:])
    b = exchanged(b, [over_y] + lines[2:])
    other_got = permute(
        after(passed, a),
        both([(m * blocks + t, m * blocks + t + 2)
              for m in range(groups) for t in range(2, blocks - 2) if t // 2 % 2]),
    )
    a = doubled(a, lines[0])
    b = doubled(b, lines[1])
    a = doubled(a, over_y)
    b = doubled(after(b, other_got), over_x)

    norm = 1.0 / math.sqrt(groups * count * blocks * length)
    square = shape((width, width), F32)

    def final(kinds, parts, grads, taps=()):
        first = 1 + len(parts) + len(taps)
        scratch = [
            pltpu.VMEM((4 * len(kinds), size, LANES), F32),
            pltpu.SemaphoreType.DMA((4 * len(kinds),)),
        ]
        return call(
            functools.partial(final_kernel, (kinds, not grads, bool(taps), width, norm)),
            (square,) * 4 + (shape((31, width), F32),) * bool(taps),
            scratch + [pltpu.VMEM((16, HALO, LANES), F32)] * bool(taps),
            10, bits, *parts, *taps, *grads, hbm=range(first, first + len(grads)),
            hbm_outs=range(4), aliases={first + i: i for i in range(len(grads))},
        )

    a_far, b_far = swap(a, over_x), swap(b, lines[0])
    a_other, b_other = swap(a, over_core), swap(b, over_core)
    (frame_grad,) = call(
        functools.partial(frame_kernel, (count, cols, length)),
        (shape(frames.shape, BF),), [], 8,
        bits, after(dconv, a), x_got, z_got, other_got, cotangent, kernel,
    )
    grads = final(((1, 0, 0), (1, 1, 0), (0, 0, 0), (0, 1, 0)), (a, b, a_other, b_other), ())
    a_far, b_far, frame_grad, *grads = lax.optimization_barrier(
        (a_far, b_far, frame_grad, *grads)
    )
    taps = (a, a_far, a_other)
    a_other, b_other = swap(a_far, over_core), swap(b_far, over_core)
    grads = final(((1, 0, 1), (1, 1, 1)), (a_far, b_far), grads)
    *grads, kernel_grad = final(
        ((0, 0, 1), (0, 1, 1)), (a_other, b_other), grads, (*taps, a_other)
    )
    return (layer_out, frame_grad, kernel_grad, *grads)


def solution(mesh):
    in_specs = (P("mic", "tm", None), P("mic", "tm", None), P(), P(), P(), P(), P())
    out_specs = (P("mic", "tm", None), P("mic", "tm", None), P(), P(), P(), P(), P())
    return jax.shard_map(shards, mesh=mesh, in_specs=in_specs, out_specs=out_specs, check_vma=False)
```

```python
import functools
import math

import jax
import jax.numpy as jnp
from jax import lax
from jax.experimental import pallas as pl
from jax.experimental.pallas import tpu as pltpu
from jax.sharding import PartitionSpec as P

HEADS = 8
LANES = 128
HALO = 16
NT = (((1,), (1,)), ((), ()))
TN = (((0,), (0,)), ((), ()))
BF = jnp.bfloat16
F32 = jnp.float32
MIB = 1024 * 1024
CORE, Y, X, Z, ZZ, ODD, SKIP, BLOCK_AT = range(8)


def mm(left, right, dims=(((1,), (0,)), ((), ()))):
    return lax.dot_general(left, right, dims, preferred_element_type=F32)


def rolled(x, shift):
    return x if shift == 0 else pltpu.roll(x, x.shape[0] - shift, axis=0)


def window(x, taps, rows):
    acc = None
    for r in range(8):
        xr = rolled(x, r)
        for k in range(4):
            o = 8 * k + r
            if o == 0:
                continue
            term = xr[8 * k : 8 * k + rows] * taps(o)
            acc = term if acc is None else acc + term
    return acc


def ways(bits, half):
    return [bits[i] for i in ((X, Y, Z), (Z, X, ZZ))[half]]


def sigmoid(v):
    return 0.5 * jnp.tanh(0.5 * v) + 0.5


def edge_kernel(sub, bits, f0, f1, f2, f3, near, side):
    odd = bits[ODD]
    for d, f in enumerate((f0, f1, f2, f3)):
        last = sub - HALO
        near[d] = f[:, pl.ds(pl.multiple_of((1 - odd) * last, HALO), HALO), :]
        side[d] = f[:, pl.ds(pl.multiple_of(odd * last, HALO), HALO), :]


def frames_window(bits, frames, near, side, a, m, lanes):
    is_odd = jnp.broadcast_to(bits[ODD], (HALO, LANES)) == 1
    one = near[a ^ 1, m, :, lanes].astype(F32)
    two = side[a ^ bits[SKIP], m, :, lanes].astype(F32)
    return jnp.concatenate(
        [
            jnp.where(is_odd, one, two),
            frames[a, m, :, lanes].astype(F32),
            jnp.where(is_odd, two, one),
        ],
        axis=0,
    )


def conv_kernel(plan, bits, f0, f1, f2, f3, near, side, kern, frames, conv_out, acted_out):
    groups, count, sub, width = plan
    mics = groups * count
    cuts = sub // HALO
    for d, f in enumerate((f0, f1, f2, f3)):
        frames[d] = f[...]

    def conv_step(n, _):
        a, m = n // count, n % count
        for lc in range(width // LANES):
            lanes = slice(lc * LANES, (lc + 1) * LANES)
            x = frames_window(bits, frames, near, side, a, m, lanes)
            conv = window(x, lambda o: kern[o - 1 : o, lanes], sub)
            acted = (conv * sigmoid(conv)).astype(BF)
            for c in range(cuts):
                at = pl.multiple_of((c * mics + n) * HALO, HALO)
                conv_out[pl.ds(at, HALO), lanes] = conv[c * HALO : (c + 1) * HALO]
                acted_out[pl.ds(at, HALO), lanes] = acted[c * HALO : (c + 1) * HALO]
        return 0

    lax.fori_loop(0, mics, conv_step, 0)


def main_kernel(
    plan, bits, frames, conv_in, acted_in, c0, c1, c2, c3, weights,
    a_keep, b_keep, a_send, b_send, back_keep, back_send, dconv_s,
    left_s, turned_s, right_s, q_s, k_s, v_s, u_s,
):
    groups, count, sub, width, factor = plan
    mics = groups * count
    cuts = sub // HALO
    block = mics * HALO
    rows = cuts * block
    cols = width // LANES

    wq, wk, wv, wo = (weights.at[i] for i in range(4))
    left_s[0] = acted_in[...]
    for d, cot in enumerate((c0, c1, c2, c3)):
        for m in range(count):
            for c in range(cuts):
                right_s[3, c, d, m] = cot[m, c * HALO : (c + 1) * HALO, :]

    def flat(i):
        return right_s[i].reshape(rows, width)

    def put(i, c, lanes, x):
        right_s[i, c, :, :, :, lanes] = x.astype(BF).reshape(groups, count, HALO, LANES)

    acted = left_s[0]
    q_s[...] = mm(acted, wq[...]).astype(BF)
    k_s[...] = mm(acted, wk[...]).astype(BF)
    v_s[...] = mm(acted, wv[...]).astype(BF)
    u_s[...] = mm(flat(3), wo[...], NT).astype(BF)
    turned_s[0] = acted.T

    depth = width // HEADS
    per = LANES // depth
    lane = lax.broadcasted_iota(jnp.int32, (block, LANES), 1)
    row_i = lax.broadcasted_iota(jnp.int32, (block, per * block), 0)
    col_i = lax.broadcasted_iota(jnp.int32, (block, per * block), 1)
    same = (row_i % HALO) == (col_i % HALO)

    def by_head(x):
        return jnp.concatenate(
            [jnp.where(lane // depth == h, x, jnp.zeros_like(x)) for h in range(per)], axis=0
        )

    def sums(x):
        return [
            jnp.sum(x[:, h * block : (h + 1) * block], axis=1, keepdims=True) for h in range(per)
        ]

    def each(x, values, op):
        return jnp.concatenate(
            [op(x[:, h * block : (h + 1) * block], values[h]) for h in range(per)], axis=1
        )

    def pick(x):
        out = x[:block]
        for h in range(1, per):
            out = jnp.where(lane // depth == h, x[h * block : (h + 1) * block], out)
        return out

    for c in range(cuts):
        part = slice(c * block, (c + 1) * block)
        for p in range(cols):
            lanes = slice(p * LANES, (p + 1) * LANES)
            q, u = q_s[part, lanes], u_s[part, lanes]
            kc, vc = by_head(k_s[part, lanes]), by_head(v_s[part, lanes])
            e = jnp.where(same, jnp.exp(mm(q, kc, NT) * factor), 0.0)
            w = each(e, [1.0 / x for x in sums(e)], lambda x, s: x * s)
            up = mm(u, vc, NT)
            inner = each(up, sums(w * up), lambda x, s: x - s) * w * factor
            wb, ib = w.astype(BF), inner.astype(BF)
            left_s[1, part, lanes] = mm(wb, vc).astype(BF)
            put(0, c, lanes, mm(ib, kc))
            put(1, c, lanes, pick(mm(ib, q, TN)))
            put(2, c, lanes, pick(mm(wb, u, TN)))

    turned_s[1] = left_s[1].T
    dacted = mm(flat(0), wq[...], NT) + mm(flat(1), wk[...], NT) + mm(flat(2), wv[...], NT)
    conv = conv_in[...]
    sig = sigmoid(conv)
    dconv_s[...] = dacted * sig * (1.0 + conv * (1.0 - sig))

    size = cols * width // 8
    core = bits[CORE]
    for out, owner, h in (
        (a_send, 1 - core, 0), (b_send, 1 - core, 1), (a_keep, core, 0), (b_keep, core, 1)
    ):
        i = owner * 2 + h
        span = size + HALO * (1 - h)
        first, second, third = ways(bits, h)
        grad = mm(turned_s[i // 3], flat(i)).astype(BF)
        for piece in range(8):
            cb, at = piece * size // width, piece * size % width
            rel = ((piece // 4) ^ first) * 4 + ((piece // 2 % 2) ^ second) * 2 + ((piece % 2) ^ third)
            start = pl.multiple_of(rel * span, HALO)
            out[pl.ds(start, size), :] = grad[at : at + size, cb * LANES : (cb + 1) * LANES]
            if h == 0:
                out[pl.ds(pl.multiple_of(start + size, HALO), HALO), :] = jnp.zeros(
                    (HALO, LANES), BF
                )

    proj = mm(left_s[1], wo[...])
    unit = 2 * count * cols * sub
    for d, (out, base) in enumerate(
        ((back_keep, 0), (back_send, 0), (back_keep, unit), (back_send, unit))
    ):
        for m in range(count):
            for c in range(cuts):
                at = c * block + (d * count + m) * HALO
                part = slice(c * HALO, (c + 1) * HALO)
                layer = (frames[d, m, part, :].astype(F32) + proj[at : at + HALO]).astype(BF)
                dconv = dconv_s[at : at + HALO, :].astype(BF)
                for lc in range(cols):
                    for kind, value in enumerate((layer, dconv)):
                        to = base + ((kind * count + m) * cols + lc) * sub + c * HALO
                        out[to : to + HALO, :] = value[:, lc * LANES : (lc + 1) * LANES]


def tap_kernel(plan, bits, frames, near, side, dconv_s, keep_in, send_in, keep, send, tap_s):
    groups, count, sub, width = plan
    mics = groups * count
    cuts = sub // HALO
    block = mics * HALO
    cols = width // LANES
    keep[...] = keep_in[...]
    send[...] = send_in[...]
    for lc in range(cols):
        lanes = slice(lc * LANES, (lc + 1) * LANES)

        def tap_step(n, accs):
            a, m = n // count, n % count
            x = frames_window(bits, frames, near, side, a, m, lanes)
            d = jnp.concatenate(
                [
                    dconv_s[pl.ds(pl.multiple_of(c * block + n * HALO, HALO), HALO), lanes]
                    for c in range(cuts)
                ],
                axis=0,
            )
            out = list(accs)
            for r in range(8):
                xr = rolled(x, r)
                for k in range(4):
                    o = 8 * k + r
                    if o == 0:
                        continue
                    prod = xr[8 * k : 8 * k + sub] * d
                    out[o - 1] = out[o - 1] + jnp.sum(prod.reshape(sub // 8, 8, LANES), axis=0)
            return tuple(out)

        accs = lax.fori_loop(0, mics, tap_step, tuple(jnp.zeros((8, LANES), F32) for _ in range(31)))
        tap_s[lc * 32 : lc * 32 + 32, :] = jnp.concatenate(
            [jnp.sum(x, axis=0, keepdims=True) for x in accs] + [jnp.zeros((1, LANES), F32)], axis=0
        )

    tap_s[cols * 32 :, :] = jnp.zeros((HALO, LANES), F32)
    size = cols * width // 8
    span = size + HALO
    core = bits[CORE]
    first, second, third = ways(bits, 0)
    for out, owner in ((send, 1 - core), (keep, core)):
        for piece in range(8):
            rel = ((piece // 4) ^ first) * 4 + ((piece // 2 % 2) ^ second) * 2 + ((piece % 2) ^ third)
            tail = tap_s[pl.ds(pl.multiple_of((owner * 8 + piece) * 8, 8), HALO), :]
            at = pl.multiple_of(rel * span + size, HALO)
            out[pl.ds(at, HALO), :] = tail.astype(BF)


def total(*parts):
    return functools.reduce(lambda x, y: x + y, [x.astype(F32) for x in parts]).astype(BF)


def final_kernel(plan, bits, *refs):
    kinds, first_call, with_taps, width, norm = plan
    cols = width // LANES
    size = cols * width // 8
    span = size + HALO
    core = bits[CORE]

    def piece_of(h, far, rel):
        first, second, third = ways(bits, h)
        return (first ^ far) * 4 + (second ^ (rel // 2)) * 2 + (third ^ (rel % 2))

    got, refs = refs[: len(kinds)], refs[len(kinds) :]
    if with_taps:
        tap_refs, refs, tap_grad, tap_s = refs[:4], refs[4:-4] + refs[-3:-1], refs[-4], refs[-1]
    *outs, piece_s, sems = refs if first_call else refs[4:]
    copies = []
    for n, (own, h, far) in enumerate(kinds):
        owner = core if own else 1 - core
        for rel in range(4):
            k = 4 * n + rel
            at = rel * (size + HALO * (1 - h))
            piece_s[k] = got[n][at : at + size, :].astype(F32) * norm
            piece = piece_of(h, far, rel)
            cb, at = piece * size // width, piece * size % width
            rows = pl.ds(pl.multiple_of(at, size), size)
            lanes = pl.ds(pl.multiple_of(cb * LANES, LANES), LANES)
            for which in range(2):
                copy = pltpu.make_async_copy(
                    piece_s.at[k], outs[2 * which + h].at[rows, lanes], sems.at[k]
                )
                copies.append((owner == which, copy))
                pl.when(owner == which)(copy.start)
    if with_taps:
        for n, ref in enumerate(tap_refs):
            owner = core if n < 2 else 1 - core
            for rel in range(4):
                at = rel * span + size
                tap_s[owner * 8 + piece_of(0, n % 2, rel)] = ref[at : at + HALO, :].astype(F32) * norm
        for g in range(16):
            lc, j = g // 4, g % 4 * 8
            kept = min(8, 31 - j)
            tap_grad[j : j + kept, lc * LANES : (lc + 1) * LANES] = tap_s[g, 0:kept]
    for here, copy in copies:
        pl.when(here)(copy.wait)


def home_kernel(plan, bits, own, core_got, y_got, layer_out, dconv, first_edge, last_edge):
    count, sub, cols = plan
    unit = 2 * count * cols * sub
    last = 4 * sub - HALO
    for d, (ref, base) in enumerate(
        ((own, 0), (core_got, 0), (y_got, 0), (y_got, unit))
    ):
        to = pl.ds(pl.multiple_of(bits[BLOCK_AT + d] * sub, sub), sub)
        for m in range(count):
            for lc in range(cols):
                at = base + (m * cols + lc) * sub
                layer_out[m, to, lc * LANES : (lc + 1) * LANES] = ref[at : at + sub, :]
                at += count * cols * sub
                dconv[m, lc, to, :] = ref[at : at + sub, :]
    for m in range(count):
        for lc in range(cols):
            at = (m * cols + lc) * HALO
            first_edge[at : at + HALO, :] = dconv[m, lc, :HALO, :]
            last_edge[at : at + HALO, :] = dconv[m, lc, last:, :]


def frame_kernel(plan, bits, dconv, x_got, z_got, other_got, cot, kern, frame_grad):
    count, cols, length = plan
    is_odd = jnp.broadcast_to(bits[X], (HALO, LANES)) == 1
    by_z = jnp.broadcast_to(bits[X] ^ bits[Z], (HALO, LANES)) == 1

    def step(m, _):
        for lc in range(cols):
            lanes = slice(lc * LANES, (lc + 1) * LANES)
            at = (m * cols + lc) * HALO
            rows = pl.ds(pl.multiple_of(at, HALO), HALO)
            x_rows = pl.ds(pl.multiple_of(bits[X] * count * cols * HALO + at, HALO), HALO)
            one = x_got[x_rows, :].astype(F32)
            two = jnp.where(by_z, z_got[rows, :].astype(F32), other_got[rows, :].astype(F32))
            x = jnp.concatenate(
                [
                    jnp.where(is_odd, one, two),
                    dconv[m, lc].astype(F32),
                    jnp.where(is_odd, two, one),
                ],
                axis=0,
            )
            grad = window(x, lambda o: kern[31 - o : 32 - o, lanes], length)
            frame_grad[m, :, lanes] = (cot[m, :, lanes].astype(F32) + grad).astype(BF)
        return 0

    lax.fori_loop(0, count, step, 0)


def call(body, outs, scratch, limit, *args, hbm=(), hbm_outs=(), aliases=None):
    spaces = [pltpu.HBM if i in hbm else pltpu.VMEM for i in range(len(args))]
    return pl.pallas_call(
        body,
        out_shape=outs,
        in_specs=[
            pl.BlockSpec(memory_space=pltpu.SMEM if x.dtype == jnp.int32 else space)
            for x, space in zip(args, spaces)
        ],
        out_specs=tuple(
            pl.BlockSpec(memory_space=pltpu.HBM if i in hbm_outs else pltpu.VMEM)
            for i in range(len(outs))
        ),
        scratch_shapes=scratch,
        input_output_aliases=aliases or {},
        compiler_params=pltpu.CompilerParams(vmem_limit_bytes=limit * MIB),
    )(*args)


def shards(frames, cotangent, kernel, w_query, w_key, w_value, w_out):
    groups, blocks = lax.axis_size("mic"), lax.axis_size("tm")
    count, length, width = frames.shape
    sub = length // groups
    cuts = sub // HALO
    cols = width // LANES
    rows = groups * count * sub
    shape = jax.ShapeDtypeStruct

    mic, tm = lax.axis_index("mic"), lax.axis_index("tm")
    over_core, over_y, over_x, over_z = blocks, 2 * blocks, 1, 2

    def order(a):
        return (a ^ (a >> 1)) ^ (3 * (tm % 2))

    mine = order(mic)
    bits = jnp.stack(
        [mic % 2, mic // 2, tm % 2, tm // 2 % 2, tm // 4 % 2, mine % 2, 2 * ((mine + 1) // 2 % 2)]
        + [order(mic ^ d) for d in range(4)]
    ).astype(jnp.int32)

    def permute(x, pairs):
        return lax.ppermute(x, ("mic", "tm"), pairs)

    def swap(x, mask):
        return permute(x, [(f, f ^ mask) for f in range(groups * blocks)])

    def both(pairs):
        return pairs + [(j, i) for i, j in pairs]

    masks = (0, over_core, over_y, over_core + over_y)

    def sub_block(x, d):
        return lax.dynamic_slice_in_dim(x, order(mic ^ d) * sub, sub, axis=1)

    def scattered(x):
        parts = [sub_block(x, d) for d in range(4)]
        got = {d: swap(parts[d], masks[d]) for d in (2, 3, 1)}
        return [parts[0], got[1], got[2], got[3]]

    f, c = scattered(frames), scattered(cotangent)
    weights = jnp.stack([w_query, w_key, w_value, w_out])
    edge = shape((groups, count, HALO, width), BF)
    near, side = call(functools.partial(edge_kernel, sub), (edge, edge), [], 8, bits, *f)
    near, side, weights = lax.optimization_barrier((near, side, weights))
    near = swap(near, over_core)
    side = permute(
        side,
        both([(blocks + t, 3 * blocks + t) for t in range(blocks)])
        + both([((2 - 2 * (t % 2)) * blocks + t, (2 - 2 * (t % 2)) * blocks + t + 1)
                for t in range(blocks - 1)]),
    )

    factor = 1.0 / math.sqrt(width // HEADS)
    size = width * width // LANES // 8
    span = size + HALO
    unit = 2 * count * cols * sub
    big = pltpu.VMEM((rows, width), BF)
    wide = pltpu.VMEM((rows, width), F32)

    def flat(n):
        return shape((n, LANES), BF)

    moved = shape((groups, count, sub, width), BF)
    placed, conv, acted = call(
        functools.partial(conv_kernel, (groups, count, sub, width)),
        (moved, shape((rows, width), F32), shape((rows, width), BF)),
        [], 8, bits, *f, near, side, kernel,
    )
    a_keep, b_keep, a_send, b_send, back_keep, back_send, dconv_here = call(
        functools.partial(main_kernel, (groups, count, sub, width, factor)),
        (flat(8 * span), flat(8 * size)) * 2 + (flat(2 * unit),) * 2 + (shape((rows, width), F32),),
        [
            pltpu.VMEM((2, rows, width), BF),
            pltpu.VMEM((2, width, rows), BF),
            pltpu.VMEM((4, cuts, groups, count, HALO, width), BF),
            big, big, big, big,
        ],
        24, bits, placed, conv, acted, *c, weights,
    )
    a_keep, a_send = call(
        functools.partial(tap_kernel, (groups, count, sub, width)), (flat(8 * span),) * 2,
        [pltpu.VMEM((32 * cols + HALO, LANES), F32)],
        8, bits, placed, near, side, dconv_here, a_keep, a_send,
    )

    lines = [2**i for i in range(1, blocks.bit_length() - 1)]

    def after(x, y):
        return lax.optimization_barrier((x, y))[0]

    def kept(parts, n):
        return lax.optimization_barrier(total(*(t[:n] for t in parts)))

    def halved(parts, mask):
        n = parts[0].shape[0] // 2
        return [kept(parts, n), swap(total(*(t[n:] for t in parts)), mask)]

    def exchanged(parts, masks):
        mine = total(*parts)
        for mask in masks:
            mine = total(mine, swap(mine, mask))
        return mine

    def doubled(x, mask):
        return jnp.concatenate([x, swap(x, mask)])

    a = [a_keep, swap(a_send, over_core)]
    b = [b_keep, swap(b_send, over_core)]
    core_got = swap(back_send, over_core)
    a_sent = total(*(t[4 * span :] for t in a))
    a = [kept(a, 4 * span), swap(a_sent, over_x)]
    b = halved(b, lines[0])
    core_got = after(core_got, a_sent)
    y_got = swap(jnp.concatenate([back_keep[unit:], core_got[unit:]]), over_y)
    y_got = after(y_got, b[-1])
    edge = flat(count * cols * HALO)
    layer_out, dconv, *edges = call(
        functools.partial(home_kernel, (count, sub, cols)),
        (shape(frames.shape, BF), shape((count, cols, length, LANES), BF), edge, edge),
        [], 8, bits, back_keep, core_got, y_got,
    )
    x_got = swap(jnp.concatenate(edges), over_x)
    n_edge = edge.shape[0]
    passed = lax.dynamic_slice_in_dim(x_got, (1 - tm % 2) * n_edge, n_edge, axis=0)
    a = halved(a, over_y)
    b = halved(b, over_x)
    got = swap(jnp.concatenate([total(*(t[span:] for t in a)), passed]), lines[0])
    a, z_got = [kept(a, span), got[:span]], got[span:]
    b = halved(b, lines[1])
    a = exchanged(a, lines[1:])
    b = exchanged(b, [over_y] + lines[2:])
    a = doubled(a, lines[0])
    b = doubled(b, lines[1])
    a = doubled(a, over_y)
    b = doubled(b, over_x)

    norm = 1.0 / math.sqrt(groups * count * blocks * length)
    square = shape((width, width), F32)

    def final(kinds, parts, grads, taps=()):
        first = 1 + len(parts) + len(taps)
        scratch = [
            pltpu.VMEM((4 * len(kinds), size, LANES), F32),
            pltpu.SemaphoreType.DMA((4 * len(kinds),)),
        ]
        return call(
            functools.partial(final_kernel, (kinds, not grads, bool(taps), width, norm)),
            (square,) * 4 + (shape((31, width), F32),) * bool(taps),
            scratch + [pltpu.VMEM((16, HALO, LANES), F32)] * bool(taps),
            10, bits, *parts, *taps, *grads, hbm=range(first, first + len(grads)),
            hbm_outs=range(4), aliases={first + i: i for i in range(len(grads))},
        )

    a_far, b_far = swap(a, over_x), swap(b, lines[0])
    other_got = permute(
        after(passed, (a, b)),
        both([(m * blocks + t, m * blocks + t + 2)
              for m in range(groups) for t in range(2, blocks - 2) if t // 2 % 2]),
    )
    a_other, b_other = swap(a, over_core), swap(b, over_core)
    (frame_grad,) = call(
        functools.partial(frame_kernel, (count, cols, length)),
        (shape(frames.shape, BF),), [], 8,
        bits, after(dconv, a), x_got, z_got, other_got, cotangent, kernel,
    )
    grads = final(((1, 0, 0), (1, 1, 0), (0, 0, 0), (0, 1, 0)), (a, b, a_other, b_other), ())
    a_far, b_far, frame_grad, *grads = lax.optimization_barrier(
        (a_far, b_far, frame_grad, *grads)
    )
    taps = (a, a_far, a_other)
    a_other, b_other = swap(a_far, over_core), swap(b_far, over_core)
    grads = final(((1, 0, 1), (1, 1, 1)), (a_far, b_far), grads)
    *grads, kernel_grad = final(
        ((0, 0, 1), (0, 1, 1)), (a_other, b_other), grads, (*taps, a_other)
    )
    return (layer_out, frame_grad, kernel_grad, *grads)


def solution(mesh):
    in_specs = (P("mic", "tm", None), P("mic", "tm", None), P(), P(), P(), P(), P())
    out_specs = (P("mic", "tm", None), P("mic", "tm", None), P(), P(), P(), P(), P())
    return jax.shard_map(shards, mesh=mesh, in_specs=in_specs, out_specs=out_specs, check_vma=False)
```

```python
import functools
import math

import jax
import jax.numpy as jnp
from jax import lax
from jax.experimental import pallas as pl
from jax.experimental.pallas import tpu as pltpu
from jax.sharding import PartitionSpec as P

HEADS = 8
LANES = 128
HALO = 16
NT = (((1,), (1,)), ((), ()))
TN = (((0,), (0,)), ((), ()))
BF = jnp.bfloat16
F32 = jnp.float32
MIB = 1024 * 1024
CORE, Y, X, Z, ZZ, ODD, SKIP, BLOCK_AT = range(8)


def mm(left, right, dims=(((1,), (0,)), ((), ()))):
    return lax.dot_general(left, right, dims, preferred_element_type=F32)


def rolled(x, shift):
    return x if shift == 0 else pltpu.roll(x, x.shape[0] - shift, axis=0)


def window(x, taps, rows):
    acc = None
    for r in range(8):
        xr = rolled(x, r)
        for k in range(4):
            o = 8 * k + r
            if o == 0:
                continue
            term = xr[8 * k : 8 * k + rows] * taps(o)
            acc = term if acc is None else acc + term
    return acc


def ways(bits, half):
    return [bits[i] for i in ((X, Y, Z), (Z, X, ZZ))[half]]


def sigmoid(v):
    return 0.5 * jnp.tanh(0.5 * v) + 0.5


def edge_kernel(sub, bits, f0, f1, f2, f3, near, side):
    odd = bits[ODD]
    for d, f in enumerate((f0, f1, f2, f3)):
        last = sub - HALO
        near[d] = f[:, pl.ds(pl.multiple_of((1 - odd) * last, HALO), HALO), :]
        side[d] = f[:, pl.ds(pl.multiple_of(odd * last, HALO), HALO), :]


def frames_window(bits, frames, near, side, a, m, lanes):
    is_odd = jnp.broadcast_to(bits[ODD], (HALO, LANES)) == 1
    one = near[a ^ 1, m, :, lanes].astype(F32)
    two = side[a ^ bits[SKIP], m, :, lanes].astype(F32)
    return jnp.concatenate(
        [
            jnp.where(is_odd, one, two),
            frames[a, m, :, lanes].astype(F32),
            jnp.where(is_odd, two, one),
        ],
        axis=0,
    )


def conv_kernel(plan, bits, f0, f1, f2, f3, near, side, kern, frames, conv_out, acted_out):
    groups, count, sub, width = plan
    mics = groups * count
    cuts = sub // HALO
    for d, f in enumerate((f0, f1, f2, f3)):
        frames[d] = f[...]

    def conv_step(n, _):
        a, m = n // count, n % count
        for lc in range(width // LANES):
            lanes = slice(lc * LANES, (lc + 1) * LANES)
            x = frames_window(bits, frames, near, side, a, m, lanes)
            conv = window(x, lambda o: kern[o - 1 : o, lanes], sub)
            acted = (conv * sigmoid(conv)).astype(BF)
            for c in range(cuts):
                at = pl.multiple_of((c * mics + n) * HALO, HALO)
                conv_out[pl.ds(at, HALO), lanes] = conv[c * HALO : (c + 1) * HALO]
                acted_out[pl.ds(at, HALO), lanes] = acted[c * HALO : (c + 1) * HALO]
        return 0

    lax.fori_loop(0, mics, conv_step, 0)


def main_kernel(
    plan, bits, frames, conv_in, acted_in, c0, c1, c2, c3, near, side, weights,
    a_keep, b_keep, a_send, b_send, back_keep, back_send,
    left_s, turned_s, right_s, q_s, k_s, v_s, u_s, dconv_s, tap_s,
):
    groups, count, sub, width, factor = plan
    mics = groups * count
    cuts = sub // HALO
    block = mics * HALO
    rows = cuts * block
    cols = width // LANES

    wq, wk, wv, wo = (weights.at[i] for i in range(4))
    left_s[0] = acted_in[...]
    for d, cot in enumerate((c0, c1, c2, c3)):
        for m in range(count):
            for c in range(cuts):
                right_s[3, c, d, m] = cot[m, c * HALO : (c + 1) * HALO, :]

    def flat(i):
        return right_s[i].reshape(rows, width)

    def put(i, c, lanes, x):
        right_s[i, c, :, :, :, lanes] = x.astype(BF).reshape(groups, count, HALO, LANES)

    acted = left_s[0]
    q_s[...] = mm(acted, wq[...]).astype(BF)
    k_s[...] = mm(acted, wk[...]).astype(BF)
    v_s[...] = mm(acted, wv[...]).astype(BF)
    u_s[...] = mm(flat(3), wo[...], NT).astype(BF)
    turned_s[0] = acted.T

    depth = width // HEADS
    per = LANES // depth
    lane = lax.broadcasted_iota(jnp.int32, (block, LANES), 1)
    row_i = lax.broadcasted_iota(jnp.int32, (block, per * block), 0)
    col_i = lax.broadcasted_iota(jnp.int32, (block, per * block), 1)
    same = (row_i % HALO) == (col_i % HALO)

    def by_head(x):
        return jnp.concatenate(
            [jnp.where(lane // depth == h, x, jnp.zeros_like(x)) for h in range(per)], axis=0
        )

    def sums(x):
        return [
            jnp.sum(x[:, h * block : (h + 1) * block], axis=1, keepdims=True) for h in range(per)
        ]

    def each(x, values, op):
        return jnp.concatenate(
            [op(x[:, h * block : (h + 1) * block], values[h]) for h in range(per)], axis=1
        )

    def pick(x):
        out = x[:block]
        for h in range(1, per):
            out = jnp.where(lane // depth == h, x[h * block : (h + 1) * block], out)
        return out

    for c in range(cuts):
        part = slice(c * block, (c + 1) * block)
        for p in range(cols):
            lanes = slice(p * LANES, (p + 1) * LANES)
            q, u = q_s[part, lanes], u_s[part, lanes]
            kc, vc = by_head(k_s[part, lanes]), by_head(v_s[part, lanes])
            e = jnp.where(same, jnp.exp(mm(q, kc, NT) * factor), 0.0)
            w = each(e, [1.0 / x for x in sums(e)], lambda x, s: x * s)
            up = mm(u, vc, NT)
            inner = each(up, sums(w * up), lambda x, s: x - s) * w * factor
            wb, ib = w.astype(BF), inner.astype(BF)
            left_s[1, part, lanes] = mm(wb, vc).astype(BF)
            put(0, c, lanes, mm(ib, kc))
            put(1, c, lanes, pick(mm(ib, q, TN)))
            put(2, c, lanes, pick(mm(wb, u, TN)))

    turned_s[1] = left_s[1].T
    dacted = mm(flat(0), wq[...], NT) + mm(flat(1), wk[...], NT) + mm(flat(2), wv[...], NT)
    conv = conv_in[...]
    sig = sigmoid(conv)
    dconv_s[...] = dacted * sig * (1.0 + conv * (1.0 - sig))

    for lc in range(cols):
        lanes = slice(lc * LANES, (lc + 1) * LANES)

        def tap_step(n, accs):
            a, m = n // count, n % count
            x = frames_window(bits, frames, near, side, a, m, lanes)
            d = jnp.concatenate(
                [
                    dconv_s[pl.ds(pl.multiple_of(c * block + n * HALO, HALO), HALO), lanes]
                    for c in range(cuts)
                ],
                axis=0,
            )
            out = list(accs)
            for r in range(8):
                xr = rolled(x, r)
                for k in range(4):
                    o = 8 * k + r
                    if o == 0:
                        continue
                    prod = xr[8 * k : 8 * k + sub] * d
                    out[o - 1] = out[o - 1] + jnp.sum(prod.reshape(sub // 8, 8, LANES), axis=0)
            return tuple(out)

        accs = lax.fori_loop(0, mics, tap_step, tuple(jnp.zeros((8, LANES), F32) for _ in range(31)))
        tap_s[lc * 32 : lc * 32 + 32, :] = jnp.concatenate(
            [jnp.sum(x, axis=0, keepdims=True) for x in accs] + [jnp.zeros((1, LANES), F32)], axis=0
        )

    tap_s[cols * 32 :, :] = jnp.zeros((HALO, LANES), F32)
    size = cols * width // 8
    core = bits[CORE]
    for out, owner, h in (
        (a_send, 1 - core, 0), (b_send, 1 - core, 1), (a_keep, core, 0), (b_keep, core, 1)
    ):
        i = owner * 2 + h
        span = size + HALO * (1 - h)
        first, second, third = ways(bits, h)
        grad = mm(turned_s[i // 3], flat(i)).astype(BF)
        for piece in range(8):
            cb, at = piece * size // width, piece * size % width
            rel = ((piece // 4) ^ first) * 4 + ((piece // 2 % 2) ^ second) * 2 + ((piece % 2) ^ third)
            start = pl.multiple_of(rel * span, HALO)
            out[pl.ds(start, size), :] = grad[at : at + size, cb * LANES : (cb + 1) * LANES]
            if h == 0:
                tail = tap_s[pl.ds(pl.multiple_of((owner * 8 + piece) * 8, 8), HALO), :]
                out[pl.ds(pl.multiple_of(start + size, HALO), HALO), :] = tail.astype(BF)

    proj = mm(left_s[1], wo[...])
    unit = 2 * count * cols * sub
    for d, (out, base) in enumerate(
        ((back_keep, 0), (back_send, 0), (back_keep, unit), (back_send, unit))
    ):
        for m in range(count):
            for c in range(cuts):
                at = c * block + (d * count + m) * HALO
                part = slice(c * HALO, (c + 1) * HALO)
                layer = (frames[d, m, part, :].astype(F32) + proj[at : at + HALO]).astype(BF)
                dconv = dconv_s[at : at + HALO, :].astype(BF)
                for lc in range(cols):
                    for kind, value in enumerate((layer, dconv)):
                        to = base + ((kind * count + m) * cols + lc) * sub + c * HALO
                        out[to : to + HALO, :] = value[:, lc * LANES : (lc + 1) * LANES]


def total(*parts):
    return functools.reduce(lambda x, y: x + y, [x.astype(F32) for x in parts]).astype(BF)


def final_kernel(plan, bits, *refs):
    kinds, first_call, with_taps, width, norm = plan
    cols = width // LANES
    size = cols * width // 8
    span = size + HALO
    core = bits[CORE]

    def piece_of(h, far, rel):
        first, second, third = ways(bits, h)
        return (first ^ far) * 4 + (second ^ (rel // 2)) * 2 + (third ^ (rel % 2))

    got, refs = refs[: len(kinds)], refs[len(kinds) :]
    if with_taps:
        tap_refs, refs, tap_grad, tap_s = refs[:4], refs[4:-4] + refs[-3:-1], refs[-4], refs[-1]
    *outs, piece_s, sems = refs if first_call else refs[4:]
    copies = []
    for n, (own, h, far) in enumerate(kinds):
        owner = core if own else 1 - core
        for rel in range(4):
            k = 4 * n + rel
            at = rel * (size + HALO * (1 - h))
            piece_s[k] = got[n][at : at + size, :].astype(F32) * norm
            piece = piece_of(h, far, rel)
            cb, at = piece * size // width, piece * size % width
            rows = pl.ds(pl.multiple_of(at, size), size)
            lanes = pl.ds(pl.multiple_of(cb * LANES, LANES), LANES)
            for which in range(2):
                copy = pltpu.make_async_copy(
                    piece_s.at[k], outs[2 * which + h].at[rows, lanes], sems.at[k]
                )
                copies.append((owner == which, copy))
                pl.when(owner == which)(copy.start)
    if with_taps:
        for n, ref in enumerate(tap_refs):
            owner = core if n < 2 else 1 - core
            for rel in range(4):
                at = rel * span + size
                tap_s[owner * 8 + piece_of(0, n % 2, rel)] = ref[at : at + HALO, :].astype(F32) * norm
        for g in range(16):
            lc, j = g // 4, g % 4 * 8
            kept = min(8, 31 - j)
            tap_grad[j : j + kept, lc * LANES : (lc + 1) * LANES] = tap_s[g, 0:kept]
    for here, copy in copies:
        pl.when(here)(copy.wait)


def home_kernel(plan, bits, own, core_got, y_got, layer_out, dconv, first_edge, last_edge):
    count, sub, cols = plan
    unit = 2 * count * cols * sub
    last = 4 * sub - HALO
    for d, (ref, base) in enumerate(
        ((own, 0), (core_got, 0), (y_got, 0), (y_got, unit))
    ):
        to = pl.ds(pl.multiple_of(bits[BLOCK_AT + d] * sub, sub), sub)
        for m in range(count):
            for lc in range(cols):
                at = base + (m * cols + lc) * sub
                layer_out[m, to, lc * LANES : (lc + 1) * LANES] = ref[at : at + sub, :]
                at += count * cols * sub
                dconv[m, lc, to, :] = ref[at : at + sub, :]
    for m in range(count):
        for lc in range(cols):
            at = (m * cols + lc) * HALO
            first_edge[at : at + HALO, :] = dconv[m, lc, :HALO, :]
            last_edge[at : at + HALO, :] = dconv[m, lc, last:, :]


def frame_kernel(plan, bits, dconv, x_got, z_got, other_got, cot, kern, frame_grad):
    count, cols, length = plan
    is_odd = jnp.broadcast_to(bits[X], (HALO, LANES)) == 1
    by_z = jnp.broadcast_to(bits[X] ^ bits[Z], (HALO, LANES)) == 1

    def step(m, _):
        for lc in range(cols):
            lanes = slice(lc * LANES, (lc + 1) * LANES)
            at = (m * cols + lc) * HALO
            rows = pl.ds(pl.multiple_of(at, HALO), HALO)
            x_rows = pl.ds(pl.multiple_of(bits[X] * count * cols * HALO + at, HALO), HALO)
            one = x_got[x_rows, :].astype(F32)
            two = jnp.where(by_z, z_got[rows, :].astype(F32), other_got[rows, :].astype(F32))
            x = jnp.concatenate(
                [
                    jnp.where(is_odd, one, two),
                    dconv[m, lc].astype(F32),
                    jnp.where(is_odd, two, one),
                ],
                axis=0,
            )
            grad = window(x, lambda o: kern[31 - o : 32 - o, lanes], length)
            frame_grad[m, :, lanes] = (cot[m, :, lanes].astype(F32) + grad).astype(BF)
        return 0

    lax.fori_loop(0, count, step, 0)


def call(body, outs, scratch, limit, *args, hbm=(), hbm_outs=(), aliases=None):
    spaces = [pltpu.HBM if i in hbm else pltpu.VMEM for i in range(len(args))]
    return pl.pallas_call(
        body,
        out_shape=outs,
        in_specs=[
            pl.BlockSpec(memory_space=pltpu.SMEM if x.dtype == jnp.int32 else space)
            for x, space in zip(args, spaces)
        ],
        out_specs=tuple(
            pl.BlockSpec(memory_space=pltpu.HBM if i in hbm_outs else pltpu.VMEM)
            for i in range(len(outs))
        ),
        scratch_shapes=scratch,
        input_output_aliases=aliases or {},
        compiler_params=pltpu.CompilerParams(vmem_limit_bytes=limit * MIB),
    )(*args)


def shards(frames, cotangent, kernel, w_query, w_key, w_value, w_out):
    groups, blocks = lax.axis_size("mic"), lax.axis_size("tm")
    count, length, width = frames.shape
    sub = length // groups
    cuts = sub // HALO
    cols = width // LANES
    rows = groups * count * sub
    shape = jax.ShapeDtypeStruct

    mic, tm = lax.axis_index("mic"), lax.axis_index("tm")
    over_core, over_y, over_x, over_z = blocks, 2 * blocks, 1, 2

    def order(a):
        return (a ^ (a >> 1)) ^ (3 * (tm % 2))

    mine = order(mic)
    bits = jnp.stack(
        [mic % 2, mic // 2, tm % 2, tm // 2 % 2, tm // 4 % 2, mine % 2, 2 * ((mine + 1) // 2 % 2)]
        + [order(mic ^ d) for d in range(4)]
    ).astype(jnp.int32)

    def permute(x, pairs):
        return lax.ppermute(x, ("mic", "tm"), pairs)

    def swap(x, mask):
        return permute(x, [(f, f ^ mask) for f in range(groups * blocks)])

    def both(pairs):
        return pairs + [(j, i) for i, j in pairs]

    masks = (0, over_core, over_y, over_core + over_y)

    def sub_block(x, d):
        return lax.dynamic_slice_in_dim(x, order(mic ^ d) * sub, sub, axis=1)

    def scattered(x):
        parts = [sub_block(x, d) for d in range(4)]
        got = {d: swap(parts[d], masks[d]) for d in (2, 3, 1)}
        return [parts[0], got[1], got[2], got[3]]

    f, c = scattered(frames), scattered(cotangent)
    weights = jnp.stack([w_query, w_key, w_value, w_out])
    edge = shape((groups, count, HALO, width), BF)
    near, side = call(functools.partial(edge_kernel, sub), (edge, edge), [], 8, bits, *f)
    near, side, weights = lax.optimization_barrier((near, side, weights))
    near = swap(near, over_core)
    side = permute(
        side,
        both([(blocks + t, 3 * blocks + t) for t in range(blocks)])
        + both([((2 - 2 * (t % 2)) * blocks + t, (2 - 2 * (t % 2)) * blocks + t + 1)
                for t in range(blocks - 1)]),
    )

    factor = 1.0 / math.sqrt(width // HEADS)
    size = width * width // LANES // 8
    span = size + HALO
    unit = 2 * count * cols * sub
    big = pltpu.VMEM((rows, width), BF)
    wide = pltpu.VMEM((rows, width), F32)

    def flat(n):
        return shape((n, LANES), BF)

    moved = shape((groups, count, sub, width), BF)
    placed, conv, acted = call(
        functools.partial(conv_kernel, (groups, count, sub, width)),
        (moved, shape((rows, width), F32), shape((rows, width), BF)),
        [], 8, bits, *f, near, side, kernel,
    )
    a_keep, b_keep, a_send, b_send, back_keep, back_send = call(
        functools.partial(main_kernel, (groups, count, sub, width, factor)),
        (flat(8 * span), flat(8 * size)) * 2 + (flat(2 * unit),) * 2,
        [
            pltpu.VMEM((2, rows, width), BF),
            pltpu.VMEM((2, width, rows), BF),
            pltpu.VMEM((4, cuts, groups, count, HALO, width), BF),
            big, big, big, big, wide,
            pltpu.VMEM((32 * cols + HALO, LANES), F32),
        ],
        24, bits, placed, conv, acted, *c, near, side, weights,
    )

    lines = [2**i for i in range(1, blocks.bit_length() - 1)]

    def after(x, y):
        return lax.optimization_barrier((x, y))[0]

    def kept(parts, n):
        return lax.optimization_barrier(total(*(t[:n] for t in parts)))

    def halved(parts, mask):
        n = parts[0].shape[0] // 2
        return [kept(parts, n), swap(total(*(t[n:] for t in parts)), mask)]

    def exchanged(parts, masks):
        mine = total(*parts)
        for mask in masks:
            mine = total(mine, swap(mine, mask))
        return mine

    def doubled(x, mask):
        return jnp.concatenate([x, swap(x, mask)])

    a = [a_keep, swap(a_send, over_core)]
    b = [b_keep, swap(b_send, over_core)]
    core_got = swap(back_send, over_core)
    a = halved(a, over_x)
    b = halved(b, lines[0])
    y_got = swap(jnp.concatenate([back_keep[unit:], core_got[unit:]]), over_y)
    y_got = after(y_got, b[-1])
    edge = flat(count * cols * HALO)
    layer_out, dconv, *edges = call(
        functools.partial(home_kernel, (count, sub, cols)),
        (shape(frames.shape, BF), shape((count, cols, length, LANES), BF), edge, edge),
        [], 8, bits, back_keep, core_got, y_got,
    )
    x_got = swap(jnp.concatenate(edges), over_x)
    n_edge = edge.shape[0]
    passed = lax.dynamic_slice_in_dim(x_got, (1 - tm % 2) * n_edge, n_edge, axis=0)
    a = halved(a, over_y)
    b = halved(b, over_x)
    got = swap(jnp.concatenate([total(*(t[span:] for t in a)), passed]), lines[0])
    a, z_got = [kept(a, span), got[:span]], got[span:]
    b = halved(b, lines[1])
    other_got = permute(
        passed,
        both([(m * blocks + t, m * blocks + t + 2)
              for m in range(groups) for t in range(2, blocks - 2) if t // 2 % 2]),
    )
    a = exchanged([after(a[0], other_got), a[1]], lines[1:])
    b = exchanged(b, [over_y] + lines[2:])
    a = doubled(a, lines[0])
    b = doubled(b, lines[1])
    a = doubled(a, over_y)
    b = doubled(b, over_x)

    norm = 1.0 / math.sqrt(groups * count * blocks * length)
    square = shape((width, width), F32)

    def final(kinds, parts, grads, taps=()):
        first = 1 + len(parts) + len(taps)
        scratch = [
            pltpu.VMEM((4 * len(kinds), size, LANES), F32),
            pltpu.SemaphoreType.DMA((4 * len(kinds),)),
        ]
        return call(
            functools.partial(final_kernel, (kinds, not grads, bool(taps), width, norm)),
            (square,) * 4 + (shape((31, width), F32),) * bool(taps),
            scratch + [pltpu.VMEM((16, HALO, LANES), F32)] * bool(taps),
            10, bits, *parts, *taps, *grads, hbm=range(first, first + len(grads)),
            hbm_outs=range(4), aliases={first + i: i for i in range(len(grads))},
        )

    a_far, b_far = swap(a, over_x), swap(b, lines[0])
    a_other, b_other = swap(a, over_core), swap(b, over_core)
    (frame_grad,) = call(
        functools.partial(frame_kernel, (count, cols, length)),
        (shape(frames.shape, BF),), [], 8,
        bits, after(dconv, a), x_got, z_got, other_got, cotangent, kernel,
    )
    grads = final(((1, 0, 0), (1, 1, 0), (0, 0, 0), (0, 1, 0)), (a, b, a_other, b_other), ())
    a_far, b_far, frame_grad, *grads = lax.optimization_barrier(
        (a_far, b_far, frame_grad, *grads)
    )
    taps = (a, a_far, a_other)
    a_other, b_other = swap(a_far, over_core), swap(b_far, over_core)
    grads = final(((1, 0, 1), (1, 1, 1)), (a_far, b_far), grads)
    *grads, kernel_grad = final(
        ((0, 0, 1), (0, 1, 1)), (a_other, b_other), grads, (*taps, a_other)
    )
    return (layer_out, frame_grad, kernel_grad, *grads)


def solution(mesh):
    in_specs = (P("mic", "tm", None), P("mic", "tm", None), P(), P(), P(), P(), P())
    out_specs = (P("mic", "tm", None), P("mic", "tm", None), P(), P(), P(), P(), P())
    return jax.shard_map(shards, mesh=mesh, in_specs=in_specs, out_specs=out_specs, check_vma=False)
```
